32 devices in a mesh: parts: 2 (over y), freq: 4 (over z), state: 4 (over x, core).
Axes of the slice: x: 2, y: 2, z: 4, core: 2. Of those that a mesh axis runs over, the one named last changes fastest.
Arguments:
- gap_in: float32 [1024, 2048], P(('parts', 'freq'), 'state'), parts along dimension 0, may hold values from -10 to 10, as said below
- coupling: bfloat16 [32, 2, 9, 128, 128], P(('parts', 'state')), parts along dimension 0, may hold values from 0 to 0.0002593994
- pair_cols: int32 [32, 2], P(('parts', 'state')), parts along dimension 0, may hold values from 0 to 15, as said below
- pair_count: int32 [32], P(('parts', 'state')), parts along dimension 0, may hold values from 1 to 2, 24 in all
- block_order: int32 [32], P('parts'), parts along dimension 0, may hold values from 0 to 15, each once
- phonon: float32 [18], P('parts'), parts along dimension 0, may hold values from 0.015 to 0.5
Outputs:
- gap_out: float32 [1024, 2048], P(('parts', 'freq'), 'state'), parts along dimension 0
- renorm: float32 [1024, 2048], P(('parts', 'freq'), 'state'), parts along dimension 0
The draws below stay inside these ranges and needn't reach their ends.
There are 2 independent parts, one for each index of `parts`. The reference program is written for one: setup_inputs(seed, part) draws one part's arguments, and reference() takes and returns one part's arrays. A program takes and returns all parts, laid end to end along the dimension named above; each array names one. Nothing has to cross between parts.
Inputs may be any that keep to these rules, and one draw needn't show every extreme that they name: gap_in[n] equals gap_in[511 - n] for every frequency row n. `pair_cols`: each row holds 2 different block numbers; every block number stands first in exactly one row. `pair_count`: the counts sum to 24. `block_order`: each block number once.
All inputs are finite; a program needn't handle non-finite values. No bound on the sum of `pair_count` on one device may be relied on, other than what follows from the above.
Results may differ from the reference program's by a relative error of at most 0.0003.
Values may be sent and summed in bfloat16 or wider, within the bound.
No kernel may reach another device: no remote copies, remote signals or barrier semaphores. Data moves between devices by JAX's collectives and lax.ppermute only.
A program may use at most 64 MiB of HBM per device.

```python
import math
import jax
import jax.numpy as jnp
import numpy as np
from jax import lax

NF = 512
MODES = 9
SB = 128
PAIRS = 2
ITERS = 2
NB = 16
STATES = 2048
TOTAL_PAIRS = 24


def draw_gap_in(key, part):
    key = jax.random.fold_in(key, 5)
    keys = jax.random.split(key, 2)
    half_rows = NF // 2
    amplitude = jax.random.uniform(keys[0], (1, STATES), jnp.float32, -0.6, 1.4)
    roughness = jax.random.uniform(keys[1], (half_rows, STATES), jnp.float32, 0.5, 1.5)
    upper_half = amplitude * roughness
    return jnp.concatenate([jnp.flip(upper_half, 0), upper_half], axis=0).astype(jnp.float32)


def draw_pair_cols(key, part):
    key = jax.random.fold_in(key, 11)
    keys = jax.random.split(key, 2)
    leading = jax.random.permutation(keys[0], NB).astype(jnp.int32)
    scores = jax.random.randint(keys[1], (NB, NB - 1), 0, 1 << 20, dtype=jnp.int32) * (NB - 1) + jnp.arange(NB - 1, dtype=jnp.int32)[None, :]
    ranked = jnp.argsort(scores, axis=1).astype(jnp.int32)
    offsets = 1 + ranked[:, :PAIRS - 1]
    others = (leading[:, None] + offsets) % NB
    return jnp.concatenate([leading[:, None], others], axis=1).astype(jnp.int32)


def levels(key, extent, cuts, least, top_value):
    gain, own = 1.0, jax.random.fold_in(key, 6)
    for axis_at, shards_of in cuts:
        heights = jnp.exp(jax.random.uniform(jax.random.fold_in(own, axis_at), (shards_of,), jnp.float32, least / len(cuts), top_value / len(cuts)))
        gain = gain * jnp.repeat(heights, extent[axis_at] // shards_of).reshape([-1 if axis == axis_at else 1 for axis in range(len(extent))])
    return gain


def split_up(amount, total, most, skew):
    weights = [(1 << 20) // math.isqrt(standing ** skew) + 1 for standing in range(2, amount + 1)]
    surplus, counts = total - most - (amount - 1), [1] * (amount - 1)
    while surplus > 0:
        free = [i for i in range(amount - 1) if counts[i] < most]
        pool, remaining = sum([weights[i] for i in free]), surplus
        for i in free:
            more = min(most - counts[i], max(1, remaining * weights[i] // pool), surplus)
            counts[i] = counts[i] + more
            surplus = surplus - more
    return np.array([most] + counts)


def uneven(stream_key, amount, total, reach, slope):
    if amount == 2:
        one = jax.random.randint(stream_key, (), max(1, total - reach), min(reach, total - 1) + 1)
        return jnp.stack([one, total - one])
    lengths = jnp.asarray(split_up(amount, total, reach, slope), jnp.int32)
    pairs = (amount - 1) // 2
    source_of, receiver = lengths[1:1 + 2 * pairs:2], lengths[2:2 + 2 * pairs:2]
    room = jnp.minimum(source_of - 1, reach - receiver)
    passed = jax.random.randint(jax.random.fold_in(stream_key, 1), (pairs,), 0, 1 << 20) % (room + 1)
    lengths = lengths.at[1:1 + 2 * pairs:2].set(source_of - passed).at[2:2 + 2 * pairs:2].set(receiver + passed)
    return lengths[jax.random.permutation(jax.random.fold_in(stream_key, 2), amount)]


def setup_inputs(seed: int = 0, part: int = 0) -> dict:
    key_of = jax.random.split(jax.random.key(seed), 7)
    own_keys = jax.random.split(jax.random.fold_in(key_of[6], part), 7)
    return {
        "gap_in": draw_gap_in(jax.random.fold_in(jax.random.fold_in(key_of[6], part), 71), part),
        "coupling": jnp.clip(0.0002593994 * jax.random.uniform(own_keys[1], (NB, PAIRS, MODES, SB, SB), jnp.float32) ** levels(own_keys[1], (NB, PAIRS, MODES, SB, SB), ((0, 4),), -0.2, 0.2), 0.0, 0.0002593994).astype(jnp.bfloat16),
        "pair_cols": draw_pair_cols(jax.random.fold_in(jax.random.fold_in(key_of[6], part), 71), part),
        "pair_count": uneven(own_keys[3], NB, TOTAL_PAIRS, PAIRS, 2).astype(jnp.int32),
        "block_order": jax.random.permutation(own_keys[4], NB).astype(jnp.int32),
        "phonon": jnp.clip(jnp.exp(jax.random.uniform(own_keys[5], (MODES,), jnp.float32, math.log(0.015), math.log(0.5))), 0.015, 0.5),
    }


CUTOFF = 4.0

def frequencies(total_rows):
    return (2.0 * jnp.arange(total_rows, dtype=jnp.float32) + 1.0 - total_rows) * (CUTOFF / total_rows)

def kernel(row_freq, col_freq, phonon):
    spacing = row_freq[:, None] - col_freq[None, :]
    return 2.0 * phonon[:, None, None] / (spacing[None, :, :] ** 2 + phonon[:, None, None] ** 2)

def reference(gap_in, coupling, pair_cols, pair_count, block_order, phonon):
    all_freq = frequencies(NF)
    coupling_kernel = kernel(all_freq, all_freq, phonon)
    numbers = jnp.arange(NB, dtype=jnp.int32)
    position = lax.optimization_barrier(jnp.sum(jnp.where(block_order[None, :] == numbers[:, None], numbers[None, :], 0), axis=1)).astype(jnp.int32)
    column_place = position[pair_cols].astype(jnp.int32)
    live_mask = (jnp.arange(PAIRS, dtype=jnp.int32)[None, :] < pair_count[:, None]).astype(jnp.float32)
    gap_now = gap_in
    renorm = jnp.ones_like(gap_in)
    for iteration in range(ITERS):
        radius = jnp.sqrt(all_freq[:, None] ** 2 + gap_now ** 2)
        ratios = jnp.stack([gap_now / radius, all_freq[:, None] / radius]).astype(jnp.bfloat16)
        ratio_blocks = ratios.reshape(2, NF, NB, SB).astype(jnp.float32)

        def one_row(inputs):
            weights, columns, live_row = inputs
            picked = ratio_blocks[:, :, columns, :] * live_row[None, None, :, None]
            partial_y = jnp.einsum('jvst,qmjt->vqms', weights.astype(jnp.float32), picked)
            return jnp.einsum('vnm,vqms->nqs', coupling_kernel, partial_y, precision=lax.Precision.HIGHEST)
        summed = lax.map(one_row, (coupling, column_place, live_mask))
        summed = jnp.transpose(summed, (1, 2, 0, 3)).reshape(NF, 2, NB * SB)
        renorm = 1.0 + CUTOFF / NF * summed[:, 1, :] / all_freq[:, None]
        gap_now = CUTOFF / NF * summed[:, 0, :] / renorm
    return (gap_now, renorm)
```

```python
import functools

import jax
import jax.numpy as jnp
from jax import lax
from jax.experimental import pallas as pl
from jax.experimental.pallas import tpu as pltpu
from jax.sharding import PartitionSpec as P

ITERS = 2
CUTOFF = 4.0
LANES = 128


def omega_of(index, freq_count):
    return (2.0 * index.astype(jnp.float32) + 1.0 - freq_count) * (CUTOFF / freq_count)


def segment_omega(shape, axis, meta, segment_rows, freq_count):
    at = lax.broadcasted_iota(jnp.int32, shape, axis)
    index = at + meta[1]
    for number, start in enumerate(range(segment_rows, shape[axis], segment_rows), 1):
        index = jnp.where(at >= start, at - start + meta[1 + number], index)
    return omega_of(index, freq_count)


def tables_kernel(dims, meta, phonon, coupling, weights, table):
    freq_count, half_rows, segment_rows, padded_rows, modes = dims
    blocks, slots = coupling.shape[:2]
    size = coupling.shape[3]
    row = lax.broadcasted_iota(jnp.int32, (padded_rows, half_rows), 0) + meta[0]
    row_omega = omega_of(row, freq_count)
    col_omega = segment_omega(
        (padded_rows, half_rows), 1, meta, segment_rows, freq_count
    )
    near = (row_omega - col_omega) ** 2
    far = (row_omega + col_omega) ** 2
    for mode in range(modes):
        strength = phonon[mode]
        direct = 2.0 * strength / (near + strength * strength)
        mirrored = 2.0 * strength / (far + strength * strength)
        for part, value in enumerate((direct + mirrored, direct - mirrored)):
            high = value.astype(jnp.bfloat16)
            low = (value - high.astype(jnp.float32)).astype(jnp.bfloat16)
            columns = slice(mode * half_rows, (mode + 1) * half_rows)
            table[part, :padded_rows, columns] = high
            table[part, padded_rows:, columns] = low
    for block in range(blocks):
        for slot in range(slots):
            for mode in range(modes):
                weights[
                    block, slot * size : (slot + 1) * size, mode * size : (mode + 1) * size
                ] = coupling[block, slot, mode].T


def step_kernel(dims, groups, segments, meta, source, *refs):
    freq_count, half_rows, segment_rows, padded_rows, modes = dims
    pieces = refs[: groups * segments]
    weights, table, gap_out, renorm_out, fetched, ratios, high, low, sems = refs[
        groups * segments :
    ]
    own_rows = gap_out.shape[0]
    blocks = weights.shape[0]
    size = LANES
    slots = weights.shape[1] // size

    def copy(pair, group, segment):
        column = pl.multiple_of(source[1, pair] * size, size)
        return pltpu.make_async_copy(
            pieces[group * segments + segment].at[:, pl.ds(column, size)],
            fetched.at[pair, pl.ds(segment * segment_rows, segment_rows), :],
            sems.at[pair, segment],
        )

    for pair in range(blocks * slots):
        for group in range(groups):

            @pl.when(source[0, pair] == group)
            def _():
                for segment in range(segments):
                    copy(pair, group, segment).start()

    col_omega = segment_omega((half_rows, size), 0, meta, segment_rows, freq_count)
    square = col_omega * col_omega
    for block in range(blocks):
        for slot in range(slots):
            pair = block * slots + slot
            for segment in range(segments):
                copy(pair, 0, segment).wait()
            gap = fetched[pair]
            live = source[2, pair].astype(jnp.float32)
            inverse = lax.rsqrt(square + gap * gap) * live
            lanes = slice(slot * size, (slot + 1) * size)
            ratios[block, :half_rows, lanes] = (gap * inverse).astype(jnp.bfloat16)
            ratios[block, half_rows:, lanes] = (col_omega * inverse).astype(jnp.bfloat16)
        for part in range(2):
            for first in range(0, modes, 2):
                last = min(first + 2, modes)
                terms = jnp.dot(
                    ratios[block, part * half_rows : (part + 1) * half_rows, :],
                    weights[block, :, first * size : last * size],
                    preferred_element_type=jnp.float32,
                )
                upper = terms.astype(jnp.bfloat16)
                lower = (terms - upper.astype(jnp.float32)).astype(jnp.bfloat16)
                for mode in range(first, last):
                    rows = slice(mode * half_rows, (mode + 1) * half_rows)
                    taken = slice((mode - first) * size, (mode - first + 1) * size)
                    lanes = slice(block * size, (block + 1) * size)
                    high[part, rows, lanes] = upper[:, taken]
                    low[part, rows, lanes] = lower[:, taken]
    summed = []
    for part in range(2):
        both = jnp.dot(table[part], high[part], preferred_element_type=jnp.float32)
        rest = jnp.dot(
            table[part, :padded_rows], low[part], preferred_element_type=jnp.float32
        )
        summed.append((both[:padded_rows] + (both[padded_rows:] + rest))[:own_rows])
    row = lax.broadcasted_iota(jnp.int32, gap_out.shape, 0) + meta[0]
    temperature = CUTOFF / freq_count
    renorm = 1.0 + temperature * summed[1] / omega_of(row, freq_count)
    renorm_out[...] = renorm
    gap_out[...] = temperature * summed[0] / renorm


def swapped(axis_size, bit):
    return [(i, i ^ bit) for i in range(axis_size)]


def gather_pairwise(gap):
    core = lambda value: lax.ppermute(value, "state", swapped(4, 1))
    joint = [(4 * f + s, 4 * (f ^ 1) + (s ^ 2)) for f in range(4) for s in range(4)]
    along_x = lax.ppermute(gap, "state", swapped(4, 2))
    along_z = lax.ppermute(gap, "freq", swapped(4, 1))
    diagonal = lax.ppermute(gap, ("freq", "state"), joint)
    return [
        gap,
        along_z,
        core(gap),
        core(along_z),
        along_x,
        diagonal,
        core(along_x),
        core(diagonal),
    ]


def gather_general(gap, half_groups):
    groups = lax.axis_size("state")
    everyone = lax.all_gather(gap, "state", axis=0, tiled=False)
    rows = lax.all_gather(everyone, "freq", axis=1, tiled=True)
    own_rows = gap.shape[0]
    start = (lax.axis_index("freq") // half_groups) * (half_groups * own_rows)
    half = lax.dynamic_slice_in_dim(rows, start, half_groups * own_rows, 1)
    return [half[group] for group in range(groups)]


def on_device(gap_in, coupling, pair_cols, pair_count, block_order, phonon):
    own_rows, row_width = gap_in.shape
    blocks, slots, modes, size, _ = coupling.shape
    block_count = block_order.shape[0]
    freq_groups = lax.axis_size("freq")
    groups = lax.axis_size("state")
    freq_count = own_rows * freq_groups
    half_rows = freq_count // 2
    half_groups = freq_groups // 2
    pairwise = freq_groups == 4 and groups == 4
    padded_rows = -(-own_rows // 16) * 16
    freq_at = lax.axis_index("freq")
    state_at = lax.axis_index("state")

    numbers = jnp.arange(block_count, dtype=jnp.int32)
    position = jnp.sum(
        jnp.where(block_order[None, :] == numbers[:, None], numbers[None, :], 0), axis=1
    )
    column_place = jnp.sum(
        jnp.where(pair_cols[:, :, None] == numbers[None, None, :], position[None, None, :], 0),
        axis=2,
    )
    live = (jnp.arange(slots, dtype=jnp.int32)[None, :] < pair_count[:, None]).astype(jnp.int32)
    holder = column_place // blocks
    if pairwise:
        segments = 2
        holder = holder ^ state_at
        meta = jnp.stack([freq_at, freq_at, freq_at ^ 1]) * own_rows
    else:
        segments = 1
        first = (freq_at // half_groups) * half_rows
        meta = jnp.stack([freq_at * own_rows, first, first])
    meta = meta.astype(jnp.int32)
    source = jnp.stack(
        [holder.reshape(-1), (column_place % blocks).reshape(-1), live.reshape(-1)]
    ).astype(jnp.int32)

    segment_rows = half_rows // segments
    dims = (freq_count, half_rows, segment_rows, padded_rows, modes)
    smem = pl.BlockSpec(memory_space=pltpu.SMEM)
    vmem = pl.BlockSpec(memory_space=pltpu.VMEM)
    weights, table = pl.pallas_call(
        functools.partial(tables_kernel, dims),
        out_shape=(
            jax.ShapeDtypeStruct((blocks, slots * size, modes * size), jnp.bfloat16),
            jax.ShapeDtypeStruct((2, 2 * padded_rows, modes * half_rows), jnp.bfloat16),
        ),
        in_specs=[smem, smem, vmem],
        out_specs=(vmem, vmem),
        compiler_params=pltpu.CompilerParams(vmem_limit_bytes=32 << 20),
        cost_estimate=pl.CostEstimate(flops=10_000_000, bytes_accessed=8_000_000, transcendentals=0),
        name="tables",
    )(meta, phonon, coupling)
    step = pl.pallas_call(
        functools.partial(step_kernel, dims, groups, segments),
        out_shape=(jax.ShapeDtypeStruct(gap_in.shape, jnp.float32),) * 2,
        in_specs=[smem, smem]
        + [pl.BlockSpec(memory_space=pl.ANY)] * (groups * segments)
        + [vmem, vmem],
        out_specs=(vmem, vmem),
        scratch_shapes=[
            pltpu.VMEM((blocks * slots, half_rows, size), jnp.float32),
            pltpu.VMEM((blocks, 2 * half_rows, slots * size), jnp.bfloat16),
            pltpu.VMEM((2, modes * half_rows, row_width), jnp.bfloat16),
            pltpu.VMEM((2, modes * half_rows, row_width), jnp.bfloat16),
            pltpu.SemaphoreType.DMA((blocks * slots, segments)),
        ],
        compiler_params=pltpu.CompilerParams(vmem_limit_bytes=40 << 20),
        cost_estimate=pl.CostEstimate(
            flops=3_000_000_000, bytes_accessed=8_000_000, transcendentals=0
        ),
        name="step",
    )
    gap, renorm = gap_in, None
    for _ in range(ITERS):
        pieces = gather_pairwise(gap) if pairwise else gather_general(gap, half_groups)
        gap, renorm = step(meta, source, *pieces, weights, table)
    return (gap, renorm)


def solution(mesh):
    return jax.shard_map(
        on_device,
        mesh=mesh,
        in_specs=(
            P(("parts", "freq"), "state"),
            P(("parts", "state"), None, None, None, None),
            P(("parts", "state"), None),
            P(("parts", "state")),
            P("parts"),
            P("parts"),
        ),
        out_specs=(P(("parts", "freq"), "state"), P(("parts", "freq"), "state")),
        check_vma=False,
    )
```

```python
import functools

import jax
import jax.numpy as jnp
from jax import lax
from jax.experimental import pallas as pl
from jax.experimental.pallas import tpu as pltpu
from jax.sharding import PartitionSpec as P

ITERS = 2
CUTOFF = 4.0
LANES = 128
GAP_LIMIT = 10.0
CODE_LIMIT = 32767.0
CODE_POWER = 5


def omega_of(index, freq_count):
    return (2.0 * index.astype(jnp.float32) + 1.0 - freq_count) * (CUTOFF / freq_count)


def segment_omega(shape, axis, meta, segment_rows, freq_count):
    at = lax.broadcasted_iota(jnp.int32, shape, axis)
    index = at + meta[1]
    for number, start in enumerate(range(segment_rows, shape[axis], segment_rows), 1):
        index = jnp.where(at >= start, at - start + meta[1 + number], index)
    return omega_of(index, freq_count)


def encoded(gap):
    share = jnp.minimum(jnp.abs(gap) * (1.0 / GAP_LIMIT), 1.0)
    root = jnp.exp2(jnp.log2(jnp.maximum(share, 1e-37)) * (1.0 / CODE_POWER))
    code = jnp.floor(root * CODE_LIMIT + 0.5)
    return jnp.where(gap < 0, -code, code).astype(jnp.int32).astype(jnp.int16)


def decoded(code):
    root = code.astype(jnp.float32) * (1.0 / CODE_LIMIT)
    square = root * root
    return (root * GAP_LIMIT) * (square * square)


def encode_kernel(gap, code):
    code[...] = encoded(gap[...])


def tables_kernel(dims, meta, phonon, coupling, weights, table):
    freq_count, half_rows, segment_rows, padded_rows, modes = dims
    blocks, slots = coupling.shape[:2]
    size = coupling.shape[3]
    row = lax.broadcasted_iota(jnp.int32, (padded_rows, half_rows), 0) + meta[0]
    row_omega = omega_of(row, freq_count)
    col_omega = segment_omega(
        (padded_rows, half_rows), 1, meta, segment_rows, freq_count
    )
    near = (row_omega - col_omega) ** 2
    far = (row_omega + col_omega) ** 2
    for mode in range(modes):
        strength = phonon[mode]
        direct = 2.0 * strength / (near + strength * strength)
        mirrored = 2.0 * strength / (far + strength * strength)
        for part, value in enumerate((direct + mirrored, direct - mirrored)):
            high = value.astype(jnp.bfloat16)
            low = (value - high.astype(jnp.float32)).astype(jnp.bfloat16)
            columns = slice(mode * half_rows, (mode + 1) * half_rows)
            table[part, :padded_rows, columns] = high
            table[part, padded_rows:, columns] = low
    for block in range(blocks):
        for slot in range(slots):
            for mode in range(modes):
                weights[
                    block, slot * size : (slot + 1) * size, mode * size : (mode + 1) * size
                ] = coupling[block, slot, mode].T


def step_kernel(dims, groups, segments, coded, final, meta, source, *refs):
    freq_count, half_rows, segment_rows, padded_rows, modes = dims
    pieces = refs[: groups * segments]
    refs = refs[groups * segments :]
    weights, table, gap_out = refs[:3]
    fetched, ratios, high, low, sems = refs[-5:]
    own_rows = gap_out.shape[0]
    blocks = weights.shape[0]
    size = LANES
    slots = weights.shape[1] // size

    def copy(pair, group, segment):
        column = pl.multiple_of(source[1, pair] * size, size)
        return pltpu.make_async_copy(
            pieces[group * segments + segment].at[:, pl.ds(column, size)],
            fetched.at[pair, pl.ds(segment * segment_rows, segment_rows), :],
            sems.at[pair, segment],
        )

    for pair in range(blocks * slots):
        for group in range(groups):

            @pl.when(source[0, pair] == group)
            def _():
                for segment in range(segments):
                    copy(pair, group, segment).start()

    col_omega = segment_omega((half_rows, size), 0, meta, segment_rows, freq_count)
    square = col_omega * col_omega
    for block in range(blocks):
        for slot in range(slots):
            pair = block * slots + slot
            for segment in range(segments):
                copy(pair, 0, segment).wait()
            gap = decoded(fetched[pair]) if coded else fetched[pair]
            live = source[2, pair].astype(jnp.float32)
            inverse = lax.rsqrt(square + gap * gap) * live
            lanes = slice(slot * size, (slot + 1) * size)
            ratios[block, :half_rows, lanes] = (gap * inverse).astype(jnp.bfloat16)
            ratios[block, half_rows:, lanes] = (col_omega * inverse).astype(jnp.bfloat16)
        for part in range(2):
            for first in range(0, modes, 2):
                last = min(first + 2, modes)
                terms = jnp.dot(
                    ratios[block, part * half_rows : (part + 1) * half_rows, :],
                    weights[block, :, first * size : last * size],
                    preferred_element_type=jnp.float32,
                )
                upper = terms.astype(jnp.bfloat16)
                lower = (terms - upper.astype(jnp.float32)).astype(jnp.bfloat16)
                for mode in range(first, last):
                    rows = slice(mode * half_rows, (mode + 1) * half_rows)
                    taken = slice((mode - first) * size, (mode - first + 1) * size)
                    lanes = slice(block * size, (block + 1) * size)
                    high[part, rows, lanes] = upper[:, taken]
                    low[part, rows, lanes] = lower[:, taken]
    summed = []
    for part in range(2):
        both = jnp.dot(table[part], high[part], preferred_element_type=jnp.float32)
        rest = jnp.dot(
            table[part, :padded_rows], low[part], preferred_element_type=jnp.float32
        )
        summed.append((both[:padded_rows] + (both[padded_rows:] + rest))[:own_rows])
    row = lax.broadcasted_iota(jnp.int32, gap_out.shape, 0) + meta[0]
    temperature = CUTOFF / freq_count
    renorm = 1.0 + temperature * summed[1] / omega_of(row, freq_count)
    gap = temperature * summed[0] / renorm
    if final:
        refs[3][...] = renorm
        gap_out[...] = gap
    else:
        gap_out[...] = encoded(gap) if coded else gap


def swapped(axis_size, bit):
    return [(i, i ^ bit) for i in range(axis_size)]


def gather_pairwise(gap):
    core = lambda value: lax.ppermute(value, "state", swapped(4, 1))
    joint = [(4 * f + s, 4 * (f ^ 1) + (s ^ 2)) for f in range(4) for s in range(4)]
    along_x = lax.ppermute(gap, "state", swapped(4, 2))
    along_z = lax.ppermute(gap, "freq", swapped(4, 1))
    diagonal = lax.ppermute(gap, ("freq", "state"), joint)
    return [
        gap,
        along_z,
        core(gap),
        core(along_z),
        along_x,
        diagonal,
        core(along_x),
        core(diagonal),
    ]


def gather_general(gap, half_groups):
    groups = lax.axis_size("state")
    everyone = lax.all_gather(gap, "state", axis=0, tiled=False)
    rows = lax.all_gather(everyone, "freq", axis=1, tiled=True)
    own_rows = gap.shape[0]
    start = (lax.axis_index("freq") // half_groups) * (half_groups * own_rows)
    half = lax.dynamic_slice_in_dim(rows, start, half_groups * own_rows, 1)
    return [half[group] for group in range(groups)]


def on_device(gap_in, coupling, pair_cols, pair_count, block_order, phonon):
    own_rows, row_width = gap_in.shape
    blocks, slots, modes, size, _ = coupling.shape
    block_count = block_order.shape[0]
    freq_groups = lax.axis_size("freq")
    groups = lax.axis_size("state")
    freq_count = own_rows * freq_groups
    half_rows = freq_count // 2
    half_groups = freq_groups // 2
    pairwise = freq_groups == 4 and groups == 4
    padded_rows = -(-own_rows // 16) * 16
    freq_at = lax.axis_index("freq")
    state_at = lax.axis_index("state")

    numbers = jnp.arange(block_count, dtype=jnp.int32)
    position = jnp.sum(
        jnp.where(block_order[None, :] == numbers[:, None], numbers[None, :], 0), axis=1
    )
    column_place = jnp.sum(
        jnp.where(pair_cols[:, :, None] == numbers[None, None, :], position[None, None, :], 0),
        axis=2,
    )
    live = (jnp.arange(slots, dtype=jnp.int32)[None, :] < pair_count[:, None]).astype(jnp.int32)
    holder = column_place // blocks
    if pairwise:
        segments = 2
        holder = holder ^ state_at
        meta = jnp.stack([freq_at, freq_at, freq_at ^ 1]) * own_rows
    else:
        segments = 1
        first = (freq_at // half_groups) * half_rows
        meta = jnp.stack([freq_at * own_rows, first, first])
    meta = meta.astype(jnp.int32)
    source = jnp.stack(
        [holder.reshape(-1), (column_place % blocks).reshape(-1), live.reshape(-1)]
    ).astype(jnp.int32)

    segment_rows = half_rows // segments
    dims = (freq_count, half_rows, segment_rows, padded_rows, modes)
    smem = pl.BlockSpec(memory_space=pltpu.SMEM)
    vmem = pl.BlockSpec(memory_space=pltpu.VMEM)
    weights, table = pl.pallas_call(
        functools.partial(tables_kernel, dims),
        out_shape=(
            jax.ShapeDtypeStruct((blocks, slots * size, modes * size), jnp.bfloat16),
            jax.ShapeDtypeStruct((2, 2 * padded_rows, modes * half_rows), jnp.bfloat16),
        ),
        in_specs=[smem, smem, vmem],
        out_specs=(vmem, vmem),
        compiler_params=pltpu.CompilerParams(vmem_limit_bytes=32 << 20),
        cost_estimate=pl.CostEstimate(flops=10_000_000, bytes_accessed=8_000_000, transcendentals=0),
        name="tables",
    )(meta, phonon, coupling)
    coded = pairwise
    link_type = jnp.int16 if coded else jnp.float32

    def step(last, pieces):
        full = jax.ShapeDtypeStruct(gap_in.shape, jnp.float32)
        passed = jax.ShapeDtypeStruct(gap_in.shape, link_type)
        return pl.pallas_call(
            functools.partial(step_kernel, dims, groups, segments, coded, last),
            out_shape=(full, full) if last else passed,
            in_specs=[smem, smem]
            + [pl.BlockSpec(memory_space=pl.ANY)] * (groups * segments)
            + [vmem, vmem],
            out_specs=(vmem, vmem) if last else vmem,
            scratch_shapes=[
                pltpu.VMEM((blocks * slots, half_rows, size), link_type),
                pltpu.VMEM((blocks, 2 * half_rows, slots * size), jnp.bfloat16),
                pltpu.VMEM((2, modes * half_rows, row_width), jnp.bfloat16),
                pltpu.VMEM((2, modes * half_rows, row_width), jnp.bfloat16),
                pltpu.SemaphoreType.DMA((blocks * slots, segments)),
            ],
            compiler_params=pltpu.CompilerParams(vmem_limit_bytes=40 << 20),
            cost_estimate=pl.CostEstimate(
                flops=3_000_000_000, bytes_accessed=8_000_000, transcendentals=0
            ),
            name="step",
        )(meta, source, *pieces, weights, table)

    passed = gap_in
    if coded:
        passed = pl.pallas_call(
            encode_kernel,
            out_shape=jax.ShapeDtypeStruct(gap_in.shape, link_type),
            in_specs=[vmem],
            out_specs=vmem,
            name="encode",
        )(gap_in)
    for iteration in range(ITERS):
        last = iteration == ITERS - 1
        pieces = gather_pairwise(passed) if pairwise else gather_general(passed, half_groups)
        passed = step(last, pieces)
    return passed


def solution(mesh):
    return jax.shard_map(
        on_device,
        mesh=mesh,
        in_specs=(
            P(("parts", "freq"), "state"),
            P(("parts", "state"), None, None, None, None),
            P(("parts", "state"), None),
            P(("parts", "state")),
            P("parts"),
            P("parts"),
        ),
        out_specs=(P(("parts", "freq"), "state"), P(("parts", "freq"), "state")),
        check_vma=False,
    )
```

```python
import functools

import jax
import jax.numpy as jnp
from jax import lax
from jax.experimental import pallas as pl
from jax.experimental.pallas import tpu as pltpu
from jax.sharding import PartitionSpec as P

ITERS = 2
CUTOFF = 4.0
LANES = 128
GAP_LIMIT = 10.0
CODE_LIMIT = 32767.0
CODE_POWER = 5
HOLDER, PLACE, LIVE, ROWS = 0, 1, 2, 3


def omega_of(index, freq_count):
    return (2.0 * index.astype(jnp.float32) + 1.0 - freq_count) * (CUTOFF / freq_count)


def encoded(gap):
    share = jnp.minimum(jnp.abs(gap) * (1.0 / GAP_LIMIT), 1.0)
    root = jnp.exp2(jnp.log2(jnp.maximum(share, 1e-37)) * (1.0 / CODE_POWER))
    code = jnp.floor(root * CODE_LIMIT + 0.5)
    return jnp.where(gap < 0, -code, code).astype(jnp.int32).astype(jnp.int16)


def decoded(code):
    root = code.astype(jnp.float32) * (1.0 / CODE_LIMIT)
    square = root * root
    return (root * GAP_LIMIT) * (square * square)


def encode_kernel(gap, code):
    code[...] = encoded(gap[...])


def split(value):
    high = value.astype(jnp.bfloat16)
    return high, (value - high.astype(jnp.float32)).astype(jnp.bfloat16)


def tables_kernel(
    dims, paired, meta, phonon, pair_cols, pair_count, block_order, coupling, plan, weights, *refs
):
    freq_count, segments, segment_rows, padded_rows, modes = dims
    tables, (held, sems) = refs[:segments], refs[segments:]
    blocks, slots = coupling.shape[:2]
    size = coupling.shape[3]

    def fetch(block):
        return pltpu.make_async_copy(coupling.at[block], held.at[block], sems.at[block])

    for block in range(blocks):
        fetch(block).start()
    for at in range(1 + segments):
        plan[ROWS, at] = meta[at]
    for block in range(blocks):
        for slot in range(slots):
            wanted = pair_cols[block, slot]
            position = jnp.int32(0)
            for at in range(block_order.shape[0]):
                position = jnp.where(block_order[at] == wanted, at, position)
            pair = block * slots + slot
            holder = position // blocks
            if paired:
                apart = holder ^ meta[1 + segments]
                holder = (apart % 2) * 2 + apart // 2
            plan[HOLDER, pair] = holder
            plan[PLACE, pair] = position % blocks
            plan[LIVE, pair] = (pair_count[block] > slot).astype(jnp.int32)
    shape = (padded_rows, segment_rows)
    row_omega = omega_of(lax.broadcasted_iota(jnp.int32, shape, 0) + meta[0], freq_count)
    for segment in range(segments):
        col = lax.broadcasted_iota(jnp.int32, shape, 1) + meta[1 + segment]
        col_omega = omega_of(col, freq_count)
        near = (row_omega - col_omega) ** 2
        far = (row_omega + col_omega) ** 2
        cross = 4.0 * (row_omega * col_omega)
        for mode in range(modes):
            strength = phonon[mode]
            below = near + strength * strength
            above = far + strength * strength
            common = (2.0 * strength) / (below * above)
            columns = slice(mode * segment_rows, (mode + 1) * segment_rows)
            for part, value in enumerate((common * (below + above), common * cross)):
                high, low = split(value)
                tables[segment][part, :padded_rows, columns] = high
                tables[segment][part, padded_rows:, columns] = low
    for block in range(blocks):
        fetch(block).wait()
        for slot in range(slots):
            for mode in range(modes):
                weights[
                    block, slot * size : (slot + 1) * size, mode * size : (mode + 1) * size
                ] = held[block, slot, mode].T


def step_kernel(dims, segment, coded, final, plan, *refs):
    freq_count, segments, segment_rows, padded_rows, modes = dims
    first, last = segment == 0, segment == segments - 1
    refs = list(refs)
    fetched, ratios, high, low = refs[-4:]
    del refs[-4:]
    outs = [refs.pop() for _ in range(2 if last and final else 1)][::-1]
    before = None if first else refs.pop()
    weights, table = refs[-2:]
    pieces = refs[:-2]
    blocks = weights.shape[0]
    size = LANES
    slots = weights.shape[1] // size
    pieces = [
        piece.at[part]
        for piece in pieces
        for part in range(piece.shape[0])
    ] if len(pieces[0].shape) == 3 else pieces
    for pair in range(blocks * slots):
        column = pl.multiple_of(plan[PLACE, pair] * size, size)
        for group, piece in enumerate(pieces):

            @pl.when(plan[HOLDER, pair] == group)
            def _():
                fetched[pair] = piece[:, pl.ds(column, size)]

    shape = (segment_rows, size)
    col = lax.broadcasted_iota(jnp.int32, shape, 0) + plan[ROWS, 1 + segment]
    col_omega = omega_of(col, freq_count)
    square = col_omega * col_omega
    for block in range(blocks):
        for slot in range(slots):
            pair = block * slots + slot
            gap = decoded(fetched[pair]) if coded else fetched[pair]
            live = plan[LIVE, pair].astype(jnp.float32)
            inverse = lax.rsqrt(square + gap * gap) * live
            lanes = slice(slot * size, (slot + 1) * size)
            ratios[block, :segment_rows, lanes] = (gap * inverse).astype(jnp.bfloat16)
            ratios[block, segment_rows:, lanes] = (col_omega * inverse).astype(jnp.bfloat16)
        lanes = slice(block * size, (block + 1) * size)
        for start in range(0, modes, 2):
            stop = min(start + 2, modes)
            terms = jnp.dot(
                ratios[block],
                weights[block, :, start * size : stop * size],
                preferred_element_type=jnp.float32,
            )
            upper, lower = split(terms)
            for mode in range(start, stop):
                rows = slice(mode * segment_rows, (mode + 1) * segment_rows)
                taken = slice((mode - start) * size, (mode - start + 1) * size)
                for part in range(2):
                    source = slice(part * segment_rows, (part + 1) * segment_rows)
                    high[part, rows, lanes] = upper[source, taken]
                    low[part, rows, lanes] = lower[source, taken]
    summed = []
    for part in range(2):
        both = jnp.dot(table[part], high[part], preferred_element_type=jnp.float32)
        rest = jnp.dot(
            table[part, :padded_rows], low[part], preferred_element_type=jnp.float32
        )
        total = both[:padded_rows] + (both[padded_rows:] + rest)
        summed.append(total if first else total + before[part])
    if not last:
        for part in range(2):
            outs[0][part] = summed[part]
        return
    own_rows = outs[0].shape[0]
    row = lax.broadcasted_iota(jnp.int32, outs[0].shape, 0) + plan[ROWS, 0]
    temperature = CUTOFF / freq_count
    renorm = 1.0 + temperature * summed[1][:own_rows] / omega_of(row, freq_count)
    gap = temperature * summed[0][:own_rows] / renorm
    if final:
        outs[1][...] = renorm
        outs[0][...] = gap
    else:
        outs[0][...] = encoded(gap) if coded else gap


def join_kernel(first, second, after, joined):
    joined[0] = first[...]
    joined[1] = second[...]


def swapped(axis_size, bit):
    return [(i, i ^ bit) for i in range(axis_size)]


def gather_pairwise(gap):
    joint = [(4 * f + s, 4 * (f ^ 1) + (s ^ 2)) for f in range(4) for s in range(4)]
    along_x = lax.ppermute(gap, "state", swapped(4, 2))
    along_z = lax.ppermute(gap, "freq", swapped(4, 1))
    diagonal = lax.ppermute(gap, ("freq", "state"), joint)
    return [[gap, along_x], [along_z, diagonal]]


def from_other_core(value):
    return lax.ppermute(value, "state", swapped(4, 1))


def gather_general(gap, half_groups):
    groups = lax.axis_size("state")
    everyone = lax.all_gather(gap, "state", axis=0, tiled=False)
    rows = lax.all_gather(everyone, "freq", axis=1, tiled=True)
    own_rows = gap.shape[0]
    start = (lax.axis_index("freq") // half_groups) * (half_groups * own_rows)
    half = lax.dynamic_slice_in_dim(rows, start, half_groups * own_rows, 1)
    return [[half[group] for group in range(groups)]]


def on_device(gap_in, coupling, pair_cols, pair_count, block_order, phonon):
    own_rows, row_width = gap_in.shape
    blocks, slots, modes, size, _ = coupling.shape
    freq_groups = lax.axis_size("freq")
    groups = lax.axis_size("state")
    freq_count = own_rows * freq_groups
    half_rows = freq_count // 2
    half_groups = freq_groups // 2
    pairwise = freq_groups == 4 and groups == 4
    padded_rows = -(-own_rows // 16) * 16
    freq_at = lax.axis_index("freq")
    if pairwise:
        segments = 2
        own = freq_at * own_rows
        meta = [own, own, (freq_at ^ 1) * own_rows, lax.axis_index("state")]
    else:
        segments = 1
        own = freq_at * own_rows
        meta = [own, (freq_at // half_groups) * half_rows]
    meta = jnp.stack([jnp.asarray(value, jnp.int32) for value in meta])
    segment_rows = half_rows // segments
    dims = (freq_count, segments, segment_rows, padded_rows, modes)
    smem = pl.BlockSpec(memory_space=pltpu.SMEM)
    vmem = pl.BlockSpec(memory_space=pltpu.VMEM)
    link_type = jnp.int16 if pairwise else jnp.float32

    passed = gap_in
    if pairwise:
        passed = pl.pallas_call(
            encode_kernel,
            out_shape=jax.ShapeDtypeStruct(gap_in.shape, link_type),
            in_specs=[vmem],
            out_specs=vmem,
            cost_estimate=pl.CostEstimate(
                flops=10_000_000_000, bytes_accessed=40_000_000, transcendentals=0
            ),
            name="encode",
        )(gap_in)

    plan, weights, *tables = pl.pallas_call(
        functools.partial(tables_kernel, dims, pairwise),
        out_shape=[
            jax.ShapeDtypeStruct((4, max(blocks * slots, 1 + segments)), jnp.int32),
            jax.ShapeDtypeStruct((blocks, slots * size, modes * size), jnp.bfloat16),
        ]
        + [jax.ShapeDtypeStruct((2, 2 * padded_rows, modes * segment_rows), jnp.bfloat16)]
        * segments,
        in_specs=[smem] * 5 + [pl.BlockSpec(memory_space=pltpu.HBM)],
        out_specs=[smem] + [vmem] * (1 + segments),
        scratch_shapes=[
            pltpu.VMEM(coupling.shape, jnp.bfloat16),
            pltpu.SemaphoreType.DMA((blocks,)),
        ],
        compiler_params=pltpu.CompilerParams(vmem_limit_bytes=32 << 20),
        cost_estimate=pl.CostEstimate(
            flops=10_000_000, bytes_accessed=8_000_000, transcendentals=0
        ),
        name="tables",
    )(meta, phonon, pair_cols, pair_count, block_order, coupling)

    def step(segment, final, pieces, before):
        full = jax.ShapeDtypeStruct(gap_in.shape, jnp.float32)
        if segment < segments - 1:
            outs = [jax.ShapeDtypeStruct((2, padded_rows, row_width), jnp.float32)]
        elif final:
            outs = [full, full]
        else:
            outs = [jax.ShapeDtypeStruct(gap_in.shape, link_type)]
        inputs = [*pieces, weights, tables[segment], *before]
        return pl.pallas_call(
            functools.partial(step_kernel, dims, segment, pairwise, final),
            out_shape=outs,
            in_specs=[smem] + [vmem] * len(inputs),
            out_specs=[vmem] * len(outs),
            scratch_shapes=[
                pltpu.VMEM((blocks * slots, segment_rows, size), link_type),
                pltpu.VMEM((blocks, 2 * segment_rows, slots * size), jnp.bfloat16),
                pltpu.VMEM((2, modes * segment_rows, row_width), jnp.bfloat16),
                pltpu.VMEM((2, modes * segment_rows, row_width), jnp.bfloat16),
            ],
            compiler_params=pltpu.CompilerParams(vmem_limit_bytes=32 << 20),
            cost_estimate=pl.CostEstimate(
                flops=1_000_000, bytes_accessed=100_000, transcendentals=0
            ),
            name="step",
        )(plan, *inputs)

    def join(near, across, after):
        return pl.pallas_call(
            join_kernel,
            out_shape=jax.ShapeDtypeStruct((2, *near.shape), near.dtype),
            in_specs=[vmem, vmem, pl.BlockSpec(memory_space=pl.ANY)],
            out_specs=vmem,
            name="join",
        )(near, across, after)

    for iteration in range(ITERS):
        final = iteration == ITERS - 1
        if pairwise:
            gathered = gather_pairwise(passed)
        else:
            gathered = gather_general(passed, half_groups)
        results = []
        for segment, pieces in enumerate(gathered):
            if pairwise and segment == 0:
                near, across = pieces
                pieces = [near, across, from_other_core(near), from_other_core(across)]
            elif pairwise:
                both = join(*pieces, *results)
                pieces = [both, from_other_core(both)]
            results = step(segment, final, pieces, results)
        passed = results[0]
    return tuple(results)


def solution(mesh):
    return jax.shard_map(
        on_device,
        mesh=mesh,
        in_specs=(
            P(("parts", "freq"), "state"),
            P(("parts", "state"), None, None, None, None),
            P(("parts", "state"), None),
            P(("parts", "state")),
            P("parts"),
            P("parts"),
        ),
        out_specs=(P(("parts", "freq"), "state"), P(("parts", "freq"), "state")),
        check_vma=False,
    )
```

```python
import functools

import jax
import jax.numpy as jnp
from jax import lax
from jax.experimental import pallas as pl
from jax.experimental.pallas import tpu as pltpu
from jax.sharding import PartitionSpec as P

ITERS = 2
CUTOFF = 4.0
LANES = 128
GAP_LIMIT = 10.0
CODE_LIMIT = 32767.0
CODE_POWER = 5
HOLDER, PLACE, LIVE, SIDE, ROWS = 0, 1, 2, 3, 4


def omega_of(index, freq_count):
    return (2.0 * index.astype(jnp.float32) + 1.0 - freq_count) * (CUTOFF / freq_count)


def encoded(gap):
    share = jnp.minimum(jnp.abs(gap) * (1.0 / GAP_LIMIT), 1.0)
    root = jnp.exp2(jnp.log2(jnp.maximum(share, 1e-37)) * (1.0 / CODE_POWER))
    code = jnp.floor(root * CODE_LIMIT + 0.5)
    return jnp.where(gap < 0, -code, code).astype(jnp.int32).astype(jnp.int16)


def decoded(code):
    root = code.astype(jnp.float32) * (1.0 / CODE_LIMIT)
    square = root * root
    return (root * GAP_LIMIT) * (square * square)


def encode_kernel(gap, codes):
    code = encoded(gap[...])
    for copy in range(codes.shape[0]):
        codes[copy] = code


def split(value):
    high = value.astype(jnp.bfloat16)
    return high, (value - high.astype(jnp.float32)).astype(jnp.bfloat16)


def tables_kernel(
    dims, meta, phonon, pair_cols, pair_count, block_order, coupling, plan, weights, table, held, sems
):
    freq_count, segments, segment_rows, padded_rows, modes, sides = dims
    blocks, slots = coupling.shape[:2]
    size = coupling.shape[3]
    half_rows = segments * segment_rows

    def fetch(block):
        return pltpu.make_async_copy(coupling.at[block], held.at[block], sems.at[block])

    for block in range(blocks):
        fetch(block).start()
    for at in range(1 + segments):
        plan[ROWS, at] = meta[at]
    for block in range(blocks):
        for slot in range(slots):
            wanted = pair_cols[block, slot]
            position = jnp.int32(0)
            for at in range(block_order.shape[0]):
                position = jnp.where(block_order[at] == wanted, at, position)
            pair = block * slots + slot
            holder = position // blocks
            plan[HOLDER, pair] = holder // sides
            plan[SIDE, pair] = (holder % sides) ^ meta[1 + segments]
            plan[PLACE, pair] = position % blocks
            plan[LIVE, pair] = (pair_count[block] > slot).astype(jnp.int32)
    shape = (padded_rows, segment_rows)
    row_omega = omega_of(lax.broadcasted_iota(jnp.int32, shape, 0) + meta[0], freq_count)
    for segment in range(segments):
        col = lax.broadcasted_iota(jnp.int32, shape, 1) + meta[1 + segment]
        col_omega = omega_of(col, freq_count)
        near = (row_omega - col_omega) ** 2
        far = (row_omega + col_omega) ** 2
        cross = 4.0 * (row_omega * col_omega)
        for mode in range(modes):
            strength = phonon[mode]
            below = near + strength * strength
            above = far + strength * strength
            common = (2.0 * strength) / (below * above)
            first = mode * half_rows + segment * segment_rows
            columns = slice(first, first + segment_rows)
            for part, value in enumerate((common * (below + above), common * cross)):
                high, low = split(value)
                table[part, :padded_rows, columns] = high
                table[part, padded_rows:, columns] = low
    for block in range(blocks):
        fetch(block).wait()
        for slot in range(slots):
            for mode in range(modes):
                weights[
                    block, slot * size : (slot + 1) * size, mode * size : (mode + 1) * size
                ] = held[block, slot, mode].T


def step_kernel(dims, coded, final, plan, *refs):
    freq_count, segments, segment_rows, padded_rows, modes, sides = dims
    pieces, (weights, table, gap_out), refs = refs[:sides], refs[sides : sides + 3], refs[sides + 3 :]
    fetched, ratios, high, low = refs[-4:]
    half_rows = segments * segment_rows
    blocks = weights.shape[0]
    size = LANES
    slots = weights.shape[1] // size
    holders = pieces[0].shape[0] // segments
    for pair in range(blocks * slots):
        column = pl.multiple_of(plan[PLACE, pair] * size, size)
        holder = plan[HOLDER, pair]
        for side, piece in enumerate(pieces):

            @pl.when(plan[SIDE, pair] == side)
            def _():
                for segment in range(segments):
                    rows = slice(segment * segment_rows, (segment + 1) * segment_rows)
                    fetched[pair, rows] = piece[
                        segment * holders + holder, :, pl.ds(column, size)
                    ]

    shape = (segment_rows, size)
    omegas = []
    for segment in range(segments):
        col = lax.broadcasted_iota(jnp.int32, shape, 0) + plan[ROWS, 1 + segment]
        omegas.append(omega_of(col, freq_count))
    col_omega = jnp.concatenate(omegas, axis=0)
    square = col_omega * col_omega
    for block in range(blocks):
        for slot in range(slots):
            pair = block * slots + slot
            gap = decoded(fetched[pair]) if coded else fetched[pair]
            live = plan[LIVE, pair].astype(jnp.float32)
            inverse = lax.rsqrt(square + gap * gap) * live
            lanes = slice(slot * size, (slot + 1) * size)
            ratios[block, :half_rows, lanes] = (gap * inverse).astype(jnp.bfloat16)
            ratios[block, half_rows:, lanes] = (col_omega * inverse).astype(jnp.bfloat16)
        lanes = slice(block * size, (block + 1) * size)
        for part in range(2):
            for start in range(0, modes, 2):
                stop = min(start + 2, modes)
                terms = jnp.dot(
                    ratios[block, part * half_rows : (part + 1) * half_rows, :],
                    weights[block, :, start * size : stop * size],
                    preferred_element_type=jnp.float32,
                )
                upper, lower = split(terms)
                for mode in range(start, stop):
                    rows = slice(mode * half_rows, (mode + 1) * half_rows)
                    taken = slice((mode - start) * size, (mode - start + 1) * size)
                    high[part, rows, lanes] = upper[:, taken]
                    low[part, rows, lanes] = lower[:, taken]
    summed = []
    for part in range(2):
        both = jnp.dot(table[part], high[part], preferred_element_type=jnp.float32)
        rest = jnp.dot(
            table[part, :padded_rows], low[part], preferred_element_type=jnp.float32
        )
        summed.append(both[:padded_rows] + (both[padded_rows:] + rest))
    own_rows, width = gap_out.shape[-2:]
    row = lax.broadcasted_iota(jnp.int32, (own_rows, width), 0) + plan[ROWS, 0]
    temperature = CUTOFF / freq_count
    renorm = 1.0 + temperature * summed[1][:own_rows] / omega_of(row, freq_count)
    gap = temperature * summed[0][:own_rows] / renorm
    if final:
        refs[0][...] = renorm
        gap_out[...] = gap
    elif coded:
        code = encoded(gap)
        for copy in range(gap_out.shape[0]):
            gap_out[copy] = code
    else:
        gap_out[...] = gap


def gather_pairwise(codes):
    chips = lax.all_to_all(codes, ("zlo", "x"), 0, 0, tiled=True)
    return [chips, lax.ppermute(chips, "core", [(0, 1), (1, 0)])]


def gather_general(gap, half_groups):
    everyone = lax.all_gather(gap, "state", axis=0, tiled=False)
    rows = lax.all_gather(everyone, "freq", axis=1, tiled=True)
    own_rows = gap.shape[0]
    start = (lax.axis_index("freq") // half_groups) * (half_groups * own_rows)
    return [lax.dynamic_slice_in_dim(rows, start, half_groups * own_rows, 1)]


def on_device(pairwise, freq_groups, gap_in, coupling, pair_cols, pair_count, block_order, phonon):
    own_rows, row_width = gap_in.shape
    blocks, slots, modes, size, _ = coupling.shape
    freq_count = own_rows * freq_groups
    half_rows = freq_count // 2
    half_groups = freq_groups // 2
    padded_rows = -(-own_rows // 16) * 16
    if pairwise:
        segments, sides = 2, 2
        half = lax.axis_index("zhi") * half_rows
        own = half + lax.axis_index("zlo") * own_rows
        meta = [own, half, half + own_rows, lax.axis_index("core")]
    else:
        segments, sides = 1, 1
        freq_at = lax.axis_index("freq")
        meta = [freq_at * own_rows, (freq_at // half_groups) * half_rows, 0]
    meta = jnp.stack([jnp.asarray(value, jnp.int32) for value in meta])
    segment_rows = half_rows // segments
    dims = (freq_count, segments, segment_rows, padded_rows, modes, sides)
    smem = pl.BlockSpec(memory_space=pltpu.SMEM)
    vmem = pl.BlockSpec(memory_space=pltpu.VMEM)
    link_type = jnp.int16 if pairwise else jnp.float32
    passed_shape = ((4,) if pairwise else ()) + gap_in.shape

    passed = gap_in
    if pairwise:
        passed = pl.pallas_call(
            encode_kernel,
            out_shape=jax.ShapeDtypeStruct(passed_shape, link_type),
            in_specs=[vmem],
            out_specs=vmem,
            compiler_params=pltpu.CompilerParams(vmem_limit_bytes=8 << 20),
            cost_estimate=pl.CostEstimate(
                flops=10_000_000_000, bytes_accessed=40_000_000, transcendentals=0
            ),
            name="encode",
        )(gap_in)

    plan, weights, table = pl.pallas_call(
        functools.partial(tables_kernel, dims),
        out_shape=[
            jax.ShapeDtypeStruct((5, max(blocks * slots, 1 + segments)), jnp.int32),
            jax.ShapeDtypeStruct((blocks, slots * size, modes * size), jnp.bfloat16),
            jax.ShapeDtypeStruct((2, 2 * padded_rows, modes * half_rows), jnp.bfloat16),
        ],
        in_specs=[smem] * 5 + [pl.BlockSpec(memory_space=pltpu.HBM)],
        out_specs=[smem, vmem, vmem],
        scratch_shapes=[
            pltpu.VMEM(coupling.shape, jnp.bfloat16),
            pltpu.SemaphoreType.DMA((blocks,)),
        ],
        compiler_params=pltpu.CompilerParams(vmem_limit_bytes=32 << 20),
        cost_estimate=pl.CostEstimate(
            flops=10_000_000, bytes_accessed=8_000_000, transcendentals=0
        ),
        name="tables",
    )(meta, phonon, pair_cols, pair_count, block_order, coupling)

    def step(final, pieces):
        full = jax.ShapeDtypeStruct(gap_in.shape, jnp.float32)
        outs = [full, full] if final else [jax.ShapeDtypeStruct(passed_shape, link_type)]
        inputs = [*pieces, weights, table]
        return pl.pallas_call(
            functools.partial(step_kernel, dims, pairwise, final),
            out_shape=outs,
            in_specs=[smem] + [vmem] * len(inputs),
            out_specs=[vmem] * len(outs),
            scratch_shapes=[
                pltpu.VMEM((blocks * slots, half_rows, size), link_type),
                pltpu.VMEM((blocks, 2 * half_rows, slots * size), jnp.bfloat16),
                pltpu.VMEM((2, modes * half_rows, row_width), jnp.bfloat16),
                pltpu.VMEM((2, modes * half_rows, row_width), jnp.bfloat16),
            ],
            compiler_params=pltpu.CompilerParams(vmem_limit_bytes=32 << 20),
            cost_estimate=pl.CostEstimate(
                flops=3_000_000_000, bytes_accessed=8_000_000, transcendentals=0
            ),
            name="step",
        )(plan, *inputs)

    for iteration in range(ITERS):
        if pairwise:
            pieces = gather_pairwise(passed)
        else:
            pieces = gather_general(passed, half_groups)
        results = step(iteration == ITERS - 1, pieces)
        passed = results[0]
    return tuple(results)


def solution(mesh):
    shape = tuple(mesh.shape[axis] for axis in ("parts", "freq", "state"))
    pairwise = shape[1:] == (4, 4)
    parts, freq, state = "parts", "freq", "state"
    if pairwise:
        names = ("parts", "zhi", "zlo", "x", "core")
        mesh = jax.sharding.Mesh(mesh.devices.reshape(shape[0], 2, 2, 2, 2), names)
        freq, state = ("zhi", "zlo"), ("x", "core")
    rows = ("parts", *freq) if pairwise else ("parts", freq)
    groups = ("parts", *state) if pairwise else ("parts", state)
    return jax.shard_map(
        functools.partial(on_device, pairwise, shape[1]),
        mesh=mesh,
        in_specs=(
            P(rows, state),
            P(groups, None, None, None, None),
            P(groups, None),
            P(groups),
            P(parts),
            P(parts),
        ),
        out_specs=(P(rows, state), P(rows, state)),
        check_vma=False,
    )
```

```python
import functools

import jax
import jax.numpy as jnp
from jax import lax
from jax.experimental import pallas as pl
from jax.experimental.pallas import tpu as pltpu
from jax.sharding import PartitionSpec as P

ITERS = 2
CUTOFF = 4.0
LANES = 128
GAP_LIMIT = 10.0
CODE_LIMIT = 32767.0
CODE_POWER = 5
STEP_FLOPS = 1_000_000
HOLDER, PLACE, LIVE, SIDE, ROWS = 0, 1, 2, 3, 4


def omega_of(index, freq_count):
    return (2.0 * index.astype(jnp.float32) + 1.0 - freq_count) * (CUTOFF / freq_count)


def encoded(gap):
    share = jnp.minimum(jnp.abs(gap) * (1.0 / GAP_LIMIT), 1.0)
    root = jnp.exp2(jnp.log2(jnp.maximum(share, 1e-37)) * (1.0 / CODE_POWER))
    code = jnp.floor(root * CODE_LIMIT + 0.5)
    return jnp.where(gap < 0, -code, code).astype(jnp.int32).astype(jnp.int16)


def decoded(code):
    root = code.astype(jnp.float32) * (1.0 / CODE_LIMIT)
    square = root * root
    return (root * GAP_LIMIT) * (square * square)


def encode_kernel(gap, code):
    code[...] = encoded(gap[...])


def join_kernel(first, second, after, joined):
    joined[0] = first[...]
    joined[1] = second[...]


def split(value):
    high = value.astype(jnp.bfloat16)
    return high, (value - high.astype(jnp.float32)).astype(jnp.bfloat16)


def tables_kernel(
    dims, sides, meta, phonon, pair_cols, pair_count, block_order, coupling, plan, weights, *tables
):
    freq_count, segments, segment_rows, padded_rows, modes = dims
    blocks, slots = coupling.shape[:2]
    size = coupling.shape[3]
    for at in range(1 + segments):
        plan[ROWS, at] = meta[at]
    for block in range(blocks):
        for slot in range(slots):
            wanted = pair_cols[block, slot]
            position = jnp.int32(0)
            for at in range(block_order.shape[0]):
                position = jnp.where(block_order[at] == wanted, at, position)
            pair = block * slots + slot
            holder = position // blocks
            plan[HOLDER, pair] = (holder // sides) ^ meta[1 + segments]
            plan[SIDE, pair] = (holder % sides) ^ meta[2 + segments]
            plan[PLACE, pair] = position % blocks
            plan[LIVE, pair] = (pair_count[block] > slot).astype(jnp.int32)
    shape = (padded_rows, segment_rows)
    row_omega = omega_of(lax.broadcasted_iota(jnp.int32, shape, 0) + meta[0], freq_count)
    for segment in range(segments):
        col = lax.broadcasted_iota(jnp.int32, shape, 1) + meta[1 + segment]
        col_omega = omega_of(col, freq_count)
        near = (row_omega - col_omega) ** 2
        far = (row_omega + col_omega) ** 2
        cross = 4.0 * (row_omega * col_omega)
        for mode in range(modes):
            strength = phonon[mode]
            below = near + strength * strength
            above = far + strength * strength
            common = (2.0 * strength) / (below * above)
            columns = slice(mode * segment_rows, (mode + 1) * segment_rows)
            for part, value in enumerate((common * (below + above), common * cross)):
                high, low = split(value)
                tables[segment][part, :padded_rows, columns] = high
                tables[segment][part, padded_rows:, columns] = low
    for block in range(blocks):
        for slot in range(slots):
            for mode in range(modes):
                weights[
                    block, slot * size : (slot + 1) * size, mode * size : (mode + 1) * size
                ] = coupling[block, slot, mode].T


def step_kernel(dims, segment, sides, coded, final, plan, *refs):
    freq_count, segments, segment_rows, padded_rows, modes = dims
    refs = list(refs)
    ratios, high, low = refs[-3:]
    first, last = segment == 0, segment == segments - 1
    outs = refs[-5:-3] if last and final else refs[-4:-3]
    inputs = refs[: -3 - len(outs)]
    before = None if first else inputs.pop()
    weights, table = inputs[-2:]
    pieces = []
    for piece in inputs[:-2]:
        if len(piece.shape) == 3:
            pieces += [piece.at[at] for at in range(piece.shape[0])]
        else:
            pieces.append(piece)
    holders = len(pieces) // sides
    blocks = weights.shape[0]
    size = LANES
    slots = weights.shape[1] // size
    shape = (segment_rows, size)
    col = lax.broadcasted_iota(jnp.int32, shape, 0) + plan[ROWS, 1 + segment]
    col_omega = omega_of(col, freq_count)
    square = col_omega * col_omega

    def fetch(pair):
        column = pl.multiple_of(plan[PLACE, pair] * size, size)
        wanted = plan[SIDE, pair] * holders + plan[HOLDER, pair]
        value = pieces[0][:, pl.ds(column, size)]
        for at in range(1, len(pieces)):
            value = lax.select(wanted == at, pieces[at][:, pl.ds(column, size)], value)
        return decoded(value) if coded else value

    def find_ratios(block):
        for slot in range(slots):
            pair = block * slots + slot
            gap = fetch(pair)
            live = plan[LIVE, pair].astype(jnp.float32)
            inverse = lax.rsqrt(square + gap * gap) * live
            lanes = slice(slot * size, (slot + 1) * size)
            ratios[block, :segment_rows, lanes] = (gap * inverse).astype(jnp.bfloat16)
            ratios[block, segment_rows:, lanes] = (col_omega * inverse).astype(jnp.bfloat16)

    def find_terms(block):
        lanes = slice(block * size, (block + 1) * size)
        for start in range(0, modes, 2):
            stop = min(start + 2, modes)
            terms = jnp.dot(
                ratios[block],
                weights[block, :, start * size : stop * size],
                preferred_element_type=jnp.float32,
            )
            upper, lower = split(terms)
            for mode in range(start, stop):
                rows = slice(mode * segment_rows, (mode + 1) * segment_rows)
                taken = slice((mode - start) * size, (mode - start + 1) * size)
                for part in range(2):
                    source = slice(part * segment_rows, (part + 1) * segment_rows)
                    high[part, rows, lanes] = upper[source, taken]
                    low[part, rows, lanes] = lower[source, taken]

    def find_sums(lanes):
        sums = []
        for part in range(2):
            both = jnp.dot(
                table[part], high[part, :, lanes], preferred_element_type=jnp.float32
            )
            rest = jnp.dot(
                table[part, :padded_rows],
                low[part, :, lanes],
                preferred_element_type=jnp.float32,
            )
            total = both[:padded_rows] + (both[padded_rows:] + rest)
            sums.append(total if first else total + before[part, :, lanes])
        if not last:
            for part in range(2):
                outs[0][part, :, lanes] = sums[part]
            return
        own_rows = outs[0].shape[0]
        width = lanes.stop - lanes.start
        row = lax.broadcasted_iota(jnp.int32, (own_rows, width), 0) + plan[ROWS, 0]
        temperature = CUTOFF / freq_count
        renorm = 1.0 + temperature * sums[1][:own_rows] / omega_of(row, freq_count)
        gap = temperature * sums[0][:own_rows] / renorm
        if final:
            outs[1][:, lanes] = renorm
            outs[0][:, lanes] = gap
        else:
            outs[0][:, lanes] = encoded(gap) if coded else gap

    for block in range(blocks):
        find_ratios(block)
    for block in range(blocks):
        find_terms(block)
        if block % 2 == 1 and block > 1:
            find_sums(slice((block - 3) * size, (block - 1) * size))
    find_sums(slice((blocks - 2) * size, blocks * size))


SWAP = [(0, 1), (1, 0)]


def gather_general(gap, half_groups):
    everyone = lax.all_gather(gap, "state", axis=0, tiled=False)
    rows = lax.all_gather(everyone, "freq", axis=1, tiled=True)
    own_rows = gap.shape[0]
    start = (lax.axis_index("freq") // half_groups) * (half_groups * own_rows)
    return [lax.dynamic_slice_in_dim(rows, start, half_groups * own_rows, 1)]


def on_device(pairwise, freq_groups, gap_in, coupling, pair_cols, pair_count, block_order, phonon):
    own_rows, row_width = gap_in.shape
    blocks, slots, modes, size, _ = coupling.shape
    freq_count = own_rows * freq_groups
    half_rows = freq_count // 2
    half_groups = freq_groups // 2
    padded_rows = -(-own_rows // 16) * 16
    if pairwise:
        segments, sides = 2, 2
        half = lax.axis_index("zhi") * half_rows
        own = half + lax.axis_index("zlo") * own_rows
        other = half + (1 - lax.axis_index("zlo")) * own_rows
        meta = [own, own, other, lax.axis_index("x"), lax.axis_index("core")]
    else:
        segments, sides = 1, 1
        freq_at = lax.axis_index("freq")
        meta = [freq_at * own_rows, (freq_at // half_groups) * half_rows, 0, 0]
    meta = jnp.stack([jnp.asarray(value, jnp.int32) for value in meta])
    segment_rows = half_rows // segments
    dims = (freq_count, segments, segment_rows, padded_rows, modes)
    smem = pl.BlockSpec(memory_space=pltpu.SMEM)
    vmem = pl.BlockSpec(memory_space=pltpu.VMEM)
    link_type = jnp.int16 if pairwise else jnp.float32

    passed = gap_in
    if pairwise:
        passed = pl.pallas_call(
            encode_kernel,
            out_shape=jax.ShapeDtypeStruct(gap_in.shape, link_type),
            in_specs=[vmem],
            out_specs=vmem,
            compiler_params=pltpu.CompilerParams(vmem_limit_bytes=8 << 20),
            cost_estimate=pl.CostEstimate(
                flops=10_000_000_000, bytes_accessed=40_000_000, transcendentals=0
            ),
            name="encode",
        )(gap_in)

    plan, weights, *tables = pl.pallas_call(
        functools.partial(tables_kernel, dims, sides),
        out_shape=[
            jax.ShapeDtypeStruct((5, max(blocks * slots, 1 + segments)), jnp.int32),
            jax.ShapeDtypeStruct((blocks, slots * size, modes * size), jnp.bfloat16),
        ]
        + [jax.ShapeDtypeStruct((2, 2 * padded_rows, modes * segment_rows), jnp.bfloat16)]
        * segments,
        in_specs=[smem] * 5 + [vmem],
        out_specs=[smem] + [vmem] * (1 + segments),
        compiler_params=pltpu.CompilerParams(vmem_limit_bytes=24 << 20),
        cost_estimate=pl.CostEstimate(
            flops=10_000_000, bytes_accessed=8_000_000, transcendentals=0
        ),
        name="tables",
    )(meta, phonon, pair_cols, pair_count, block_order, coupling)

    def step(plan, segment, final, pieces, before):
        full = jax.ShapeDtypeStruct(gap_in.shape, jnp.float32)
        if segment < segments - 1:
            outs = [jax.ShapeDtypeStruct((2, padded_rows, row_width), jnp.float32)]
        elif final:
            outs = [full, full]
        else:
            outs = [jax.ShapeDtypeStruct(gap_in.shape, link_type)]
        inputs = [*pieces, weights, tables[segment], *before]
        return pl.pallas_call(
            functools.partial(step_kernel, dims, segment, sides, pairwise, final),
            out_shape=outs,
            in_specs=[smem] + [vmem] * len(inputs),
            out_specs=[vmem] * len(outs),
            scratch_shapes=[
                pltpu.VMEM((blocks, 2 * segment_rows, slots * size), jnp.bfloat16),
                pltpu.VMEM((2, modes * segment_rows, row_width), jnp.bfloat16),
                pltpu.VMEM((2, modes * segment_rows, row_width), jnp.bfloat16),
            ],
            compiler_params=pltpu.CompilerParams(vmem_limit_bytes=24 << 20),
            cost_estimate=pl.CostEstimate(
                flops=STEP_FLOPS, bytes_accessed=100_000, transcendentals=0
            ),
            name="step",
        )(plan, *inputs)

    def join(near, across, after):
        return pl.pallas_call(
            join_kernel,
            out_shape=jax.ShapeDtypeStruct((2, *near.shape), near.dtype),
            in_specs=[vmem, vmem, pl.BlockSpec(memory_space=pl.ANY)],
            out_specs=vmem,
            compiler_params=pltpu.CompilerParams(vmem_limit_bytes=4 << 20),
            cost_estimate=pl.CostEstimate(flops=1000, bytes_accessed=1000, transcendentals=0),
            name="join",
        )(near, across, after)

    for iteration in range(ITERS):
        final = iteration == ITERS - 1
        if not pairwise:
            results = step(plan, 0, final, gather_general(passed, half_groups), [])
        else:
            along_x = lax.ppermute(passed, "x", SWAP)
            along_z = lax.ppermute(passed, "zlo", SWAP)
            if iteration == 0:
                along_x, plan = lax.optimization_barrier((along_x, plan))
            relayed = lax.ppermute(along_z, "x", SWAP)
            near = [passed, along_x]
            pieces = near + [lax.ppermute(piece, "core", SWAP) for piece in near]
            results = step(plan, 0, final, pieces, [])
            far = join(along_z, relayed, *results)
            results = step(plan, 1, final, [far, lax.ppermute(far, "core", SWAP)], results)
        passed = results[0]
    return tuple(results)


def solution(mesh):
    shape = tuple(mesh.shape[axis] for axis in ("parts", "freq", "state"))
    pairwise = shape[1:] == (4, 4)
    parts, freq, state = "parts", "freq", "state"
    if pairwise:
        names = ("parts", "zhi", "zlo", "x", "core")
        mesh = jax.sharding.Mesh(mesh.devices.reshape(shape[0], 2, 2, 2, 2), names)
        freq, state = ("zhi", "zlo"), ("x", "core")
    rows = ("parts", *freq) if pairwise else ("parts", freq)
    groups = ("parts", *state) if pairwise else ("parts", state)
    return jax.shard_map(
        functools.partial(on_device, pairwise, shape[1]),
        mesh=mesh,
        in_specs=(
            P(rows, state),
            P(groups, None, None, None, None),
            P(groups, None),
            P(groups),
            P(parts),
            P(parts),
        ),
        out_specs=(P(rows, state), P(rows, state)),
        check_vma=False,
    )
```

```python
import functools

import jax
import jax.numpy as jnp
from jax import lax
from jax.experimental import pallas as pl
from jax.experimental.pallas import tpu as pltpu
from jax.sharding import PartitionSpec as P

ITERS = 2
CUTOFF = 4.0
LANES = 128
GAP_LIMIT = 10.0
CODE_LIMIT = 32767.0
CODE_POWER = 5
STEP_FLOPS = 1_000_000
HOLDER, PLACE, LIVE, SIDE, ROWS = 0, 1, 2, 3, 4


def omega_of(index, freq_count):
    return (2.0 * index.astype(jnp.float32) + 1.0 - freq_count) * (CUTOFF / freq_count)


def encoded(gap):
    share = jnp.minimum(jnp.abs(gap) * (1.0 / GAP_LIMIT), 1.0)
    root = jnp.exp2(jnp.log2(jnp.maximum(share, 1e-37)) * (1.0 / CODE_POWER))
    code = jnp.floor(root * CODE_LIMIT + 0.5)
    return jnp.where(gap < 0, -code, code).astype(jnp.int32).astype(jnp.int16)


def decoded(code):
    root = code.astype(jnp.float32) * (1.0 / CODE_LIMIT)
    square = root * root
    return (root * GAP_LIMIT) * (square * square)


def encode_kernel(gap, code):
    code[...] = encoded(gap[...])


def join_kernel(first, second, after, joined):
    joined[0] = first[...]
    joined[1] = second[...]


def split(value):
    high = value.astype(jnp.bfloat16)
    return high, (value - high.astype(jnp.float32)).astype(jnp.bfloat16)


def fill_tables(dims, meta, row_from, phonon, tables):
    freq_count, segments, segment_rows, padded_rows, modes = dims
    shape = (padded_rows, segment_rows)
    row_omega = omega_of(lax.broadcasted_iota(jnp.int32, shape, 0) + meta[row_from], freq_count)
    for segment in range(len(tables)):
        col = lax.broadcasted_iota(jnp.int32, shape, 1) + meta[1 + segment]
        col_omega = omega_of(col, freq_count)
        near = (row_omega - col_omega) ** 2
        far = (row_omega + col_omega) ** 2
        cross = 4.0 * (row_omega * col_omega)
        for mode in range(modes):
            strength = phonon[mode]
            below = near + strength * strength
            above = far + strength * strength
            common = (2.0 * strength) / (below * above)
            columns = slice(mode * segment_rows, (mode + 1) * segment_rows)
            for part, value in enumerate((common * (below + above), common * cross)):
                high, low = split(value)
                tables[segment][part, :padded_rows, columns] = high
                tables[segment][part, padded_rows:, columns] = low


def other_tables_kernel(dims, meta, phonon, *tables):
    fill_tables(dims, meta, 2, phonon, tables)


def tables_kernel(
    dims, sides, meta, phonon, pair_cols, pair_count, block_order, coupling, plan, weights, *tables
):
    freq_count, segments, segment_rows, padded_rows, modes = dims
    blocks, slots = coupling.shape[:2]
    size = coupling.shape[3]
    for at in range(1 + segments):
        plan[ROWS, at] = meta[at]
    for block in range(blocks):
        for slot in range(slots):
            wanted = pair_cols[block, slot]
            position = jnp.int32(0)
            for at in range(block_order.shape[0]):
                position = jnp.where(block_order[at] == wanted, at, position)
            pair = block * slots + slot
            holder = position // blocks
            plan[HOLDER, pair] = (holder // sides) ^ meta[1 + segments]
            plan[SIDE, pair] = (holder % sides) ^ meta[2 + segments]
            plan[PLACE, pair] = position % blocks
            plan[LIVE, pair] = (pair_count[block] > slot).astype(jnp.int32)
    fill_tables(dims, meta, 0, phonon, tables)
    for block in range(blocks):
        for slot in range(slots):
            for mode in range(modes):
                weights[
                    block, slot * size : (slot + 1) * size, mode * size : (mode + 1) * size
                ] = coupling[block, slot, mode].T


def step_kernel(dims, segment, span, sides, coded, final, keep, parted, plan, *refs):
    freq_count, segments, segment_rows, padded_rows, modes = dims
    refs = list(refs)
    first, last = segment == 0, segment == segments - 1
    take = lambda count: [refs.pop() for _ in range(count)][::-1]
    copied = last and final
    if copied:
        *held, sems = take(3)
    high, low = (None, None) if keep else take(2)
    ratios = refs.pop()
    if keep:
        high, low = take(2)
    outs = take(2 if copied else 1)
    inputs = refs
    before = [inputs.pop() for _ in range(0 if first else parted)][::-1]
    weights, table = inputs[-2:]
    pieces = []
    for piece in inputs[:-2]:
        if len(piece.shape) == 3:
            pieces += [piece.at[at] for at in range(piece.shape[0])]
        else:
            pieces.append(piece)
    holders = len(pieces) // sides
    blocks = span[1] - span[0]
    size = LANES
    slots = weights.shape[1] // size
    shape = (segment_rows, size)
    col = lax.broadcasted_iota(jnp.int32, shape, 0) + plan[ROWS, 1 + segment]
    col_omega = omega_of(col, freq_count)
    square = col_omega * col_omega

    def fetch(pair):
        column = pl.multiple_of(plan[PLACE, pair] * size, size)
        wanted = plan[SIDE, pair] * holders + plan[HOLDER, pair]
        value = pieces[0][:, pl.ds(column, size)]
        for at in range(1, len(pieces)):
            value = lax.select(wanted == at, pieces[at][:, pl.ds(column, size)], value)
        return decoded(value) if coded else value

    def find_ratios(block):
        for slot in range(slots):
            pair = (span[0] + block) * slots + slot
            gap = fetch(pair)
            live = plan[LIVE, pair].astype(jnp.float32)
            inverse = lax.rsqrt(square + gap * gap) * live
            lanes = slice(slot * size, (slot + 1) * size)
            ratios[block, :segment_rows, lanes] = (gap * inverse).astype(jnp.bfloat16)
            ratios[block, segment_rows:, lanes] = (col_omega * inverse).astype(jnp.bfloat16)

    def find_terms(block):
        lanes = slice(block * size, (block + 1) * size)
        for start in range(0, modes, 2):
            stop = min(start + 2, modes)
            terms = jnp.dot(
                ratios[block],
                weights[span[0] + block, :, start * size : stop * size],
                preferred_element_type=jnp.float32,
            )
            upper, lower = split(terms)
            for mode in range(start, stop):
                rows = slice(mode * segment_rows, (mode + 1) * segment_rows)
                taken = slice((mode - start) * size, (mode - start + 1) * size)
                for part in range(2):
                    source = slice(part * segment_rows, (part + 1) * segment_rows)
                    high[part, rows, lanes] = upper[source, taken]
                    low[part, rows, lanes] = lower[source, taken]

    def earlier(part, lanes):
        width = before[0].shape[-1]
        start = lanes.start % width
        return before[lanes.start // width][part, :, start : start + lanes.stop - lanes.start]

    def find_sums(lanes):
        sums = []
        for part in range(2):
            both = jnp.dot(
                table[part], high[part, :, lanes], preferred_element_type=jnp.float32
            )
            rest = jnp.dot(
                table[part, :padded_rows],
                low[part, :, lanes],
                preferred_element_type=jnp.float32,
            )
            total = both[:padded_rows] + (both[padded_rows:] + rest)
            sums.append(total if first else total + earlier(part, lanes))
        if not last:
            for part in range(2):
                outs[0][part, :, lanes] = sums[part]
            return
        own_rows = outs[0].shape[0]
        width = lanes.stop - lanes.start
        row = lax.broadcasted_iota(jnp.int32, (own_rows, width), 0) + plan[ROWS, 0]
        temperature = CUTOFF / freq_count
        renorm = 1.0 + temperature * sums[1][:own_rows] / omega_of(row, freq_count)
        gap = temperature * sums[0][:own_rows] / renorm
        if not final:
            outs[0][:, lanes] = encoded(gap) if coded else gap
            return
        for at, value in enumerate((gap, renorm)):
            held[at][:, lanes] = value
            copy_out(at, lanes).start()

    def copy_out(at, lanes):
        width = lanes.stop - lanes.start
        return pltpu.make_async_copy(
            held[at].at[:, pl.ds(lanes.start, width)],
            outs[at].at[:, pl.ds(lanes.start, width)],
            sems.at[at, lanes.start // width],
        )

    halves = [slice(start * size, (start + 2) * size) for start in range(0, blocks, 2)]
    for block in range(blocks):
        find_ratios(block)
    for block in range(blocks):
        find_terms(block)
        if block % 2 == 1 and block > 1:
            find_sums(halves[block // 2 - 1])
    find_sums(halves[-1])
    if copied:
        for lanes in halves:
            for at in range(2):
                copy_out(at, lanes).wait()


def other_rows_kernel(dims, plan, *refs):
    freq_count, segments, segment_rows, padded_rows, modes = dims
    tables, terms, code = refs[:segments], refs[segments:-1], refs[-1]
    sums = []
    for part in range(2):
        total = None
        for segment in range(segments):
            table, high, low = tables[segment], terms[2 * segment], terms[2 * segment + 1]
            both = jnp.dot(table[part], high[part], preferred_element_type=jnp.float32)
            rest = jnp.dot(
                table[part, :padded_rows], low[part], preferred_element_type=jnp.float32
            )
            piece = both[:padded_rows] + (both[padded_rows:] + rest)
            total = piece if total is None else total + piece
        sums.append(total)
    row = lax.broadcasted_iota(jnp.int32, code.shape, 0) + plan[ROWS, 2]
    temperature = CUTOFF / freq_count
    renorm = 1.0 + temperature * sums[1] / omega_of(row, freq_count)
    code[...] = encoded(temperature * sums[0] / renorm)


SWAP = [(0, 1), (1, 0)]


def gather_general(gap, half_groups):
    everyone = lax.all_gather(gap, "state", axis=0, tiled=False)
    rows = lax.all_gather(everyone, "freq", axis=1, tiled=True)
    own_rows = gap.shape[0]
    start = (lax.axis_index("freq") // half_groups) * (half_groups * own_rows)
    return [lax.dynamic_slice_in_dim(rows, start, half_groups * own_rows, 1)]


def on_device(pairwise, freq_groups, gap_in, coupling, pair_cols, pair_count, block_order, phonon):
    own_rows, row_width = gap_in.shape
    blocks, slots, modes, size, _ = coupling.shape
    freq_count = own_rows * freq_groups
    half_rows = freq_count // 2
    half_groups = freq_groups // 2
    padded_rows = -(-own_rows // 16) * 16
    if pairwise:
        segments, sides = 2, 2
        half = lax.axis_index("zhi") * half_rows
        own = half + lax.axis_index("zlo") * own_rows
        other = half + (1 - lax.axis_index("zlo")) * own_rows
        meta = [own, own, other, lax.axis_index("x"), lax.axis_index("core")]
    else:
        segments, sides = 1, 1
        freq_at = lax.axis_index("freq")
        meta = [freq_at * own_rows, (freq_at // half_groups) * half_rows, 0, 0]
    meta = jnp.stack([jnp.asarray(value, jnp.int32) for value in meta])
    segment_rows = half_rows // segments
    dims = (freq_count, segments, segment_rows, padded_rows, modes)
    smem = pl.BlockSpec(memory_space=pltpu.SMEM)
    vmem = pl.BlockSpec(memory_space=pltpu.VMEM)
    link_type = jnp.int16 if pairwise else jnp.float32

    passed = gap_in
    if pairwise:
        passed = pl.pallas_call(
            encode_kernel,
            out_shape=jax.ShapeDtypeStruct(gap_in.shape, link_type),
            in_specs=[vmem],
            out_specs=vmem,
            compiler_params=pltpu.CompilerParams(vmem_limit_bytes=8 << 20),
            cost_estimate=pl.CostEstimate(
                flops=10_000_000_000, bytes_accessed=40_000_000, transcendentals=0
            ),
            name="encode",
        )(gap_in)

    table_shape = jax.ShapeDtypeStruct(
        (2, 2 * padded_rows, modes * segment_rows), jnp.bfloat16
    )
    plan, weights, *tables = pl.pallas_call(
        functools.partial(tables_kernel, dims, sides),
        out_shape=[
            jax.ShapeDtypeStruct((5, max(blocks * slots, 1 + segments)), jnp.int32),
            jax.ShapeDtypeStruct((blocks, slots * size, modes * size), jnp.bfloat16),
        ]
        + [table_shape] * segments,
        in_specs=[smem] * 5 + [vmem],
        out_specs=[smem] + [vmem] * (1 + segments),
        compiler_params=pltpu.CompilerParams(vmem_limit_bytes=24 << 20),
        cost_estimate=pl.CostEstimate(
            flops=10_000_000, bytes_accessed=8_000_000, transcendentals=0
        ),
        name="tables",
    )(meta, phonon, pair_cols, pair_count, block_order, coupling)

    full = jax.ShapeDtypeStruct(gap_in.shape, jnp.float32)
    passed_out = jax.ShapeDtypeStruct(gap_in.shape, link_type)
    step_params = dict(
        compiler_params=pltpu.CompilerParams(vmem_limit_bytes=24 << 20),
        cost_estimate=pl.CostEstimate(
            flops=STEP_FLOPS, bytes_accessed=100_000, transcendentals=0
        ),
    )

    def step(plan, segment, final, pieces, before, keep=False, span=(0, blocks)):
        copied = final and segment == segments - 1
        width = (span[1] - span[0]) * size
        terms_shape = (2, modes * segment_rows, width)
        if segment < segments - 1:
            outs = [jax.ShapeDtypeStruct((2, padded_rows, width), jnp.float32)]
        else:
            outs = [full, full] if final else [passed_out]
        out_specs = [pl.BlockSpec(memory_space=pl.ANY) if copied else vmem] * len(outs)
        scratch = [pltpu.VMEM((span[1] - span[0], 2 * segment_rows, slots * size), jnp.bfloat16)]
        if keep:
            outs += [jax.ShapeDtypeStruct(terms_shape, jnp.bfloat16)] * 2
            out_specs += [vmem] * 2
        else:
            scratch += [pltpu.VMEM(terms_shape, jnp.bfloat16)] * 2
        if copied:
            scratch += [pltpu.VMEM(gap_in.shape, jnp.float32)] * 2
            scratch += [pltpu.SemaphoreType.DMA((2, blocks // 2))]
        inputs = [*pieces, weights, tables[segment], *before]
        return pl.pallas_call(
            functools.partial(
                step_kernel, dims, segment, span, sides, pairwise, final, keep, len(before)
            ),
            out_shape=outs,
            in_specs=[smem] + [vmem] * len(inputs),
            out_specs=out_specs,
            scratch_shapes=scratch,
            name="step",
            **step_params,
        )(plan, *inputs)

    if not pairwise:
        for iteration in range(ITERS):
            final = iteration == ITERS - 1
            results = step(plan, 0, final, gather_general(passed, half_groups), [])
            passed = results[0]
        return tuple(results)

    def join(near, across, after):
        return pl.pallas_call(
            join_kernel,
            out_shape=jax.ShapeDtypeStruct((2, *near.shape), near.dtype),
            in_specs=[vmem, vmem, pl.BlockSpec(memory_space=pl.ANY)],
            out_specs=vmem,
            compiler_params=pltpu.CompilerParams(vmem_limit_bytes=4 << 20),
            cost_estimate=pl.CostEstimate(flops=1000, bytes_accessed=1000, transcendentals=0),
            name="join",
        )(near, across, after)

    def with_core(near):
        return near + [lax.ppermute(piece, "core", SWAP) for piece in near]

    other_tables = pl.pallas_call(
        functools.partial(other_tables_kernel, dims),
        out_shape=[table_shape] * segments,
        in_specs=[smem, smem],
        out_specs=[vmem] * segments,
        compiler_params=pltpu.CompilerParams(vmem_limit_bytes=12 << 20),
        cost_estimate=pl.CostEstimate(
            flops=10_000_000, bytes_accessed=3_000_000, transcendentals=0
        ),
        name="other_tables",
    )(meta, phonon)
    along_x = lax.ppermute(passed, "x", SWAP)
    along_z = lax.ppermute(passed, "zlo", SWAP)
    along_x, plan = lax.optimization_barrier((along_x, plan))
    relayed = lax.ppermute(along_z, "x", SWAP)
    partial, *near_terms = step(plan, 0, False, with_core([passed, along_x]), [], keep=True)
    far = join(along_z, relayed, partial)
    pieces = [far, lax.ppermute(far, "core", SWAP)]
    plan, *other_tables = lax.optimization_barrier((plan, *other_tables))
    own, *far_terms = step(plan, 1, False, pieces, [partial], keep=True)
    inputs = [*other_tables, *near_terms, *far_terms]
    other = pl.pallas_call(
        functools.partial(other_rows_kernel, dims),
        out_shape=passed_out,
        in_specs=[smem] + [vmem] * len(inputs),
        out_specs=vmem,
        name="other_rows",
        **step_params,
    )(plan, *inputs)
    along_x, other = lax.optimization_barrier((lax.ppermute(own, "x", SWAP), other))
    near = with_core([own, along_x])
    middle = blocks // 2
    partial = step(plan, 0, True, near, [], span=(0, middle))
    far = join(other, lax.ppermute(other, "x", SWAP), *partial)
    partial += step(plan, 0, True, near, [], span=(middle, blocks))
    return tuple(step(plan, 1, True, [far, lax.ppermute(far, "core", SWAP)], partial))


def solution(mesh):
    shape = tuple(mesh.shape[axis] for axis in ("parts", "freq", "state"))
    pairwise = shape[1:] == (4, 4)
    parts, freq, state = "parts", "freq", "state"
    if pairwise:
        names = ("parts", "zhi", "zlo", "x", "core")
        mesh = jax.sharding.Mesh(mesh.devices.reshape(shape[0], 2, 2, 2, 2), names)
        freq, state = ("zhi", "zlo"), ("x", "core")
    rows = ("parts", *freq) if pairwise else ("parts", freq)
    groups = ("parts", *state) if pairwise else ("parts", state)
    return jax.shard_map(
        functools.partial(on_device, pairwise, shape[1]),
        mesh=mesh,
        in_specs=(
            P(rows, state),
            P(groups, None, None, None, None),
            P(groups, None),
            P(groups),
            P(parts),
            P(parts),
        ),
        out_specs=(P(rows, state), P(rows, state)),
        check_vma=False,
    )
```

```python
import functools

import jax
import jax.numpy as jnp
from jax import lax
from jax.experimental import pallas as pl
from jax.experimental.pallas import tpu as pltpu
from jax.sharding import PartitionSpec as P

ITERS = 2
CUTOFF = 4.0
LANES = 128
GAP_LIMIT = 10.0
CODE_LIMIT = 32767.0
CODE_POWER = 5
STEP_FLOPS = 1_000_000
SPARE_ROWS = 16
HOLDER, PLACE, LIVE, SIDE, ROWS = 0, 1, 2, 3, 4


def omega_of(index, freq_count):
    return (2.0 * index.astype(jnp.float32) + 1.0 - freq_count) * (CUTOFF / freq_count)


def encoded(gap):
    share = jnp.minimum(jnp.abs(gap) * (1.0 / GAP_LIMIT), 1.0)
    root = jnp.exp2(jnp.log2(jnp.maximum(share, 1e-37)) * (1.0 / CODE_POWER))
    code = jnp.floor(root * CODE_LIMIT + 0.5)
    return jnp.where(gap < 0, -code, code).astype(jnp.int32).astype(jnp.int16)


def decoded(code):
    root = code.astype(jnp.float32) * (1.0 / CODE_LIMIT)
    square = root * root
    return (root * GAP_LIMIT) * (square * square)


def encode_kernel(gap, code, *longer):
    code[...] = encoded(gap[...])
    for other in longer:
        other[: code.shape[0]] = code[...]
        other[code.shape[0] :] = jnp.zeros((SPARE_ROWS, code.shape[1]), code.dtype)


def join_kernel(first, second, after, joined):
    rows = joined.shape[1]
    joined[0] = first[:rows]
    joined[1] = second[:rows]


def split(value):
    high = value.astype(jnp.bfloat16)
    return high, (value - high.astype(jnp.float32)).astype(jnp.bfloat16)


def fill_tables(dims, meta, row_from, phonon, tables):
    freq_count, segments, segment_rows, padded_rows, modes = dims
    shape = (padded_rows, segment_rows)
    row_omega = omega_of(lax.broadcasted_iota(jnp.int32, shape, 0) + meta[row_from], freq_count)
    for segment in range(len(tables)):
        col = lax.broadcasted_iota(jnp.int32, shape, 1) + meta[1 + segment]
        col_omega = omega_of(col, freq_count)
        near = (row_omega - col_omega) ** 2
        far = (row_omega + col_omega) ** 2
        cross = 4.0 * (row_omega * col_omega)
        for mode in range(modes):
            strength = phonon[mode]
            below = near + strength * strength
            above = far + strength * strength
            common = (2.0 * strength) / (below * above)
            columns = slice(mode * segment_rows, (mode + 1) * segment_rows)
            for part, value in enumerate((common * (below + above), common * cross)):
                high, low = split(value)
                tables[segment][part, :padded_rows, columns] = high
                tables[segment][part, padded_rows:, columns] = low


def other_tables_kernel(dims, meta, phonon, *tables):
    fill_tables(dims, meta, 2, phonon, tables)


def tables_kernel(
    dims, sides, meta, phonon, pair_cols, pair_count, block_order, coupling, plan, weights, *tables
):
    freq_count, segments, segment_rows, padded_rows, modes = dims
    blocks, slots = coupling.shape[:2]
    size = coupling.shape[3]
    for at in range(1 + segments):
        plan[ROWS, at] = meta[at]
    for block in range(blocks):
        for slot in range(slots):
            wanted = pair_cols[block, slot]
            position = jnp.int32(0)
            for at in range(block_order.shape[0]):
                position = jnp.where(block_order[at] == wanted, at, position)
            pair = block * slots + slot
            holder = position // blocks
            plan[HOLDER, pair] = (holder // sides) ^ meta[1 + segments]
            plan[SIDE, pair] = (holder % sides) ^ meta[2 + segments]
            plan[PLACE, pair] = position % blocks
            plan[LIVE, pair] = (pair_count[block] > slot).astype(jnp.int32)
    fill_tables(dims, meta, 0, phonon, tables)
    for block in range(blocks):
        for slot in range(slots):
            for mode in range(modes):
                weights[
                    block, slot * size : (slot + 1) * size, mode * size : (mode + 1) * size
                ] = coupling[block, slot, mode].T


def step_kernel(dims, segment, span, sides, coded, final, keep, parted, plan, *refs):
    freq_count, segments, segment_rows, padded_rows, modes = dims
    refs = list(refs)
    first, last = segment == 0, segment == segments - 1
    take = lambda count: [refs.pop() for _ in range(count)][::-1]
    copied = last and final
    if copied:
        *held, sems = take(3)
    high, low = (None, None) if keep else take(2)
    ratios = refs.pop()
    if keep:
        high, low = take(2)
    outs = take(2 if copied else 1)
    inputs = refs
    before = [inputs.pop() for _ in range(0 if first else parted)][::-1]
    weights, table = inputs[-2:]
    pieces = []
    for piece in inputs[:-2]:
        if len(piece.shape) == 3:
            pieces += [piece.at[at] for at in range(piece.shape[0])]
        else:
            pieces.append(piece)
    holders = len(pieces) // sides
    blocks = span[1] - span[0]
    size = LANES
    slots = weights.shape[1] // size
    shape = (segment_rows, size)
    col = lax.broadcasted_iota(jnp.int32, shape, 0) + plan[ROWS, 1 + segment]
    col_omega = omega_of(col, freq_count)
    square = col_omega * col_omega

    def fetch(pair):
        column = pl.multiple_of(plan[PLACE, pair] * size, size)
        wanted = plan[SIDE, pair] * holders + plan[HOLDER, pair]
        value = pieces[0][:, pl.ds(column, size)]
        for at in range(1, len(pieces)):
            value = lax.select(wanted == at, pieces[at][:, pl.ds(column, size)], value)
        return decoded(value) if coded else value

    def find_ratios(block):
        for slot in range(slots):
            pair = (span[0] + block) * slots + slot
            gap = fetch(pair)
            live = plan[LIVE, pair].astype(jnp.float32)
            inverse = lax.rsqrt(square + gap * gap) * live
            lanes = slice(slot * size, (slot + 1) * size)
            ratios[block, :segment_rows, lanes] = (gap * inverse).astype(jnp.bfloat16)
            ratios[block, segment_rows:, lanes] = (col_omega * inverse).astype(jnp.bfloat16)

    def find_terms(block):
        lanes = slice(block * size, (block + 1) * size)
        for start in range(0, modes, 2):
            stop = min(start + 2, modes)
            terms = jnp.dot(
                ratios[block],
                weights[span[0] + block, :, start * size : stop * size],
                preferred_element_type=jnp.float32,
            )
            upper, lower = split(terms)
            for mode in range(start, stop):
                rows = slice(mode * segment_rows, (mode + 1) * segment_rows)
                taken = slice((mode - start) * size, (mode - start + 1) * size)
                for part in range(2):
                    source = slice(part * segment_rows, (part + 1) * segment_rows)
                    high[part, rows, lanes] = upper[source, taken]
                    low[part, rows, lanes] = lower[source, taken]

    def earlier(part, lanes):
        width = before[0].shape[-1]
        start = lanes.start % width
        return before[lanes.start // width][part, :, start : start + lanes.stop - lanes.start]

    def find_sums(lanes):
        sums = []
        for part in range(2):
            both = jnp.dot(
                table[part], high[part, :, lanes], preferred_element_type=jnp.float32
            )
            rest = jnp.dot(
                table[part, :padded_rows],
                low[part, :, lanes],
                preferred_element_type=jnp.float32,
            )
            total = both[:padded_rows] + (both[padded_rows:] + rest)
            sums.append(total if first else total + earlier(part, lanes))
        if not last:
            for part in range(2):
                outs[0][part, :, lanes] = sums[part]
            return
        own_rows = outs[0].shape[0]
        width = lanes.stop - lanes.start
        row = lax.broadcasted_iota(jnp.int32, (own_rows, width), 0) + plan[ROWS, 0]
        temperature = CUTOFF / freq_count
        renorm = 1.0 + temperature * sums[1][:own_rows] / omega_of(row, freq_count)
        gap = temperature * sums[0][:own_rows] / renorm
        if not final:
            outs[0][:, lanes] = encoded(gap) if coded else gap
            return
        for at, value in enumerate((gap, renorm)):
            held[at][:, lanes] = value
            copy_out(at, lanes).start()

    def copy_out(at, lanes):
        width = lanes.stop - lanes.start
        return pltpu.make_async_copy(
            held[at].at[:, pl.ds(lanes.start, width)],
            outs[at].at[:, pl.ds(lanes.start, width)],
            sems.at[at, lanes.start // width],
        )

    halves = [slice(start * size, (start + 2) * size) for start in range(0, blocks, 2)]
    for block in range(blocks):
        find_ratios(block)
    for block in range(blocks):
        find_terms(block)
        if block % 2 == 1 and block > 1:
            find_sums(halves[block // 2 - 1])
    find_sums(halves[-1])
    if copied:
        for lanes in halves:
            for at in range(2):
                copy_out(at, lanes).wait()


def other_rows_kernel(dims, plan, *refs):
    freq_count, segments, segment_rows, padded_rows, modes = dims
    tables, terms, code = refs[:segments], refs[segments:-1], refs[-1]
    sums = []
    for part in range(2):
        total = None
        for segment in range(segments):
            table, high, low = tables[segment], terms[2 * segment], terms[2 * segment + 1]
            both = jnp.dot(table[part], high[part], preferred_element_type=jnp.float32)
            rest = jnp.dot(
                table[part, :padded_rows], low[part], preferred_element_type=jnp.float32
            )
            piece = both[:padded_rows] + (both[padded_rows:] + rest)
            total = piece if total is None else total + piece
        sums.append(total)
    row = lax.broadcasted_iota(jnp.int32, (padded_rows, code.shape[1]), 0) + plan[ROWS, 2]
    temperature = CUTOFF / freq_count
    renorm = 1.0 + temperature * sums[1] / omega_of(row, freq_count)
    code[:padded_rows] = encoded(temperature * sums[0] / renorm)
    code[padded_rows:] = jnp.zeros((SPARE_ROWS, code.shape[1]), code.dtype)


SWAP = [(0, 1), (1, 0)]


def gather_general(gap, half_groups):
    everyone = lax.all_gather(gap, "state", axis=0, tiled=False)
    rows = lax.all_gather(everyone, "freq", axis=1, tiled=True)
    own_rows = gap.shape[0]
    start = (lax.axis_index("freq") // half_groups) * (half_groups * own_rows)
    return [lax.dynamic_slice_in_dim(rows, start, half_groups * own_rows, 1)]


def on_device(pairwise, freq_groups, gap_in, coupling, pair_cols, pair_count, block_order, phonon):
    own_rows, row_width = gap_in.shape
    blocks, slots, modes, size, _ = coupling.shape
    freq_count = own_rows * freq_groups
    half_rows = freq_count // 2
    half_groups = freq_groups // 2
    padded_rows = -(-own_rows // 16) * 16
    if pairwise:
        segments, sides = 2, 2
        half = lax.axis_index("zhi") * half_rows
        own = half + lax.axis_index("zlo") * own_rows
        other = half + (1 - lax.axis_index("zlo")) * own_rows
        meta = [own, own, other, lax.axis_index("x"), lax.axis_index("core")]
    else:
        segments, sides = 1, 1
        freq_at = lax.axis_index("freq")
        meta = [freq_at * own_rows, (freq_at // half_groups) * half_rows, 0, 0]
    meta = jnp.stack([jnp.asarray(value, jnp.int32) for value in meta])
    segment_rows = half_rows // segments
    dims = (freq_count, segments, segment_rows, padded_rows, modes)
    smem = pl.BlockSpec(memory_space=pltpu.SMEM)
    vmem = pl.BlockSpec(memory_space=pltpu.VMEM)
    link_type = jnp.int16 if pairwise else jnp.float32

    passed = gap_in
    if pairwise:
        passed, longer = pl.pallas_call(
            encode_kernel,
            out_shape=[
                jax.ShapeDtypeStruct(gap_in.shape, link_type),
                jax.ShapeDtypeStruct((own_rows + SPARE_ROWS, row_width), link_type),
            ],
            in_specs=[vmem],
            out_specs=[vmem, vmem],
            compiler_params=pltpu.CompilerParams(vmem_limit_bytes=8 << 20),
            cost_estimate=pl.CostEstimate(
                flops=10_000_000_000, bytes_accessed=40_000_000, transcendentals=0
            ),
            name="encode",
        )(gap_in)

    table_shape = jax.ShapeDtypeStruct(
        (2, 2 * padded_rows, modes * segment_rows), jnp.bfloat16
    )
    plan, weights, *tables = pl.pallas_call(
        functools.partial(tables_kernel, dims, sides),
        out_shape=[
            jax.ShapeDtypeStruct((5, max(blocks * slots, 1 + segments)), jnp.int32),
            jax.ShapeDtypeStruct((blocks, slots * size, modes * size), jnp.bfloat16),
        ]
        + [table_shape] * segments,
        in_specs=[smem] * 5 + [vmem],
        out_specs=[smem] + [vmem] * (1 + segments),
        compiler_params=pltpu.CompilerParams(vmem_limit_bytes=24 << 20),
        cost_estimate=pl.CostEstimate(
            flops=10_000_000, bytes_accessed=8_000_000, transcendentals=0
        ),
        name="tables",
    )(meta, phonon, pair_cols, pair_count, block_order, coupling)

    full = jax.ShapeDtypeStruct(gap_in.shape, jnp.float32)
    passed_out = jax.ShapeDtypeStruct(gap_in.shape, link_type)
    step_params = dict(
        compiler_params=pltpu.CompilerParams(vmem_limit_bytes=24 << 20),
        cost_estimate=pl.CostEstimate(
            flops=STEP_FLOPS, bytes_accessed=100_000, transcendentals=0
        ),
    )

    def step(plan, segment, final, pieces, before, keep=False, span=(0, blocks)):
        copied = final and segment == segments - 1
        width = (span[1] - span[0]) * size
        terms_shape = (2, modes * segment_rows, width)
        if segment < segments - 1:
            outs = [jax.ShapeDtypeStruct((2, padded_rows, width), jnp.float32)]
        else:
            outs = [full, full] if final else [passed_out]
        out_specs = [pl.BlockSpec(memory_space=pl.ANY) if copied else vmem] * len(outs)
        scratch = [pltpu.VMEM((span[1] - span[0], 2 * segment_rows, slots * size), jnp.bfloat16)]
        if keep:
            outs += [jax.ShapeDtypeStruct(terms_shape, jnp.bfloat16)] * 2
            out_specs += [vmem] * 2
        else:
            scratch += [pltpu.VMEM(terms_shape, jnp.bfloat16)] * 2
        if copied:
            scratch += [pltpu.VMEM(gap_in.shape, jnp.float32)] * 2
            scratch += [pltpu.SemaphoreType.DMA((2, blocks // 2))]
        inputs = [*pieces, weights, tables[segment], *before]
        return pl.pallas_call(
            functools.partial(
                step_kernel, dims, segment, span, sides, pairwise, final, keep, len(before)
            ),
            out_shape=outs,
            in_specs=[smem] + [vmem] * len(inputs),
            out_specs=out_specs,
            scratch_shapes=scratch,
            name="step",
            **step_params,
        )(plan, *inputs)

    if not pairwise:
        for iteration in range(ITERS):
            final = iteration == ITERS - 1
            results = step(plan, 0, final, gather_general(passed, half_groups), [])
            passed = results[0]
        return tuple(results)

    def join(near, across, after):
        return pl.pallas_call(
            join_kernel,
            out_shape=jax.ShapeDtypeStruct((2, *gap_in.shape), near.dtype),
            in_specs=[vmem, vmem, pl.BlockSpec(memory_space=pl.ANY)],
            out_specs=vmem,
            compiler_params=pltpu.CompilerParams(vmem_limit_bytes=4 << 20),
            cost_estimate=pl.CostEstimate(flops=1000, bytes_accessed=1000, transcendentals=0),
            name="join",
        )(near, across, after)

    def with_core(near):
        return near + [lax.ppermute(piece, "core", SWAP) for piece in near]

    other_tables = pl.pallas_call(
        functools.partial(other_tables_kernel, dims),
        out_shape=[table_shape] * segments,
        in_specs=[smem, smem],
        out_specs=[vmem] * segments,
        compiler_params=pltpu.CompilerParams(vmem_limit_bytes=12 << 20),
        cost_estimate=pl.CostEstimate(
            flops=10_000_000, bytes_accessed=3_000_000, transcendentals=0
        ),
        name="other_tables",
    )(meta, phonon)
    along_x = lax.ppermute(passed, "x", SWAP)
    along_z = lax.ppermute(longer, "zlo", SWAP)
    diagonal = lax.ppermute(longer, ("zlo", "x"), [(at, 3 - at) for at in range(4)])
    along_x, plan = lax.optimization_barrier((along_x, plan))
    partial, *near_terms = step(plan, 0, False, with_core([passed, along_x]), [], keep=True)
    far = join(along_z, diagonal, partial)
    pieces = [far, lax.ppermute(far, "core", SWAP)]
    plan, *other_tables = lax.optimization_barrier((plan, *other_tables))
    own, *far_terms = step(plan, 1, False, pieces, [partial], keep=True)
    inputs = [*other_tables, *near_terms, *far_terms]
    other = pl.pallas_call(
        functools.partial(other_rows_kernel, dims),
        out_shape=jax.ShapeDtypeStruct((own_rows + SPARE_ROWS, row_width), link_type),
        in_specs=[smem] + [vmem] * len(inputs),
        out_specs=vmem,
        name="other_rows",
        **step_params,
    )(plan, *inputs)
    along_x = lax.ppermute(own, "x", SWAP)
    near = with_core([own, along_x])
    middle = blocks // 2
    partial = step(plan, 0, True, near, [], span=(0, middle))
    far = join(other, lax.ppermute(other, "x", SWAP), *partial)
    partial += step(plan, 0, True, near, [], span=(middle, blocks))
    return tuple(step(plan, 1, True, [far, lax.ppermute(far, "core", SWAP)], partial))


def solution(mesh):
    shape = tuple(mesh.shape[axis] for axis in ("parts", "freq", "state"))
    pairwise = shape[1:] == (4, 4)
    parts, freq, state = "parts", "freq", "state"
    if pairwise:
        names = ("parts", "zhi", "zlo", "x", "core")
        mesh = jax.sharding.Mesh(mesh.devices.reshape(shape[0], 2, 2, 2, 2), names)
        freq, state = ("zhi", "zlo"), ("x", "core")
    rows = ("parts", *freq) if pairwise else ("parts", freq)
    groups = ("parts", *state) if pairwise else ("parts", state)
    return jax.shard_map(
        functools.partial(on_device, pairwise, shape[1]),
        mesh=mesh,
        in_specs=(
            P(rows, state),
            P(groups, None, None, None, None),
            P(groups, None),
            P(groups),
            P(parts),
            P(parts),
        ),
        out_specs=(P(rows, state), P(rows, state)),
        check_vma=False,
    )
```

```python
import functools

import jax
import jax.numpy as jnp
from jax import lax
from jax.experimental import pallas as pl
from jax.experimental.pallas import tpu as pltpu
from jax.sharding import PartitionSpec as P

ITERS = 2
CUTOFF = 4.0
LANES = 128
GAP_LIMIT = 10.0
CODE_LIMIT = 32767.0
CODE_POWER = 5
STEP_FLOPS = 1_000_000
SPARE_ROWS = 16
HOLDER, PLACE, LIVE, SIDE, ROWS = 0, 1, 2, 3, 4


def omega_of(index, freq_count):
    return (2.0 * index.astype(jnp.float32) + 1.0 - freq_count) * (CUTOFF / freq_count)


def encoded(gap):
    share = jnp.minimum(jnp.abs(gap) * (1.0 / GAP_LIMIT), 1.0)
    root = jnp.exp2(jnp.log2(jnp.maximum(share, 1e-37)) * (1.0 / CODE_POWER))
    code = jnp.floor(root * CODE_LIMIT + 0.5)
    return jnp.where(gap < 0, -code, code).astype(jnp.int32).astype(jnp.int16)


def decoded(code):
    root = code.astype(jnp.float32) * (1.0 / CODE_LIMIT)
    square = root * root
    return (root * GAP_LIMIT) * (square * square)


def encode_kernel(gap, code):
    code[...] = encoded(gap[...])


def join_kernel(first, second, after, joined):
    rows = joined.shape[1]
    joined[0] = first[:rows]
    joined[1] = second[:rows]


def split(value):
    high = value.astype(jnp.bfloat16)
    return high, (value - high.astype(jnp.float32)).astype(jnp.bfloat16)


def fill_tables(dims, meta, row_from, phonon, tables):
    freq_count, segments, segment_rows, padded_rows, modes = dims
    shape = (padded_rows, segment_rows)
    row_omega = omega_of(lax.broadcasted_iota(jnp.int32, shape, 0) + meta[row_from], freq_count)
    for segment in range(len(tables)):
        col = lax.broadcasted_iota(jnp.int32, shape, 1) + meta[1 + segment]
        col_omega = omega_of(col, freq_count)
        near = (row_omega - col_omega) ** 2
        far = (row_omega + col_omega) ** 2
        cross = 4.0 * (row_omega * col_omega)
        for mode in range(modes):
            strength = phonon[mode]
            below = near + strength * strength
            above = far + strength * strength
            common = (2.0 * strength) / (below * above)
            columns = slice(mode * segment_rows, (mode + 1) * segment_rows)
            for part, value in enumerate((common * (below + above), common * cross)):
                high, low = split(value)
                tables[segment][part, :padded_rows, columns] = high
                tables[segment][part, padded_rows:, columns] = low


def other_tables_kernel(dims, meta, phonon, *tables):
    fill_tables(dims, meta, 2, phonon, tables)


def tables_kernel(
    dims, sides, meta, phonon, pair_cols, pair_count, block_order, coupling, plan, weights, *tables
):
    freq_count, segments, segment_rows, padded_rows, modes = dims
    blocks, slots = coupling.shape[:2]
    size = coupling.shape[3]
    for at in range(1 + segments):
        plan[ROWS, at] = meta[at]
    for block in range(blocks):
        for slot in range(slots):
            wanted = pair_cols[block, slot]
            position = jnp.int32(0)
            for at in range(block_order.shape[0]):
                position = jnp.where(block_order[at] == wanted, at, position)
            pair = block * slots + slot
            holder = position // blocks
            plan[HOLDER, pair] = (holder // sides) ^ meta[1 + segments]
            plan[SIDE, pair] = (holder % sides) ^ meta[2 + segments]
            plan[PLACE, pair] = position % blocks
            plan[LIVE, pair] = (pair_count[block] > slot).astype(jnp.int32)
    fill_tables(dims, meta, 0, phonon, tables)
    for block in range(blocks):
        for slot in range(slots):
            for mode in range(modes):
                weights[
                    block, slot * size : (slot + 1) * size, mode * size : (mode + 1) * size
                ] = coupling[block, slot, mode].T


def step_kernel(dims, segment, span, sides, coded, final, keep, parted, plan, *refs):
    freq_count, segments, segment_rows, padded_rows, modes = dims
    refs = list(refs)
    first, last = segment == 0, segment == segments - 1
    take = lambda count: [refs.pop() for _ in range(count)][::-1]
    copied = last and final
    if copied:
        *held, sems = take(3)
    high, low = (None, None) if keep else take(2)
    ratios = refs.pop()
    if keep:
        high, low = take(2)
    outs = take(2 if copied else 1)
    inputs = refs
    before = [inputs.pop() for _ in range(0 if first else parted)][::-1]
    weights, table = inputs[-2:]
    pieces = []
    for piece in inputs[:-2]:
        if len(piece.shape) == 3:
            pieces += [piece.at[at] for at in range(piece.shape[0])]
        else:
            pieces.append(piece)
    holders = len(pieces) // sides
    blocks = span[1] - span[0]
    size = LANES
    slots = weights.shape[1] // size
    shape = (segment_rows, size)
    col = lax.broadcasted_iota(jnp.int32, shape, 0) + plan[ROWS, 1 + segment]
    col_omega = omega_of(col, freq_count)
    square = col_omega * col_omega

    def fetch(pair):
        column = pl.multiple_of(plan[PLACE, pair] * size, size)
        wanted = plan[SIDE, pair] * holders + plan[HOLDER, pair]
        value = pieces[0][:, pl.ds(column, size)]
        for at in range(1, len(pieces)):
            value = lax.select(wanted == at, pieces[at][:, pl.ds(column, size)], value)
        return decoded(value) if coded else value

    def find_ratios(block):
        for slot in range(slots):
            pair = (span[0] + block) * slots + slot
            gap = fetch(pair)
            live = plan[LIVE, pair].astype(jnp.float32)
            inverse = lax.rsqrt(square + gap * gap) * live
            lanes = slice(slot * size, (slot + 1) * size)
            ratios[block, :segment_rows, lanes] = (gap * inverse).astype(jnp.bfloat16)
            ratios[block, segment_rows:, lanes] = (col_omega * inverse).astype(jnp.bfloat16)

    def find_terms(block):
        lanes = slice(block * size, (block + 1) * size)
        for start in range(0, modes, 2):
            stop = min(start + 2, modes)
            terms = jnp.dot(
                ratios[block],
                weights[span[0] + block, :, start * size : stop * size],
                preferred_element_type=jnp.float32,
            )
            upper, lower = split(terms)
            for mode in range(start, stop):
                rows = slice(mode * segment_rows, (mode + 1) * segment_rows)
                taken = slice((mode - start) * size, (mode - start + 1) * size)
                for part in range(2):
                    source = slice(part * segment_rows, (part + 1) * segment_rows)
                    high[part, rows, lanes] = upper[source, taken]
                    low[part, rows, lanes] = lower[source, taken]

    def earlier(part, lanes):
        width = before[0].shape[-1]
        start = lanes.start % width
        return before[lanes.start // width][part, :, start : start + lanes.stop - lanes.start]

    def find_sums(lanes):
        sums = []
        for part in range(2):
            both = jnp.dot(
                table[part], high[part, :, lanes], preferred_element_type=jnp.float32
            )
            rest = jnp.dot(
                table[part, :padded_rows],
                low[part, :, lanes],
                preferred_element_type=jnp.float32,
            )
            total = both[:padded_rows] + (both[padded_rows:] + rest)
            sums.append(total if first else total + earlier(part, lanes))
        if not last:
            for part in range(2):
                outs[0][part, :, lanes] = sums[part]
            return
        own_rows = outs[0].shape[0]
        width = lanes.stop - lanes.start
        row = lax.broadcasted_iota(jnp.int32, (own_rows, width), 0) + plan[ROWS, 0]
        temperature = CUTOFF / freq_count
        renorm = 1.0 + temperature * sums[1][:own_rows] / omega_of(row, freq_count)
        gap = temperature * sums[0][:own_rows] / renorm
        if not final:
            outs[0][:, lanes] = encoded(gap) if coded else gap
            return
        for at, value in enumerate((gap, renorm)):
            held[at][:, lanes] = value
            copy_out(at, lanes).start()

    def copy_out(at, lanes):
        width = lanes.stop - lanes.start
        return pltpu.make_async_copy(
            held[at].at[:, pl.ds(lanes.start, width)],
            outs[at].at[:, pl.ds(lanes.start, width)],
            sems.at[at, lanes.start // width],
        )

    halves = [slice(start * size, (start + 2) * size) for start in range(0, blocks, 2)]
    for block in range(blocks):
        find_ratios(block)
    for block in range(blocks):
        find_terms(block)
        if block % 2 == 1 and block > 1:
            find_sums(halves[block // 2 - 1])
    find_sums(halves[-1])
    if copied:
        for lanes in halves:
            for at in range(2):
                copy_out(at, lanes).wait()


def other_rows_kernel(dims, plan, *refs):
    freq_count, segments, segment_rows, padded_rows, modes = dims
    tables, terms, code = refs[:segments], refs[segments:-1], refs[-1]
    sums = []
    for part in range(2):
        total = None
        for segment in range(segments):
            table, high, low = tables[segment], terms[2 * segment], terms[2 * segment + 1]
            both = jnp.dot(table[part], high[part], preferred_element_type=jnp.float32)
            rest = jnp.dot(
                table[part, :padded_rows], low[part], preferred_element_type=jnp.float32
            )
            piece = both[:padded_rows] + (both[padded_rows:] + rest)
            total = piece if total is None else total + piece
        sums.append(total)
    row = lax.broadcasted_iota(jnp.int32, (padded_rows, code.shape[1]), 0) + plan[ROWS, 2]
    temperature = CUTOFF / freq_count
    renorm = 1.0 + temperature * sums[1] / omega_of(row, freq_count)
    code[:padded_rows] = encoded(temperature * sums[0] / renorm)
    code[padded_rows:] = jnp.zeros((SPARE_ROWS, code.shape[1]), code.dtype)


SWAP = [(0, 1), (1, 0)]


def gather_general(gap, half_groups):
    everyone = lax.all_gather(gap, "state", axis=0, tiled=False)
    rows = lax.all_gather(everyone, "freq", axis=1, tiled=True)
    own_rows = gap.shape[0]
    start = (lax.axis_index("freq") // half_groups) * (half_groups * own_rows)
    return [lax.dynamic_slice_in_dim(rows, start, half_groups * own_rows, 1)]


def on_device(pairwise, freq_groups, gap_in, coupling, pair_cols, pair_count, block_order, phonon):
    own_rows, row_width = gap_in.shape
    blocks, slots, modes, size, _ = coupling.shape
    freq_count = own_rows * freq_groups
    half_rows = freq_count // 2
    half_groups = freq_groups // 2
    padded_rows = -(-own_rows // 16) * 16
    if pairwise:
        segments, sides = 2, 2
        half = lax.axis_index("zhi") * half_rows
        own = half + lax.axis_index("zlo") * own_rows
        other = half + (1 - lax.axis_index("zlo")) * own_rows
        meta = [own, own, other, lax.axis_index("x"), lax.axis_index("core")]
    else:
        segments, sides = 1, 1
        freq_at = lax.axis_index("freq")
        meta = [freq_at * own_rows, (freq_at // half_groups) * half_rows, 0, 0]
    meta = jnp.stack([jnp.asarray(value, jnp.int32) for value in meta])
    segment_rows = half_rows // segments
    dims = (freq_count, segments, segment_rows, padded_rows, modes)
    smem = pl.BlockSpec(memory_space=pltpu.SMEM)
    vmem = pl.BlockSpec(memory_space=pltpu.VMEM)
    link_type = jnp.int16 if pairwise else jnp.float32

    passed = gap_in
    if pairwise:
        passed = pl.pallas_call(
            encode_kernel,
            out_shape=jax.ShapeDtypeStruct(gap_in.shape, link_type),
            in_specs=[vmem],
            out_specs=vmem,
            compiler_params=pltpu.CompilerParams(vmem_limit_bytes=8 << 20),
            cost_estimate=pl.CostEstimate(
                flops=10_000_000_000, bytes_accessed=40_000_000, transcendentals=0
            ),
            name="encode",
        )(gap_in)

    table_shape = jax.ShapeDtypeStruct(
        (2, 2 * padded_rows, modes * segment_rows), jnp.bfloat16
    )
    plan, weights, *tables = pl.pallas_call(
        functools.partial(tables_kernel, dims, sides),
        out_shape=[
            jax.ShapeDtypeStruct((5, max(blocks * slots, 1 + segments)), jnp.int32),
            jax.ShapeDtypeStruct((blocks, slots * size, modes * size), jnp.bfloat16),
        ]
        + [table_shape] * segments,
        in_specs=[smem] * 5 + [vmem],
        out_specs=[smem] + [vmem] * (1 + segments),
        compiler_params=pltpu.CompilerParams(vmem_limit_bytes=24 << 20),
        cost_estimate=pl.CostEstimate(
            flops=10_000_000, bytes_accessed=8_000_000, transcendentals=0
        ),
        name="tables",
    )(meta, phonon, pair_cols, pair_count, block_order, coupling)

    full = jax.ShapeDtypeStruct(gap_in.shape, jnp.float32)
    passed_out = jax.ShapeDtypeStruct(gap_in.shape, link_type)
    step_params = dict(
        compiler_params=pltpu.CompilerParams(vmem_limit_bytes=24 << 20),
        cost_estimate=pl.CostEstimate(
            flops=STEP_FLOPS, bytes_accessed=100_000, transcendentals=0
        ),
    )

    def step(plan, segment, final, pieces, before, keep=False, span=(0, blocks)):
        copied = final and segment == segments - 1
        width = (span[1] - span[0]) * size
        terms_shape = (2, modes * segment_rows, width)
        if segment < segments - 1:
            outs = [jax.ShapeDtypeStruct((2, padded_rows, width), jnp.float32)]
        else:
            outs = [full, full] if final else [passed_out]
        out_specs = [pl.BlockSpec(memory_space=pl.ANY) if copied else vmem] * len(outs)
        scratch = [pltpu.VMEM((span[1] - span[0], 2 * segment_rows, slots * size), jnp.bfloat16)]
        if keep:
            outs += [jax.ShapeDtypeStruct(terms_shape, jnp.bfloat16)] * 2
            out_specs += [vmem] * 2
        else:
            scratch += [pltpu.VMEM(terms_shape, jnp.bfloat16)] * 2
        if copied:
            scratch += [pltpu.VMEM(gap_in.shape, jnp.float32)] * 2
            scratch += [pltpu.SemaphoreType.DMA((2, blocks // 2))]
        inputs = [*pieces, weights, tables[segment], *before]
        return pl.pallas_call(
            functools.partial(
                step_kernel, dims, segment, span, sides, pairwise, final, keep, len(before)
            ),
            out_shape=outs,
            in_specs=[smem] + [vmem] * len(inputs),
            out_specs=out_specs,
            scratch_shapes=scratch,
            name="step",
            **step_params,
        )(plan, *inputs)

    if not pairwise:
        for iteration in range(ITERS):
            final = iteration == ITERS - 1
            results = step(plan, 0, final, gather_general(passed, half_groups), [])
            passed = results[0]
        return tuple(results)

    def join(near, across, after):
        return pl.pallas_call(
            join_kernel,
            out_shape=jax.ShapeDtypeStruct((2, *gap_in.shape), near.dtype),
            in_specs=[vmem, vmem, pl.BlockSpec(memory_space=pl.ANY)],
            out_specs=vmem,
            compiler_params=pltpu.CompilerParams(vmem_limit_bytes=4 << 20),
            cost_estimate=pl.CostEstimate(flops=1000, bytes_accessed=1000, transcendentals=0),
            name="join",
        )(near, across, after)

    def with_core(near):
        return near + [lax.ppermute(piece, "core", SWAP) for piece in near]

    other_tables = pl.pallas_call(
        functools.partial(other_tables_kernel, dims),
        out_shape=[table_shape] * segments,
        in_specs=[smem, smem],
        out_specs=[vmem] * segments,
        compiler_params=pltpu.CompilerParams(vmem_limit_bytes=12 << 20),
        cost_estimate=pl.CostEstimate(
            flops=10_000_000, bytes_accessed=3_000_000, transcendentals=0
        ),
        name="other_tables",
    )(meta, phonon)
    along_x = lax.ppermute(passed, "x", SWAP)
    along_z = lax.ppermute(passed, "zlo", SWAP)
    along_x, plan = lax.optimization_barrier((along_x, plan))
    relayed = lax.ppermute(along_z, "x", SWAP)
    partial, *near_terms = step(plan, 0, False, with_core([passed, along_x]), [], keep=True)
    far = join(along_z, relayed, partial)
    pieces = [far, lax.ppermute(far, "core", SWAP)]
    plan, *other_tables = lax.optimization_barrier((plan, *other_tables))
    own, *far_terms = step(plan, 1, False, pieces, [partial], keep=True)
    inputs = [*other_tables, *near_terms, *far_terms]
    other = pl.pallas_call(
        functools.partial(other_rows_kernel, dims),
        out_shape=jax.ShapeDtypeStruct((own_rows + SPARE_ROWS, row_width), link_type),
        in_specs=[smem] + [vmem] * len(inputs),
        out_specs=vmem,
        name="other_rows",
        **step_params,
    )(plan, *inputs)
    along_x = lax.ppermute(own, "x", SWAP)
    near = with_core([own, along_x])
    middle = blocks // 2
    partial = step(plan, 0, True, near, [], span=(0, middle))
    far = join(other, lax.ppermute(other, "x", SWAP), *partial)
    partial += step(plan, 0, True, near, [], span=(middle, blocks))
    return tuple(step(plan, 1, True, [far, lax.ppermute(far, "core", SWAP)], partial))


def solution(mesh):
    shape = tuple(mesh.shape[axis] for axis in ("parts", "freq", "state"))
    pairwise = shape[1:] == (4, 4)
    parts, freq, state = "parts", "freq", "state"
    if pairwise:
        names = ("parts", "zhi", "zlo", "x", "core")
        mesh = jax.sharding.Mesh(mesh.devices.reshape(shape[0], 2, 2, 2, 2), names)
        freq, state = ("zhi", "zlo"), ("x", "core")
    rows = ("parts", *freq) if pairwise else ("parts", freq)
    groups = ("parts", *state) if pairwise else ("parts", state)
    return jax.shard_map(
        functools.partial(on_device, pairwise, shape[1]),
        mesh=mesh,
        in_specs=(
            P(rows, state),
            P(groups, None, None, None, None),
            P(groups, None),
            P(groups),
            P(parts),
            P(parts),
        ),
        out_specs=(P(rows, state), P(rows, state)),
        check_vma=False,
    )
```

```python
import functools

import jax
import jax.numpy as jnp
from jax import lax
from jax.experimental import pallas as pl
from jax.experimental.pallas import tpu as pltpu
from jax.sharding import PartitionSpec as P

ITERS = 2
CUTOFF = 4.0
LANES = 128
GAP_LIMIT = 10.0
CODE_LIMIT = 32767.0
CODE_POWER = 5
STEP_FLOPS = 1_000_000
SPARE_ROWS = 32
HOLDER, PLACE, LIVE, SIDE, ROWS = 0, 1, 2, 3, 4


def omega_of(index, freq_count):
    return (2.0 * index.astype(jnp.float32) + 1.0 - freq_count) * (CUTOFF / freq_count)


def encoded(gap):
    share = jnp.minimum(jnp.abs(gap) * (1.0 / GAP_LIMIT), 1.0)
    root = jnp.exp2(jnp.log2(jnp.maximum(share, 1e-37)) * (1.0 / CODE_POWER))
    code = jnp.floor(root * CODE_LIMIT + 0.5)
    return jnp.where(gap < 0, -code, code).astype(jnp.int32).astype(jnp.int16)


def decoded(code):
    root = code.astype(jnp.float32) * (1.0 / CODE_LIMIT)
    square = root * root
    return (root * GAP_LIMIT) * (square * square)


def encode_kernel(gap, code):
    code[...] = encoded(gap[...].T)


def join_kernel(first, second, after, joined):
    rows = joined.shape[1]
    joined[0] = first[:rows]
    joined[1] = second[:rows]


def split(value):
    high = value.astype(jnp.bfloat16)
    return high, (value - high.astype(jnp.float32)).astype(jnp.bfloat16)


def fill_tables(dims, meta, row_from, phonon, tables):
    freq_count, segments, segment_rows, padded_rows, modes = dims
    shape = (segment_rows, padded_rows)
    row = lax.broadcasted_iota(jnp.int32, shape, 1) + meta[row_from]
    row_omega = omega_of(row, freq_count)
    for segment in range(segments):
        col = lax.broadcasted_iota(jnp.int32, shape, 0) + meta[1 + segment]
        col_omega = omega_of(col, freq_count)
        near = (row_omega - col_omega) ** 2
        far = (row_omega + col_omega) ** 2
        cross = 4.0 * (row_omega * col_omega)
        for mode in range(modes):
            strength = phonon[mode]
            below = near + strength * strength
            above = far + strength * strength
            common = (2.0 * strength) / (below * above)
            rows = slice(mode * segment_rows, (mode + 1) * segment_rows)
            for part, value in enumerate((common * (below + above), common * cross)):
                high, low = split(value)
                tables[segment][part, rows, :padded_rows] = high
                tables[segment][part, rows, padded_rows:] = low


def other_tables_kernel(dims, meta, phonon, *tables):
    fill_tables(dims, meta, 2, phonon, tables)


def tables_kernel(
    dims, sides, meta, phonon, pair_cols, pair_count, block_order, coupling, plan, weights, *tables
):
    freq_count, segments, segment_rows, padded_rows, modes = dims
    blocks, slots = coupling.shape[:2]
    size = coupling.shape[3]
    for at in range(1 + segments):
        plan[ROWS, at] = meta[at]
    for block in range(blocks):
        for slot in range(slots):
            wanted = pair_cols[block, slot]
            position = jnp.int32(0)
            for at in range(block_order.shape[0]):
                position = jnp.where(block_order[at] == wanted, at, position)
            pair = block * slots + slot
            holder = position // blocks
            plan[HOLDER, pair] = (holder // sides) ^ meta[1 + segments]
            plan[SIDE, pair] = (holder % sides) ^ meta[2 + segments]
            plan[PLACE, pair] = position % blocks
            plan[LIVE, pair] = (pair_count[block] > slot).astype(jnp.int32)
    fill_tables(dims, meta, 0, phonon, tables)
    for block in range(blocks):
        for slot in range(slots):
            for mode in range(modes):
                weights[
                    block, mode * size : (mode + 1) * size, slot * size : (slot + 1) * size
                ] = coupling[block, slot, mode]


def step_kernel(dims, segment, span, sides, coded, final, keep, parted, plan, *refs):
    freq_count, segments, segment_rows, padded_rows, modes = dims
    refs = list(refs)
    first, last = segment == 0, segment == segments - 1
    take = lambda count: [refs.pop() for _ in range(count)][::-1]
    copied = last and final
    if copied:
        *held, sems = take(3)
    high, low = (None, None) if keep else take(2)
    ratios = refs.pop()
    if keep:
        high, low = take(2)
    outs = take(2 if copied else 1)
    inputs = refs
    before = [inputs.pop() for _ in range(0 if first else parted)][::-1]
    weights, table = inputs[-2:]
    pieces = []
    for piece in inputs[:-2]:
        if len(piece.shape) == 3:
            pieces += [piece.at[at] for at in range(piece.shape[0])]
        else:
            pieces.append(piece)
    holders = len(pieces) // sides
    blocks = span[1] - span[0]
    size = LANES
    slots = weights.shape[2] // size
    shape = (size, segment_rows)
    col = lax.broadcasted_iota(jnp.int32, shape, 1) + plan[ROWS, 1 + segment]
    col_omega = omega_of(col, freq_count)
    square = col_omega * col_omega

    def fetch(pair):
        start = pl.multiple_of(plan[PLACE, pair] * size, size)
        wanted = plan[SIDE, pair] * holders + plan[HOLDER, pair]
        value = pieces[0][pl.ds(start, size), :]
        for at in range(1, len(pieces)):
            value = lax.select(wanted == at, pieces[at][pl.ds(start, size), :], value)
        return decoded(value) if coded else value

    def find_ratios(block):
        for slot in range(slots):
            pair = (span[0] + block) * slots + slot
            gap = fetch(pair)
            live = plan[LIVE, pair].astype(jnp.float32)
            inverse = lax.rsqrt(square + gap * gap) * live
            rows = slice(slot * size, (slot + 1) * size)
            ratios[block, rows, :segment_rows] = (gap * inverse).astype(jnp.bfloat16)
            ratios[block, rows, segment_rows:] = (col_omega * inverse).astype(jnp.bfloat16)

    def find_terms(block):
        rows = slice(block * size, (block + 1) * size)
        for start in range(0, modes, 2):
            stop = min(start + 2, modes)
            terms = jnp.dot(
                weights[span[0] + block, start * size : stop * size, :],
                ratios[block],
                preferred_element_type=jnp.float32,
            )
            upper, lower = split(terms)
            for mode in range(start, stop):
                lanes = slice(mode * segment_rows, (mode + 1) * segment_rows)
                taken = slice((mode - start) * size, (mode - start + 1) * size)
                for part in range(2):
                    source = slice(part * segment_rows, (part + 1) * segment_rows)
                    high[part, rows, lanes] = upper[taken, source]
                    low[part, rows, lanes] = lower[taken, source]

    def earlier(part, rows):
        height = before[0].shape[1]
        start = rows.start % height
        return before[rows.start // height][part, start : start + rows.stop - rows.start, :]

    def find_sums(rows):
        sums = []
        for part in range(2):
            total = table_sums(padded_rows, table, high, low, part, rows)
            sums.append(total if first else total + earlier(part, rows))
        if not last:
            for part in range(2):
                outs[0][part, rows, :] = sums[part]
            return
        gap, renorm = finished(freq_count, plan[ROWS, 0], sums)
        if coded and not final:
            outs[0][rows, :] = encoded(gap)
            return
        for at, value in enumerate((gap, renorm)[: len(outs)]):
            for start in range(0, rows.stop - rows.start, size):
                turned = value[start : start + size].T
                lanes = slice(rows.start + start, rows.start + start + size)
                if copied:
                    held[at][:, lanes] = turned[: held[at].shape[0]]
                else:
                    outs[at][:, lanes] = turned[: outs[at].shape[0]]
            if copied:
                copy_out(at, rows).start()

    def copy_out(at, rows):
        width = rows.stop - rows.start
        return pltpu.make_async_copy(
            held[at].at[:, pl.ds(rows.start, width)],
            outs[at].at[:, pl.ds(rows.start, width)],
            sems.at[at, rows.start // width],
        )

    halves = [slice(start * size, (start + 2) * size) for start in range(0, blocks, 2)]
    for block in range(blocks):
        find_ratios(block)
    for block in range(blocks):
        find_terms(block)
        if block % 2 == 1 and block > 1:
            find_sums(halves[block // 2 - 1])
    find_sums(halves[-1])
    if copied:
        for rows in halves:
            for at in range(2):
                copy_out(at, rows).wait()


def table_sums(padded_rows, table, high, low, part, rows):
    both = jnp.dot(high[part, rows, :], table[part], preferred_element_type=jnp.float32)
    rest = jnp.dot(
        low[part, rows, :], table[part, :, :padded_rows], preferred_element_type=jnp.float32
    )
    return both[:, :padded_rows] + (both[:, padded_rows:] + rest)


def finished(freq_count, first_row, sums):
    row = lax.broadcasted_iota(jnp.int32, sums[0].shape, 1) + first_row
    temperature = CUTOFF / freq_count
    renorm = 1.0 + temperature * sums[1] / omega_of(row, freq_count)
    return temperature * sums[0] / renorm, renorm


def other_rows_kernel(dims, plan, *refs):
    freq_count, segments, segment_rows, padded_rows, modes = dims
    tables, terms, code = refs[:segments], refs[segments:-1], refs[-1]
    states = terms[0].shape[1]
    sums = []
    for part in range(2):
        total = None
        for segment in range(segments):
            high, low = terms[2 * segment], terms[2 * segment + 1]
            piece = table_sums(padded_rows, tables[segment], high, low, part, slice(0, states))
            total = piece if total is None else total + piece
        sums.append(total)
    gap, _ = finished(freq_count, plan[ROWS, 2], sums)
    code[:states] = encoded(gap)
    code[states:] = jnp.zeros((SPARE_ROWS, code.shape[1]), code.dtype)


SWAP = [(0, 1), (1, 0)]


def gather_general(gap, half_groups):
    everyone = lax.all_gather(gap, "state", axis=0, tiled=False)
    rows = lax.all_gather(everyone, "freq", axis=1, tiled=True)
    own_rows = gap.shape[0]
    start = (lax.axis_index("freq") // half_groups) * (half_groups * own_rows)
    half = lax.dynamic_slice_in_dim(rows, start, half_groups * own_rows, 1)
    return [jnp.swapaxes(half, 1, 2)]


def on_device(pairwise, freq_groups, gap_in, coupling, pair_cols, pair_count, block_order, phonon):
    own_rows, row_width = gap_in.shape
    blocks, slots, modes, size, _ = coupling.shape
    freq_count = own_rows * freq_groups
    half_rows = freq_count // 2
    half_groups = freq_groups // 2
    padded_rows = -(-own_rows // LANES) * LANES
    if pairwise:
        segments, sides = 2, 2
        half = lax.axis_index("zhi") * half_rows
        own = half + lax.axis_index("zlo") * own_rows
        other = half + (1 - lax.axis_index("zlo")) * own_rows
        meta = [own, own, other, lax.axis_index("x"), lax.axis_index("core")]
    else:
        segments, sides = 1, 1
        freq_at = lax.axis_index("freq")
        meta = [freq_at * own_rows, (freq_at // half_groups) * half_rows, 0, 0]
    meta = jnp.stack([jnp.asarray(value, jnp.int32) for value in meta])
    segment_rows = half_rows // segments
    dims = (freq_count, segments, segment_rows, padded_rows, modes)
    smem = pl.BlockSpec(memory_space=pltpu.SMEM)
    vmem = pl.BlockSpec(memory_space=pltpu.VMEM)
    link_type = jnp.int16 if pairwise else jnp.float32

    passed = gap_in
    if pairwise:
        passed = pl.pallas_call(
            encode_kernel,
            out_shape=jax.ShapeDtypeStruct((row_width, own_rows), link_type),
            in_specs=[vmem],
            out_specs=vmem,
            compiler_params=pltpu.CompilerParams(vmem_limit_bytes=8 << 20),
            cost_estimate=pl.CostEstimate(
                flops=10_000_000_000, bytes_accessed=40_000_000, transcendentals=0
            ),
            name="encode",
        )(gap_in)

    table_shape = jax.ShapeDtypeStruct(
        (2, modes * segment_rows, 2 * padded_rows), jnp.bfloat16
    )
    plan, weights, *tables = pl.pallas_call(
        functools.partial(tables_kernel, dims, sides),
        out_shape=[
            jax.ShapeDtypeStruct((5, max(blocks * slots, 1 + segments)), jnp.int32),
            jax.ShapeDtypeStruct((blocks, modes * size, slots * size), jnp.bfloat16),
        ]
        + [table_shape] * segments,
        in_specs=[smem] * 5 + [vmem],
        out_specs=[smem] + [vmem] * (1 + segments),
        compiler_params=pltpu.CompilerParams(vmem_limit_bytes=24 << 20),
        cost_estimate=pl.CostEstimate(
            flops=10_000_000, bytes_accessed=8_000_000, transcendentals=0
        ),
        name="tables",
    )(meta, phonon, pair_cols, pair_count, block_order, coupling)

    full = jax.ShapeDtypeStruct(gap_in.shape, jnp.float32)
    passed_shape = (row_width, own_rows) if pairwise else gap_in.shape
    passed_out = jax.ShapeDtypeStruct(passed_shape, link_type)
    step_params = dict(
        compiler_params=pltpu.CompilerParams(vmem_limit_bytes=24 << 20),
        cost_estimate=pl.CostEstimate(
            flops=STEP_FLOPS, bytes_accessed=100_000, transcendentals=0
        ),
    )

    def step(plan, segment, final, pieces, before, keep=False, span=(0, blocks)):
        copied = final and segment == segments - 1
        width = (span[1] - span[0]) * size
        terms_shape = (2, width, modes * segment_rows)
        if segment < segments - 1:
            outs = [jax.ShapeDtypeStruct((2, width, padded_rows), jnp.float32)]
        else:
            outs = [full, full] if final else [passed_out]
        out_specs = [pl.BlockSpec(memory_space=pl.ANY) if copied else vmem] * len(outs)
        scratch = [pltpu.VMEM((span[1] - span[0], slots * size, 2 * segment_rows), jnp.bfloat16)]
        if keep:
            outs += [jax.ShapeDtypeStruct(terms_shape, jnp.bfloat16)] * 2
            out_specs += [vmem] * 2
        else:
            scratch += [pltpu.VMEM(terms_shape, jnp.bfloat16)] * 2
        if copied:
            scratch += [pltpu.VMEM(gap_in.shape, jnp.float32)] * 2
            scratch += [pltpu.SemaphoreType.DMA((2, blocks // 2))]
        inputs = [*pieces, weights, tables[segment], *before]
        return pl.pallas_call(
            functools.partial(
                step_kernel, dims, segment, span, sides, pairwise, final, keep, len(before)
            ),
            out_shape=outs,
            in_specs=[smem] + [vmem] * len(inputs),
            out_specs=out_specs,
            scratch_shapes=scratch,
            name="step",
            **step_params,
        )(plan, *inputs)

    if not pairwise:
        for iteration in range(ITERS):
            final = iteration == ITERS - 1
            results = step(plan, 0, final, gather_general(passed, half_groups), [])
            passed = results[0]
        return tuple(results)

    def join(near, across, after):
        return pl.pallas_call(
            join_kernel,
            out_shape=jax.ShapeDtypeStruct((2, *passed_shape), near.dtype),
            in_specs=[vmem, vmem, pl.BlockSpec(memory_space=pl.ANY)],
            out_specs=vmem,
            compiler_params=pltpu.CompilerParams(vmem_limit_bytes=4 << 20),
            cost_estimate=pl.CostEstimate(flops=1000, bytes_accessed=1000, transcendentals=0),
            name="join",
        )(near, across, after)

    def with_core(near):
        return near + [lax.ppermute(piece, "core", SWAP) for piece in near]

    other_tables = pl.pallas_call(
        functools.partial(other_tables_kernel, dims),
        out_shape=[table_shape] * segments,
        in_specs=[smem, smem],
        out_specs=[vmem] * segments,
        compiler_params=pltpu.CompilerParams(vmem_limit_bytes=12 << 20),
        cost_estimate=pl.CostEstimate(
            flops=10_000_000, bytes_accessed=3_000_000, transcendentals=0
        ),
        name="other_tables",
    )(meta, phonon)
    along_x = lax.ppermute(passed, "x", SWAP)
    along_z = lax.ppermute(passed, "zlo", SWAP)
    along_x, plan = lax.optimization_barrier((along_x, plan))
    relayed = lax.ppermute(along_z, "x", SWAP)
    partial, *near_terms = step(plan, 0, False, with_core([passed, along_x]), [], keep=True)
    far = join(along_z, relayed, partial)
    pieces = [far, lax.ppermute(far, "core", SWAP)]
    plan, *other_tables = lax.optimization_barrier((plan, *other_tables))
    own, *far_terms = step(plan, 1, False, pieces, [partial], keep=True)
    inputs = [*other_tables, *near_terms, *far_terms]
    other = pl.pallas_call(
        functools.partial(other_rows_kernel, dims),
        out_shape=jax.ShapeDtypeStruct((row_width + SPARE_ROWS, own_rows), link_type),
        in_specs=[smem] + [vmem] * len(inputs),
        out_specs=vmem,
        name="other_rows",
        **step_params,
    )(plan, *inputs)
    along_x = lax.ppermute(own, "x", SWAP)
    near = with_core([own, along_x])
    middle = blocks // 2
    partial = step(plan, 0, True, near, [], span=(0, middle))
    far = join(other, lax.ppermute(other, "x", SWAP), *partial)
    partial += step(plan, 0, True, near, [], span=(middle, blocks))
    return tuple(step(plan, 1, True, [far, lax.ppermute(far, "core", SWAP)], partial))


def solution(mesh):
    shape = tuple(mesh.shape[axis] for axis in ("parts", "freq", "state"))
    pairwise = shape[1:] == (4, 4)
    parts, freq, state = "parts", "freq", "state"
    if pairwise:
        names = ("parts", "zhi", "zlo", "x", "core")
        mesh = jax.sharding.Mesh(mesh.devices.reshape(shape[0], 2, 2, 2, 2), names)
        freq, state = ("zhi", "zlo"), ("x", "core")
    rows = ("parts", *freq) if pairwise else ("parts", freq)
    groups = ("parts", *state) if pairwise else ("parts", state)
    return jax.shard_map(
        functools.partial(on_device, pairwise, shape[1]),
        mesh=mesh,
        in_specs=(
            P(rows, state),
            P(groups, None, None, None, None),
            P(groups, None),
            P(groups),
            P(parts),
            P(parts),
        ),
        out_specs=(P(rows, state), P(rows, state)),
        check_vma=False,
    )
```

```python
import functools

import jax
import jax.numpy as jnp
from jax import lax
from jax.experimental import pallas as pl
from jax.experimental.pallas import tpu as pltpu
from jax.sharding import PartitionSpec as P

ITERS = 2
CUTOFF = 4.0
LANES = 128
GAP_LIMIT = 10.0
CODE_LIMIT = 32767.0
CODE_POWER = 5
STEP_FLOPS = 1_000_000
SPARE_ROWS = 16
HOLDER, PLACE, LIVE, SIDE, ROWS = 0, 1, 2, 3, 4


def omega_of(index, freq_count):
    return (2.0 * index.astype(jnp.float32) + 1.0 - freq_count) * (CUTOFF / freq_count)


def encoded(gap):
    share = jnp.minimum(jnp.abs(gap) * (1.0 / GAP_LIMIT), 1.0)
    root = jnp.exp2(jnp.log2(jnp.maximum(share, 1e-37)) * (1.0 / CODE_POWER))
    code = jnp.floor(root * CODE_LIMIT + 0.5)
    return jnp.where(gap < 0, -code, code).astype(jnp.int32).astype(jnp.int16)


def decoded(code):
    root = code.astype(jnp.float32) * (1.0 / CODE_LIMIT)
    square = root * root
    return (root * GAP_LIMIT) * (square * square)


def encode_kernel(gap, code):
    code[...] = encoded(gap[...])


def join_kernel(first, second, after, joined):
    rows = joined.shape[1]
    joined[0] = first[:rows]
    joined[1] = second[:rows]


def split(value):
    high = value.astype(jnp.bfloat16)
    return high, (value - high.astype(jnp.float32)).astype(jnp.bfloat16)


def fill_tables(dims, meta, row_from, phonon, tables):
    freq_count, segments, segment_rows, padded_rows, modes = dims
    shape = (padded_rows, segment_rows)
    row_omega = omega_of(lax.broadcasted_iota(jnp.int32, shape, 0) + meta[row_from], freq_count)
    for segment in range(len(tables)):
        col = lax.broadcasted_iota(jnp.int32, shape, 1) + meta[1 + segment]
        col_omega = omega_of(col, freq_count)
        near = (row_omega - col_omega) ** 2
        far = (row_omega + col_omega) ** 2
        cross = 4.0 * (row_omega * col_omega)
        for mode in range(modes):
            strength = phonon[mode]
            below = near + strength * strength
            above = far + strength * strength
            common = (2.0 * strength) / (below * above)
            columns = slice(mode * segment_rows, (mode + 1) * segment_rows)
            for part, value in enumerate((common * (below + above), common * cross)):
                high, low = split(value)
                tables[segment][part, :padded_rows, columns] = high
                if tables[segment].shape[1] > padded_rows:
                    tables[segment][part, padded_rows:, columns] = low


def other_tables_kernel(dims, meta, phonon, *tables):
    fill_tables(dims, meta, 2, phonon, tables)


def tables_kernel(
    dims, sides, meta, phonon, pair_cols, pair_count, block_order, coupling, plan, weights, *tables
):
    freq_count, segments, segment_rows, padded_rows, modes = dims
    blocks, slots = coupling.shape[:2]
    size = coupling.shape[3]
    for at in range(1 + segments):
        plan[ROWS, at] = meta[at]
    for block in range(blocks):
        for slot in range(slots):
            wanted = pair_cols[block, slot]
            position = jnp.int32(0)
            for at in range(block_order.shape[0]):
                position = jnp.where(block_order[at] == wanted, at, position)
            pair = block * slots + slot
            holder = position // blocks
            plan[HOLDER, pair] = (holder // sides) ^ meta[1 + segments]
            plan[SIDE, pair] = (holder % sides) ^ meta[2 + segments]
            plan[PLACE, pair] = position % blocks
            plan[LIVE, pair] = (pair_count[block] > slot).astype(jnp.int32)
    fill_tables(dims, meta, 0, phonon, tables)
    for block in range(blocks):
        for slot in range(slots):
            for mode in range(modes):
                weights[
                    block, slot * size : (slot + 1) * size, mode * size : (mode + 1) * size
                ] = coupling[block, slot, mode].T


def step_kernel(dims, segment, span, sides, coded, final, keep, parted, plan, *refs):
    freq_count, segments, segment_rows, padded_rows, modes = dims
    refs = list(refs)
    first, last = segment == 0, segment == segments - 1
    take = lambda count: [refs.pop() for _ in range(count)][::-1]
    copied = last and final
    if copied:
        *held, sems = take(3)
    terms = [] if keep else take(2 if first else 1)
    ratios = refs.pop()
    terms = terms or take(2)
    outs = take(2 if copied else 1)
    inputs = refs
    before = [inputs.pop() for _ in range(0 if first else parted)][::-1]
    weights, table = inputs[-2:]
    pieces = []
    for piece in inputs[:-2]:
        if len(piece.shape) == 3:
            pieces += [piece.at[at] for at in range(piece.shape[0])]
        else:
            pieces.append(piece)
    holders = len(pieces) // sides
    blocks = span[1] - span[0]
    size = LANES
    slots = weights.shape[1] // size
    shape = (segment_rows, size)
    col = lax.broadcasted_iota(jnp.int32, shape, 0) + plan[ROWS, 1 + segment]
    col_omega = omega_of(col, freq_count)
    square = col_omega * col_omega

    def fetch(pair):
        column = pl.multiple_of(plan[PLACE, pair] * size, size)
        wanted = plan[SIDE, pair] * holders + plan[HOLDER, pair]
        value = pieces[0][:, pl.ds(column, size)]
        for at in range(1, len(pieces)):
            value = lax.select(wanted == at, pieces[at][:, pl.ds(column, size)], value)
        return decoded(value) if coded else value

    def find_ratios(block):
        for slot in range(slots):
            pair = (span[0] + block) * slots + slot
            gap = fetch(pair)
            live = plan[LIVE, pair].astype(jnp.float32)
            inverse = lax.rsqrt(square + gap * gap) * live
            lanes = slice(slot * size, (slot + 1) * size)
            ratios[block, :segment_rows, lanes] = (gap * inverse).astype(jnp.bfloat16)
            ratios[block, segment_rows:, lanes] = (col_omega * inverse).astype(jnp.bfloat16)

    def find_terms(block):
        lanes = slice(block * size, (block + 1) * size)
        for start in range(0, modes, 2):
            stop = min(start + 2, modes)
            found = jnp.dot(
                ratios[block],
                weights[span[0] + block, :, start * size : stop * size],
                preferred_element_type=jnp.float32,
            )
            pieces_of = split(found) if len(terms) > 1 else [found.astype(jnp.bfloat16)]
            for mode in range(start, stop):
                rows = slice(mode * segment_rows, (mode + 1) * segment_rows)
                taken = slice((mode - start) * size, (mode - start + 1) * size)
                for part in range(2):
                    source = slice(part * segment_rows, (part + 1) * segment_rows)
                    for held_terms, value in zip(terms, pieces_of):
                        held_terms[part, rows, lanes] = value[source, taken]

    def earlier(part, lanes):
        width = before[0].shape[-1]
        start = lanes.start % width
        return before[lanes.start // width][part, :, start : start + lanes.stop - lanes.start]

    def find_sums(lanes):
        sums = []
        for part in range(2):
            views = [held_terms.at[part, :, lanes] for held_terms in terms]
            total = table_sums(padded_rows, table.at[part], *views)
            sums.append(total if first else total + earlier(part, lanes))
        if not last:
            for part in range(2):
                outs[0][part, :, lanes] = sums[part]
            return
        own_rows = outs[0].shape[0]
        width = lanes.stop - lanes.start
        row = lax.broadcasted_iota(jnp.int32, (own_rows, width), 0) + plan[ROWS, 0]
        temperature = CUTOFF / freq_count
        renorm = 1.0 + temperature * sums[1][:own_rows] / omega_of(row, freq_count)
        gap = temperature * sums[0][:own_rows] / renorm
        if not final:
            outs[0][:, lanes] = encoded(gap) if coded else gap
            return
        for at, value in enumerate((gap, renorm)):
            held[at][:, lanes] = value
            copy_out(at, lanes).start()

    def copy_out(at, lanes):
        width = lanes.stop - lanes.start
        return pltpu.make_async_copy(
            held[at].at[:, pl.ds(lanes.start, width)],
            outs[at].at[:, pl.ds(lanes.start, width)],
            sems.at[at, lanes.start // width],
        )

    halves = [slice(start * size, (start + 2) * size) for start in range(0, blocks, 2)]
    for block in range(blocks):
        find_ratios(block)
    for block in range(blocks):
        find_terms(block)
        if block % 2 == 1 and block > 1:
            find_sums(halves[block // 2 - 1])
    find_sums(halves[-1])
    if copied:
        for lanes in halves:
            for at in range(2):
                copy_out(at, lanes).wait()


def table_sums(padded_rows, table, high, low=None):
    both = jnp.dot(table[...], high[...], preferred_element_type=jnp.float32)
    if table.shape[0] == padded_rows:
        return both
    rest = jnp.dot(table[:padded_rows], low[...], preferred_element_type=jnp.float32)
    return both[:padded_rows] + (both[padded_rows:] + rest)


def other_rows_kernel(dims, plan, *refs):
    freq_count, segments, segment_rows, padded_rows, modes = dims
    tables, terms, code = refs[:segments], refs[segments:-1], refs[-1]
    sums = []
    for part in range(2):
        total = None
        for segment in range(segments):
            views = [terms[2 * segment + at].at[part] for at in range(2)]
            piece = table_sums(padded_rows, tables[segment].at[part], *views)
            total = piece if total is None else total + piece
        sums.append(total)
    row = lax.broadcasted_iota(jnp.int32, (padded_rows, code.shape[1]), 0) + plan[ROWS, 2]
    temperature = CUTOFF / freq_count
    renorm = 1.0 + temperature * sums[1] / omega_of(row, freq_count)
    code[:padded_rows] = encoded(temperature * sums[0] / renorm)
    code[padded_rows:] = jnp.zeros((SPARE_ROWS, code.shape[1]), code.dtype)


SWAP = [(0, 1), (1, 0)]


def gather_general(gap, half_groups):
    everyone = lax.all_gather(gap, "state", axis=0, tiled=False)
    rows = lax.all_gather(everyone, "freq", axis=1, tiled=True)
    own_rows = gap.shape[0]
    start = (lax.axis_index("freq") // half_groups) * (half_groups * own_rows)
    return [lax.dynamic_slice_in_dim(rows, start, half_groups * own_rows, 1)]


def on_device(pairwise, freq_groups, gap_in, coupling, pair_cols, pair_count, block_order, phonon):
    own_rows, row_width = gap_in.shape
    blocks, slots, modes, size, _ = coupling.shape
    freq_count = own_rows * freq_groups
    half_rows = freq_count // 2
    half_groups = freq_groups // 2
    padded_rows = -(-own_rows // 16) * 16
    if pairwise:
        segments, sides = 2, 2
        half = lax.axis_index("zhi") * half_rows
        own = half + lax.axis_index("zlo") * own_rows
        other = half + (1 - lax.axis_index("zlo")) * own_rows
        meta = [own, own, other, lax.axis_index("x"), lax.axis_index("core")]
    else:
        segments, sides = 1, 1
        freq_at = lax.axis_index("freq")
        meta = [freq_at * own_rows, (freq_at // half_groups) * half_rows, 0, 0]
    meta = jnp.stack([jnp.asarray(value, jnp.int32) for value in meta])
    segment_rows = half_rows // segments
    dims = (freq_count, segments, segment_rows, padded_rows, modes)
    smem = pl.BlockSpec(memory_space=pltpu.SMEM)
    vmem = pl.BlockSpec(memory_space=pltpu.VMEM)
    link_type = jnp.int16 if pairwise else jnp.float32

    passed = gap_in
    if pairwise:
        passed = pl.pallas_call(
            encode_kernel,
            out_shape=jax.ShapeDtypeStruct(gap_in.shape, link_type),
            in_specs=[vmem],
            out_specs=vmem,
            compiler_params=pltpu.CompilerParams(vmem_limit_bytes=8 << 20),
            cost_estimate=pl.CostEstimate(
                flops=10_000_000_000, bytes_accessed=40_000_000, transcendentals=0
            ),
            name="encode",
        )(gap_in)

    near_table, far_table = [
        jax.ShapeDtypeStruct((2, count * padded_rows, modes * segment_rows), jnp.bfloat16)
        for count in (2, 1)
    ]
    plan, weights, *tables = pl.pallas_call(
        functools.partial(tables_kernel, dims, sides),
        out_shape=[
            jax.ShapeDtypeStruct((5, max(blocks * slots, 1 + segments)), jnp.int32),
            jax.ShapeDtypeStruct((blocks, slots * size, modes * size), jnp.bfloat16),
        ]
        + [near_table, far_table][:segments],
        in_specs=[smem] * 5 + [vmem],
        out_specs=[smem] + [vmem] * (1 + segments),
        compiler_params=pltpu.CompilerParams(vmem_limit_bytes=24 << 20),
        cost_estimate=pl.CostEstimate(
            flops=10_000_000, bytes_accessed=8_000_000, transcendentals=0
        ),
        name="tables",
    )(meta, phonon, pair_cols, pair_count, block_order, coupling)

    full = jax.ShapeDtypeStruct(gap_in.shape, jnp.float32)
    passed_out = jax.ShapeDtypeStruct(gap_in.shape, link_type)
    step_params = dict(
        compiler_params=pltpu.CompilerParams(vmem_limit_bytes=24 << 20),
        cost_estimate=pl.CostEstimate(
            flops=STEP_FLOPS, bytes_accessed=100_000, transcendentals=0
        ),
    )

    def step(plan, segment, final, pieces, before, keep=False, span=(0, blocks)):
        copied = final and segment == segments - 1
        width = (span[1] - span[0]) * size
        terms_shape = (2, modes * segment_rows, width)
        if segment < segments - 1:
            outs = [jax.ShapeDtypeStruct((2, padded_rows, width), jnp.float32)]
        else:
            outs = [full, full] if final else [passed_out]
        out_specs = [pl.BlockSpec(memory_space=pl.ANY) if copied else vmem] * len(outs)
        scratch = [pltpu.VMEM((span[1] - span[0], 2 * segment_rows, slots * size), jnp.bfloat16)]
        if keep:
            outs += [jax.ShapeDtypeStruct(terms_shape, jnp.bfloat16)] * 2
            out_specs += [vmem] * 2
        else:
            scratch += [pltpu.VMEM(terms_shape, jnp.bfloat16)] * (2 if segment == 0 else 1)
        if copied:
            scratch += [pltpu.VMEM(gap_in.shape, jnp.float32)] * 2
            scratch += [pltpu.SemaphoreType.DMA((2, blocks // 2))]
        inputs = [*pieces, weights, tables[segment], *before]
        return pl.pallas_call(
            functools.partial(
                step_kernel, dims, segment, span, sides, pairwise, final, keep, len(before)
            ),
            out_shape=outs,
            in_specs=[smem] + [vmem] * len(inputs),
            out_specs=out_specs,
            scratch_shapes=scratch,
            name="step",
            **step_params,
        )(plan, *inputs)

    if not pairwise:
        for iteration in range(ITERS):
            final = iteration == ITERS - 1
            results = step(plan, 0, final, gather_general(passed, half_groups), [])
            passed = results[0]
        return tuple(results)

    def join(near, across, after):
        return pl.pallas_call(
            join_kernel,
            out_shape=jax.ShapeDtypeStruct((2, *gap_in.shape), near.dtype),
            in_specs=[vmem, vmem, pl.BlockSpec(memory_space=pl.ANY)],
            out_specs=vmem,
            compiler_params=pltpu.CompilerParams(vmem_limit_bytes=4 << 20),
            cost_estimate=pl.CostEstimate(flops=1000, bytes_accessed=1000, transcendentals=0),
            name="join",
        )(near, across, after)

    def with_core(near):
        return near + [lax.ppermute(piece, "core", SWAP) for piece in near]

    other_tables = pl.pallas_call(
        functools.partial(other_tables_kernel, dims),
        out_shape=[far_table, near_table],
        in_specs=[smem, smem],
        out_specs=[vmem] * segments,
        compiler_params=pltpu.CompilerParams(vmem_limit_bytes=12 << 20),
        cost_estimate=pl.CostEstimate(
            flops=10_000_000, bytes_accessed=3_000_000, transcendentals=0
        ),
        name="other_tables",
    )(meta, phonon)
    along_x = lax.ppermute(passed, "x", SWAP)
    along_z = lax.ppermute(passed, "zlo", SWAP)
    along_x, plan = lax.optimization_barrier((along_x, plan))
    relayed = lax.ppermute(along_z, "x", SWAP)
    partial, *near_terms = step(plan, 0, False, with_core([passed, along_x]), [], keep=True)
    far = join(along_z, relayed, partial)
    pieces = [far, lax.ppermute(far, "core", SWAP)]
    plan, *other_tables = lax.optimization_barrier((plan, *other_tables))
    own, *far_terms = step(plan, 1, False, pieces, [partial], keep=True)
    inputs = [*other_tables, *near_terms, *far_terms]
    other = pl.pallas_call(
        functools.partial(other_rows_kernel, dims),
        out_shape=jax.ShapeDtypeStruct((own_rows + SPARE_ROWS, row_width), link_type),
        in_specs=[smem] + [vmem] * len(inputs),
        out_specs=vmem,
        name="other_rows",
        **step_params,
    )(plan, *inputs)
    along_x = lax.ppermute(own, "x", SWAP)
    near = with_core([own, along_x])
    middle = blocks // 2
    partial = step(plan, 0, True, near, [], span=(0, middle))
    far = join(other, lax.ppermute(other, "x", SWAP), *partial)
    partial += step(plan, 0, True, near, [], span=(middle, blocks))
    return tuple(step(plan, 1, True, [far, lax.ppermute(far, "core", SWAP)], partial))


def solution(mesh):
    shape = tuple(mesh.shape[axis] for axis in ("parts", "freq", "state"))
    pairwise = shape[1:] == (4, 4)
    parts, freq, state = "parts", "freq", "state"
    if pairwise:
        names = ("parts", "zhi", "zlo", "x", "core")
        mesh = jax.sharding.Mesh(mesh.devices.reshape(shape[0], 2, 2, 2, 2), names)
        freq, state = ("zhi", "zlo"), ("x", "core")
    rows = ("parts", *freq) if pairwise else ("parts", freq)
    groups = ("parts", *state) if pairwise else ("parts", state)
    return jax.shard_map(
        functools.partial(on_device, pairwise, shape[1]),
        mesh=mesh,
        in_specs=(
            P(rows, state),
            P(groups, None, None, None, None),
            P(groups, None),
            P(groups),
            P(parts),
            P(parts),
        ),
        out_specs=(P(rows, state), P(rows, state)),
        check_vma=False,
    )
```

```python
import functools

import jax
import jax.numpy as jnp
from jax import lax
from jax.experimental import pallas as pl
from jax.experimental.pallas import tpu as pltpu
from jax.sharding import PartitionSpec as P

ITERS = 2
CUTOFF = 4.0
LANES = 128
GAP_LIMIT = 10.0
CODE_LIMIT = 32767.0
CODE_POWER = 5
STEP_FLOPS = 1_000_000
SPARE_ROWS = 16
HOLDER, PLACE, LIVE, SIDE, ROWS = 0, 1, 2, 3, 4


def omega_of(index, freq_count):
    return (2.0 * index.astype(jnp.float32) + 1.0 - freq_count) * (CUTOFF / freq_count)


def encoded(gap):
    share = jnp.minimum(jnp.abs(gap) * (1.0 / GAP_LIMIT), 1.0)
    root = jnp.exp2(jnp.log2(jnp.maximum(share, 1e-37)) * (1.0 / CODE_POWER))
    code = jnp.floor(root * CODE_LIMIT + 0.5)
    return jnp.where(gap < 0, -code, code).astype(jnp.int32).astype(jnp.int16)


def decoded(code):
    root = code.astype(jnp.float32) * (1.0 / CODE_LIMIT)
    square = root * root
    return (root * GAP_LIMIT) * (square * square)


def encode_kernel(gap, code):
    code[...] = encoded(gap[...])


def join_kernel(first, second, after, joined):
    rows = joined.shape[1]
    joined[0] = first[:rows]
    joined[1] = second[:rows]


def split(value):
    high = value.astype(jnp.bfloat16)
    return high, (value - high.astype(jnp.float32)).astype(jnp.bfloat16)


def fill_tables(dims, meta, row_from, phonon, tables):
    freq_count, segments, segment_rows, padded_rows, modes = dims
    shape = (padded_rows, segment_rows)
    row_omega = omega_of(lax.broadcasted_iota(jnp.int32, shape, 0) + meta[row_from], freq_count)
    for segment in range(len(tables)):
        col = lax.broadcasted_iota(jnp.int32, shape, 1) + meta[1 + segment]
        col_omega = omega_of(col, freq_count)
        near = (row_omega - col_omega) ** 2
        far = (row_omega + col_omega) ** 2
        cross = 4.0 * (row_omega * col_omega)
        for mode in range(modes):
            strength = phonon[mode]
            below = near + strength * strength
            above = far + strength * strength
            common = (2.0 * strength) / (below * above)
            columns = slice(mode * segment_rows, (mode + 1) * segment_rows)
            for part, value in enumerate((common * (below + above), common * cross)):
                high, low = split(value)
                tables[segment][part, :padded_rows, columns] = high
                if tables[segment].shape[1] > padded_rows:
                    tables[segment][part, padded_rows:, columns] = low


def other_tables_kernel(dims, meta, phonon, *tables):
    fill_tables(dims, meta, 2, phonon, tables)


def tables_kernel(
    dims, sides, meta, phonon, pair_cols, pair_count, block_order, coupling, plan, weights, *tables
):
    freq_count, segments, segment_rows, padded_rows, modes = dims
    blocks, slots = coupling.shape[:2]
    size = coupling.shape[3]
    for at in range(1 + segments):
        plan[ROWS, at] = meta[at]
    for block in range(blocks):
        for slot in range(slots):
            wanted = pair_cols[block, slot]
            position = jnp.int32(0)
            for at in range(block_order.shape[0]):
                position = jnp.where(block_order[at] == wanted, at, position)
            pair = block * slots + slot
            holder = position // blocks
            plan[HOLDER, pair] = (holder // sides) ^ meta[1 + segments]
            plan[SIDE, pair] = (holder % sides) ^ meta[2 + segments]
            plan[PLACE, pair] = position % blocks
            plan[LIVE, pair] = (pair_count[block] > slot).astype(jnp.int32)
    fill_tables(dims, meta, 0, phonon, tables)
    for block in range(blocks):
        for slot in range(slots):
            for mode in range(modes):
                weights[
                    block, slot * size : (slot + 1) * size, mode * size : (mode + 1) * size
                ] = coupling[block, slot, mode].T


def repeat(count, body):
    lax.fori_loop(0, count, lambda at, none: body(at), None)


def lanes_of(start, width):
    return pl.ds(pl.multiple_of(start, LANES), width)


def step_kernel(dims, segment, span, sides, coded, final, keep, parted, plan, *refs):
    freq_count, segments, segment_rows, padded_rows, modes = dims
    refs = list(refs)
    first, last = segment == 0, segment == segments - 1
    take = lambda count: [refs.pop() for _ in range(count)][::-1]
    copied = last and final
    if copied:
        *held, sems = take(3)
    sums = refs.pop()
    terms = [] if keep else take(2 if first else 1)
    ratios = refs.pop()
    terms = terms or take(2)
    outs = take(2 if copied else 1)
    inputs = refs
    before = [inputs.pop() for _ in range(0 if first else parted)][::-1]
    weights, table = inputs[-2:]
    pieces = []
    for piece in inputs[:-2]:
        if len(piece.shape) == 3:
            pieces += [piece.at[at] for at in range(piece.shape[0])]
        else:
            pieces.append(piece)
    holders = len(pieces) // sides
    blocks = span[1] - span[0]
    size = LANES
    slots = weights.shape[1] // size
    shape = (segment_rows, size)
    col = lax.broadcasted_iota(jnp.int32, shape, 0) + plan[ROWS, 1 + segment]
    col_omega = omega_of(col, freq_count)
    square = col_omega * col_omega

    def fetch(pair):
        column = pl.multiple_of(plan[PLACE, pair] * size, size)
        wanted = plan[SIDE, pair] * holders + plan[HOLDER, pair]
        value = pieces[0][:, pl.ds(column, size)]
        for at in range(1, len(pieces)):
            value = lax.select(wanted == at, pieces[at][:, pl.ds(column, size)], value)
        return decoded(value) if coded else value

    def find_ratios(block):
        for slot in range(slots):
            pair = (span[0] + block) * slots + slot
            gap = fetch(pair)
            live = plan[LIVE, pair].astype(jnp.float32)
            inverse = lax.rsqrt(square + gap * gap) * live
            lanes = slice(slot * size, (slot + 1) * size)
            ratios[block, :segment_rows, lanes] = (gap * inverse).astype(jnp.bfloat16)
            ratios[block, segment_rows:, lanes] = (col_omega * inverse).astype(jnp.bfloat16)

    def find_terms(block):
        lanes = lanes_of(block * size, size)
        for start in range(0, modes, 2):
            stop = min(start + 2, modes)
            found = jnp.dot(
                ratios[block],
                weights[span[0] + block, :, start * size : stop * size],
                preferred_element_type=jnp.float32,
            )
            pieces_of = split(found) if len(terms) > 1 else [found.astype(jnp.bfloat16)]
            for mode in range(start, stop):
                rows = slice(mode * segment_rows, (mode + 1) * segment_rows)
                taken = slice((mode - start) * size, (mode - start + 1) * size)
                for part in range(2):
                    source = slice(part * segment_rows, (part + 1) * segment_rows)
                    for held_terms, value in zip(terms, pieces_of):
                        held_terms[part, rows, lanes] = value[source, taken]

    def earlier(part, lanes):
        width = before[0].shape[-1]
        start = lanes.start % width
        return before[lanes.start // width][part, :, start : start + lanes.stop - lanes.start]

    def find_sums(lanes):
        def find(part):
            views = [held_terms.at[part, :, lanes] for held_terms in terms]
            total = table_sums(padded_rows, table.at[part], *views)
            sums[part] = total if first else total + earlier(part, lanes)

        repeat(2, find)
        if not last:
            for part in range(2):
                outs[0][part, :, lanes] = sums[part]
            return
        own_rows = outs[0].shape[0]
        width = lanes.stop - lanes.start
        row = lax.broadcasted_iota(jnp.int32, (own_rows, width), 0) + plan[ROWS, 0]
        temperature = CUTOFF / freq_count
        renorm = 1.0 + temperature * sums[1][:own_rows] / omega_of(row, freq_count)
        gap = temperature * sums[0][:own_rows] / renorm
        if not final:
            outs[0][:, lanes] = encoded(gap) if coded else gap
            return
        for at, value in enumerate((gap, renorm)):
            held[at][:, lanes] = value
            copy_out(at, lanes).start()

    def copy_out(at, lanes):
        width = lanes.stop - lanes.start
        return pltpu.make_async_copy(
            held[at].at[:, pl.ds(lanes.start, width)],
            outs[at].at[:, pl.ds(lanes.start, width)],
            sems.at[at, lanes.start // width],
        )

    halves = [slice(start * size, (start + 2) * size) for start in range(0, blocks, 2)]

    def find_block(block):
        find_ratios(block)
        find_terms(block)

    repeat(blocks, find_block)
    for lanes in halves:
        find_sums(lanes)
    if copied:
        for lanes in halves:
            for at in range(2):
                copy_out(at, lanes).wait()


def table_sums(padded_rows, table, high, low=None):
    both = jnp.dot(table[...], high[...], preferred_element_type=jnp.float32)
    if table.shape[0] == padded_rows:
        return both
    rest = jnp.dot(table[:padded_rows], low[...], preferred_element_type=jnp.float32)
    return both[:padded_rows] + (both[padded_rows:] + rest)


def other_rows_kernel(dims, plan, *refs):
    freq_count, segments, segment_rows, padded_rows, modes = dims
    tables, terms, code, sums = refs[:segments], refs[segments:-2], refs[-2], refs[-1]

    def find(part):
        total = None
        for segment in range(segments):
            views = [terms[2 * segment + at].at[part] for at in range(2)]
            piece = table_sums(padded_rows, tables[segment].at[part], *views)
            total = piece if total is None else total + piece
        sums[part] = total

    repeat(2, find)
    row = lax.broadcasted_iota(jnp.int32, (padded_rows, code.shape[1]), 0) + plan[ROWS, 2]
    temperature = CUTOFF / freq_count
    renorm = 1.0 + temperature * sums[1] / omega_of(row, freq_count)
    code[:padded_rows] = encoded(temperature * sums[0] / renorm)
    code[padded_rows:] = jnp.zeros((SPARE_ROWS, code.shape[1]), code.dtype)


SWAP = [(0, 1), (1, 0)]


def gather_general(gap, half_groups):
    everyone = lax.all_gather(gap, "state", axis=0, tiled=False)
    rows = lax.all_gather(everyone, "freq", axis=1, tiled=True)
    own_rows = gap.shape[0]
    start = (lax.axis_index("freq") // half_groups) * (half_groups * own_rows)
    return [lax.dynamic_slice_in_dim(rows, start, half_groups * own_rows, 1)]


def on_device(pairwise, freq_groups, gap_in, coupling, pair_cols, pair_count, block_order, phonon):
    own_rows, row_width = gap_in.shape
    blocks, slots, modes, size, _ = coupling.shape
    freq_count = own_rows * freq_groups
    half_rows = freq_count // 2
    half_groups = freq_groups // 2
    padded_rows = -(-own_rows // 16) * 16
    if pairwise:
        segments, sides = 2, 2
        half = lax.axis_index("zhi") * half_rows
        own = half + lax.axis_index("zlo") * own_rows
        other = half + (1 - lax.axis_index("zlo")) * own_rows
        meta = [own, own, other, lax.axis_index("x"), lax.axis_index("core")]
    else:
        segments, sides = 1, 1
        freq_at = lax.axis_index("freq")
        meta = [freq_at * own_rows, (freq_at // half_groups) * half_rows, 0, 0]
    meta = jnp.stack([jnp.asarray(value, jnp.int32) for value in meta])
    segment_rows = half_rows // segments
    dims = (freq_count, segments, segment_rows, padded_rows, modes)
    smem = pl.BlockSpec(memory_space=pltpu.SMEM)
    vmem = pl.BlockSpec(memory_space=pltpu.VMEM)
    link_type = jnp.int16 if pairwise else jnp.float32

    passed = gap_in
    if pairwise:
        passed = pl.pallas_call(
            encode_kernel,
            out_shape=jax.ShapeDtypeStruct(gap_in.shape, link_type),
            in_specs=[vmem],
            out_specs=vmem,
            compiler_params=pltpu.CompilerParams(vmem_limit_bytes=8 << 20),
            cost_estimate=pl.CostEstimate(
                flops=10_000_000_000, bytes_accessed=40_000_000, transcendentals=0
            ),
            name="encode",
        )(gap_in)

    near_table, far_table = [
        jax.ShapeDtypeStruct((2, count * padded_rows, modes * segment_rows), jnp.bfloat16)
        for count in (2, 1)
    ]
    plan, weights, *tables = pl.pallas_call(
        functools.partial(tables_kernel, dims, sides),
        out_shape=[
            jax.ShapeDtypeStruct((5, max(blocks * slots, 1 + segments)), jnp.int32),
            jax.ShapeDtypeStruct((blocks, slots * size, modes * size), jnp.bfloat16),
        ]
        + [near_table, far_table][:segments],
        in_specs=[smem] * 5 + [vmem],
        out_specs=[smem] + [vmem] * (1 + segments),
        compiler_params=pltpu.CompilerParams(vmem_limit_bytes=24 << 20),
        cost_estimate=pl.CostEstimate(
            flops=10_000_000, bytes_accessed=8_000_000, transcendentals=0
        ),
        name="tables",
    )(meta, phonon, pair_cols, pair_count, block_order, coupling)

    full = jax.ShapeDtypeStruct(gap_in.shape, jnp.float32)
    passed_out = jax.ShapeDtypeStruct(gap_in.shape, link_type)
    step_params = dict(
        compiler_params=pltpu.CompilerParams(vmem_limit_bytes=24 << 20),
        cost_estimate=pl.CostEstimate(
            flops=STEP_FLOPS, bytes_accessed=100_000, transcendentals=0
        ),
    )

    def step(plan, segment, final, pieces, before, keep=False, span=(0, blocks)):
        copied = final and segment == segments - 1
        width = (span[1] - span[0]) * size
        terms_shape = (2, modes * segment_rows, width)
        if segment < segments - 1:
            outs = [jax.ShapeDtypeStruct((2, padded_rows, width), jnp.float32)]
        else:
            outs = [full, full] if final else [passed_out]
        out_specs = [pl.BlockSpec(memory_space=pl.ANY) if copied else vmem] * len(outs)
        scratch = [pltpu.VMEM((span[1] - span[0], 2 * segment_rows, slots * size), jnp.bfloat16)]
        if keep:
            outs += [jax.ShapeDtypeStruct(terms_shape, jnp.bfloat16)] * 2
            out_specs += [vmem] * 2
        else:
            scratch += [pltpu.VMEM(terms_shape, jnp.bfloat16)] * (2 if segment == 0 else 1)
        scratch += [pltpu.VMEM((2, padded_rows, 2 * size), jnp.float32)]
        if copied:
            scratch += [pltpu.VMEM(gap_in.shape, jnp.float32)] * 2
            scratch += [pltpu.SemaphoreType.DMA((2, blocks // 2))]
        inputs = [*pieces, weights, tables[segment], *before]
        return pl.pallas_call(
            functools.partial(
                step_kernel, dims, segment, span, sides, pairwise, final, keep, len(before)
            ),
            out_shape=outs,
            in_specs=[smem] + [vmem] * len(inputs),
            out_specs=out_specs,
            scratch_shapes=scratch,
            name="step",
            **step_params,
        )(plan, *inputs)

    if not pairwise:
        for iteration in range(ITERS):
            final = iteration == ITERS - 1
            results = step(plan, 0, final, gather_general(passed, half_groups), [])
            passed = results[0]
        return tuple(results)

    def join(near, across, after):
        return pl.pallas_call(
            join_kernel,
            out_shape=jax.ShapeDtypeStruct((2, *gap_in.shape), near.dtype),
            in_specs=[vmem, vmem, pl.BlockSpec(memory_space=pl.ANY)],
            out_specs=vmem,
            compiler_params=pltpu.CompilerParams(vmem_limit_bytes=4 << 20),
            cost_estimate=pl.CostEstimate(flops=1000, bytes_accessed=1000, transcendentals=0),
            name="join",
        )(near, across, after)

    def with_core(near):
        return near + [lax.ppermute(piece, "core", SWAP) for piece in near]

    other_tables = pl.pallas_call(
        functools.partial(other_tables_kernel, dims),
        out_shape=[far_table, near_table],
        in_specs=[smem, smem],
        out_specs=[vmem] * segments,
        compiler_params=pltpu.CompilerParams(vmem_limit_bytes=12 << 20),
        cost_estimate=pl.CostEstimate(
            flops=10_000_000, bytes_accessed=3_000_000, transcendentals=0
        ),
        name="other_tables",
    )(meta, phonon)
    along_x = lax.ppermute(passed, "x", SWAP)
    along_z = lax.ppermute(passed, "zlo", SWAP)
    along_x, plan = lax.optimization_barrier((along_x, plan))
    relayed = lax.ppermute(along_z, "x", SWAP)
    partial, *near_terms = step(plan, 0, False, with_core([passed, along_x]), [], keep=True)
    far = join(along_z, relayed, partial)
    pieces = [far, lax.ppermute(far, "core", SWAP)]
    plan, *other_tables = lax.optimization_barrier((plan, *other_tables))
    own, *far_terms = step(plan, 1, False, pieces, [partial], keep=True)
    inputs = [*other_tables, *near_terms, *far_terms]
    other = pl.pallas_call(
        functools.partial(other_rows_kernel, dims),
        out_shape=jax.ShapeDtypeStruct((own_rows + SPARE_ROWS, row_width), link_type),
        in_specs=[smem] + [vmem] * len(inputs),
        out_specs=vmem,
        scratch_shapes=[pltpu.VMEM((2, padded_rows, row_width), jnp.float32)],
        name="other_rows",
        **step_params,
    )(plan, *inputs)
    along_x = lax.ppermute(own, "x", SWAP)
    near = with_core([own, along_x])
    middle = blocks // 2
    partial = step(plan, 0, True, near, [], span=(0, middle))
    far = join(other, lax.ppermute(other, "x", SWAP), *partial)
    partial += step(plan, 0, True, near, [], span=(middle, blocks))
    return tuple(step(plan, 1, True, [far, lax.ppermute(far, "core", SWAP)], partial))


def solution(mesh):
    shape = tuple(mesh.shape[axis] for axis in ("parts", "freq", "state"))
    pairwise = shape[1:] == (4, 4)
    parts, freq, state = "parts", "freq", "state"
    if pairwise:
        names = ("parts", "zhi", "zlo", "x", "core")
        mesh = jax.sharding.Mesh(mesh.devices.reshape(shape[0], 2, 2, 2, 2), names)
        freq, state = ("zhi", "zlo"), ("x", "core")
    rows = ("parts", *freq) if pairwise else ("parts", freq)
    groups = ("parts", *state) if pairwise else ("parts", state)
    return jax.shard_map(
        functools.partial(on_device, pairwise, shape[1]),
        mesh=mesh,
        in_specs=(
            P(rows, state),
            P(groups, None, None, None, None),
            P(groups, None),
            P(groups),
            P(parts),
            P(parts),
        ),
        out_specs=(P(rows, state), P(rows, state)),
        check_vma=False,
    )
```

```python
import functools

import jax
import jax.numpy as jnp
from jax import lax
from jax.experimental import pallas as pl
from jax.experimental.pallas import tpu as pltpu
from jax.sharding import PartitionSpec as P

ITERS = 2
CUTOFF = 4.0
LANES = 128
GAP_LIMIT = 10.0
CODE_LIMIT = 32767.0
CODE_POWER = 5
STEP_FLOPS = 1_000_000
SPARE_ROWS = 16
HOLDER, PLACE, LIVE, SIDE, ROWS = 0, 1, 2, 3, 4


def omega_of(index, freq_count):
    return (2.0 * index.astype(jnp.float32) + 1.0 - freq_count) * (CUTOFF / freq_count)


def encoded(gap):
    share = jnp.minimum(jnp.abs(gap) * (1.0 / GAP_LIMIT), 1.0)
    root = jnp.exp2(jnp.log2(jnp.maximum(share, 1e-37)) * (1.0 / CODE_POWER))
    code = jnp.floor(root * CODE_LIMIT + 0.5)
    return jnp.where(gap < 0, -code, code).astype(jnp.int32).astype(jnp.int16)


def decoded(code):
    root = code.astype(jnp.float32) * (1.0 / CODE_LIMIT)
    square = root * root
    return (root * GAP_LIMIT) * (square * square)


def encode_kernel(gap, code):
    code[...] = encoded(gap[...])


def join_kernel(first, second, after, joined):
    rows = joined.shape[1]
    joined[0] = first[:rows]
    joined[1] = second[:rows]


def split(value):
    high = value.astype(jnp.bfloat16)
    return high, (value - high.astype(jnp.float32)).astype(jnp.bfloat16)


def fill_tables(dims, meta, row_from, phonon, tables):
    freq_count, segments, segment_rows, padded_rows, modes = dims
    shape = (padded_rows, segment_rows)
    row_omega = omega_of(lax.broadcasted_iota(jnp.int32, shape, 0) + meta[row_from], freq_count)
    for segment in range(len(tables)):
        col = lax.broadcasted_iota(jnp.int32, shape, 1) + meta[1 + segment]
        col_omega = omega_of(col, freq_count)
        near = (row_omega - col_omega) ** 2
        far = (row_omega + col_omega) ** 2
        cross = 4.0 * (row_omega * col_omega)
        for mode in range(modes):
            strength = phonon[mode]
            below = near + strength * strength
            above = far + strength * strength
            common = (2.0 * strength) / (below * above)
            columns = slice(mode * segment_rows, (mode + 1) * segment_rows)
            for part, value in enumerate((common * (below + above), common * cross)):
                high, low = split(value)
                tables[segment][part, :padded_rows, columns] = high
                if tables[segment].shape[1] > padded_rows:
                    tables[segment][part, padded_rows:, columns] = low


def other_tables_kernel(dims, meta, phonon, *tables):
    fill_tables(dims, meta, 2, phonon, tables)


def tables_kernel(
    dims, sides, meta, phonon, pair_cols, pair_count, block_order, coupling, plan, weights, *tables
):
    freq_count, segments, segment_rows, padded_rows, modes = dims
    blocks, slots = coupling.shape[:2]
    size = coupling.shape[3]
    for at in range(1 + segments):
        plan[ROWS, at] = meta[at]
    for block in range(blocks):
        for slot in range(slots):
            wanted = pair_cols[block, slot]
            position = jnp.int32(0)
            for at in range(block_order.shape[0]):
                position = jnp.where(block_order[at] == wanted, at, position)
            pair = block * slots + slot
            holder = position // blocks
            plan[HOLDER, pair] = (holder // sides) ^ meta[1 + segments]
            plan[SIDE, pair] = (holder % sides) ^ meta[2 + segments]
            plan[PLACE, pair] = position % blocks
            plan[LIVE, pair] = (pair_count[block] > slot).astype(jnp.int32)
    fill_tables(dims, meta, 0, phonon, tables)
    for block in range(blocks):
        for slot in range(slots):
            for mode in range(modes):
                weights[
                    block, slot * size : (slot + 1) * size, mode * size : (mode + 1) * size
                ] = coupling[block, slot, mode].T


def step_kernel(dims, segment, span, sides, coded, final, keep, parted, plan, *refs):
    freq_count, segments, segment_rows, padded_rows, modes = dims
    refs = list(refs)
    first, last = segment == 0, segment == segments - 1
    take = lambda count: [refs.pop() for _ in range(count)][::-1]
    copied = last and final
    if copied:
        *held, sems = take(3)
    terms = [] if keep else take(2 if first else 1)
    ratios = refs.pop()
    terms = terms or take(2)
    outs = take(2 if copied else 1)
    inputs = refs
    before = [inputs.pop() for _ in range(0 if first else parted)][::-1]
    weights, table = inputs[-2:]
    pieces = []
    for piece in inputs[:-2]:
        if len(piece.shape) == 3:
            pieces += [piece.at[at] for at in range(piece.shape[0])]
        else:
            pieces.append(piece)
    holders = len(pieces) // sides
    blocks = span[1] - span[0]
    size = LANES
    slots = weights.shape[1] // size
    shape = (segment_rows, size)
    col = lax.broadcasted_iota(jnp.int32, shape, 0) + plan[ROWS, 1 + segment]
    col_omega = omega_of(col, freq_count)
    square = col_omega * col_omega

    def fetch(pair):
        column = pl.multiple_of(plan[PLACE, pair] * size, size)
        wanted = plan[SIDE, pair] * holders + plan[HOLDER, pair]
        value = pieces[0][:, pl.ds(column, size)]
        for at in range(1, len(pieces)):
            value = lax.select(wanted == at, pieces[at][:, pl.ds(column, size)], value)
        return decoded(value) if coded else value

    def find_ratios(block):
        for slot in range(slots):
            pair = (span[0] + block) * slots + slot
            gap = fetch(pair)
            live = plan[LIVE, pair].astype(jnp.float32)
            inverse = lax.rsqrt(square + gap * gap) * live
            lanes = slice(slot * size, (slot + 1) * size)
            ratios[block, :segment_rows, lanes] = (gap * inverse).astype(jnp.bfloat16)
            ratios[block, segment_rows:, lanes] = (col_omega * inverse).astype(jnp.bfloat16)

    def find_terms(block):
        lanes = slice(block * size, (block + 1) * size)
        for start in range(0, modes, 2):
            stop = min(start + 2, modes)
            found = jnp.dot(
                ratios[block],
                weights[span[0] + block, :, start * size : stop * size],
                preferred_element_type=jnp.float32,
            )
            pieces_of = split(found) if len(terms) > 1 else [found.astype(jnp.bfloat16)]
            for mode in range(start, stop):
                rows = slice(mode * segment_rows, (mode + 1) * segment_rows)
                taken = slice((mode - start) * size, (mode - start + 1) * size)
                for part in range(2):
                    source = slice(part * segment_rows, (part + 1) * segment_rows)
                    for held_terms, value in zip(terms, pieces_of):
                        held_terms[part, rows, lanes] = value[source, taken]

    def earlier(part, lanes):
        width = before[0].shape[-1]
        start = lanes.start % width
        return before[lanes.start // width][part, :, start : start + lanes.stop - lanes.start]

    def find_sums(lanes):
        def total_of(part):
            views = [held_terms.at[part, :, lanes] for held_terms in terms]
            total = table_sums(padded_rows, table.at[part], *views)
            return total if first else total + earlier(part, lanes)

        if not last:
            for part in range(2):
                outs[0][part, :, lanes] = total_of(part)
            return
        own_rows = outs[0].shape[0]
        width = lanes.stop - lanes.start
        row = lax.broadcasted_iota(jnp.int32, (own_rows, width), 0) + plan[ROWS, 0]
        temperature = CUTOFF / freq_count
        renorm = 1.0 + temperature * total_of(1)[:own_rows] / omega_of(row, freq_count)
        if final:
            held[1][:, lanes] = renorm
            copy_out(1, lanes).start()
        gap = temperature * total_of(0)[:own_rows] / renorm
        if final:
            held[0][:, lanes] = gap
            copy_out(0, lanes).start()
        else:
            outs[0][:, lanes] = encoded(gap) if coded else gap

    def copy_out(at, lanes):
        width = lanes.stop - lanes.start
        return pltpu.make_async_copy(
            held[at].at[:, pl.ds(lanes.start, width)],
            outs[at].at[:, pl.ds(lanes.start, width)],
            sems.at[at, lanes.start // width],
        )

    halves = [slice(start * size, (start + 2) * size) for start in range(0, blocks, 2)]
    find_ratios(0)
    for block in range(blocks):
        if block + 1 < blocks:
            find_ratios(block + 1)
        find_terms(block)
        if block % 2 == 0 and block > 1:
            find_sums(halves[block // 2 - 1])
    find_sums(halves[-1])
    if copied:
        for lanes in halves:
            for at in range(2):
                copy_out(at, lanes).wait()


def table_sums(padded_rows, table, high, low=None):
    both = jnp.dot(table[...], high[...], preferred_element_type=jnp.float32)
    if table.shape[0] == padded_rows:
        return both
    rest = jnp.dot(table[:padded_rows], low[...], preferred_element_type=jnp.float32)
    return both[:padded_rows] + (both[padded_rows:] + rest)


def other_rows_kernel(dims, plan, *refs):
    freq_count, segments, segment_rows, padded_rows, modes = dims
    tables, terms, code = refs[:segments], refs[segments:-1], refs[-1]
    states = code.shape[1]
    temperature = CUTOFF / freq_count
    for start in range(0, states, 2 * LANES):
        lanes = slice(start, min(start + 2 * LANES, states))

        def total_of(part):
            total = None
            for segment in range(segments):
                views = [terms[2 * segment + at].at[part, :, lanes] for at in range(2)]
                piece = table_sums(padded_rows, tables[segment].at[part], *views)
                total = piece if total is None else total + piece
            return total

        row = lax.broadcasted_iota(jnp.int32, (padded_rows, lanes.stop - start), 0)
        omega = omega_of(row + plan[ROWS, 2], freq_count)
        renorm = 1.0 + temperature * total_of(1) / omega
        code[:padded_rows, lanes] = encoded(temperature * total_of(0) / renorm)
    code[padded_rows:] = jnp.zeros((SPARE_ROWS, states), code.dtype)


SWAP = [(0, 1), (1, 0)]


def gather_general(gap, half_groups):
    everyone = lax.all_gather(gap, "state", axis=0, tiled=False)
    rows = lax.all_gather(everyone, "freq", axis=1, tiled=True)
    own_rows = gap.shape[0]
    start = (lax.axis_index("freq") // half_groups) * (half_groups * own_rows)
    return [lax.dynamic_slice_in_dim(rows, start, half_groups * own_rows, 1)]


def on_device(pairwise, freq_groups, gap_in, coupling, pair_cols, pair_count, block_order, phonon):
    own_rows, row_width = gap_in.shape
    blocks, slots, modes, size, _ = coupling.shape
    freq_count = own_rows * freq_groups
    half_rows = freq_count // 2
    half_groups = freq_groups // 2
    padded_rows = -(-own_rows // 16) * 16
    if pairwise:
        segments, sides = 2, 2
        half = lax.axis_index("zhi") * half_rows
        own = half + lax.axis_index("zlo") * own_rows
        other = half + (1 - lax.axis_index("zlo")) * own_rows
        meta = [own, own, other, lax.axis_index("x"), lax.axis_index("core")]
    else:
        segments, sides = 1, 1
        freq_at = lax.axis_index("freq")
        meta = [freq_at * own_rows, (freq_at // half_groups) * half_rows, 0, 0]
    meta = jnp.stack([jnp.asarray(value, jnp.int32) for value in meta])
    segment_rows = half_rows // segments
    dims = (freq_count, segments, segment_rows, padded_rows, modes)
    smem = pl.BlockSpec(memory_space=pltpu.SMEM)
    vmem = pl.BlockSpec(memory_space=pltpu.VMEM)
    link_type = jnp.int16 if pairwise else jnp.float32

    passed = gap_in
    if pairwise:
        passed = pl.pallas_call(
            encode_kernel,
            out_shape=jax.ShapeDtypeStruct(gap_in.shape, link_type),
            in_specs=[vmem],
            out_specs=vmem,
            compiler_params=pltpu.CompilerParams(vmem_limit_bytes=8 << 20),
            cost_estimate=pl.CostEstimate(
                flops=10_000_000_000, bytes_accessed=40_000_000, transcendentals=0
            ),
            name="encode",
        )(gap_in)

    near_table, far_table = [
        jax.ShapeDtypeStruct((2, count * padded_rows, modes * segment_rows), jnp.bfloat16)
        for count in (2, 1)
    ]
    plan, weights, *tables = pl.pallas_call(
        functools.partial(tables_kernel, dims, sides),
        out_shape=[
            jax.ShapeDtypeStruct((5, max(blocks * slots, 1 + segments)), jnp.int32),
            jax.ShapeDtypeStruct((blocks, slots * size, modes * size), jnp.bfloat16),
        ]
        + [near_table, far_table][:segments],
        in_specs=[smem] * 5 + [vmem],
        out_specs=[smem] + [vmem] * (1 + segments),
        compiler_params=pltpu.CompilerParams(vmem_limit_bytes=24 << 20),
        cost_estimate=pl.CostEstimate(
            flops=10_000_000, bytes_accessed=8_000_000, transcendentals=0
        ),
        name="tables",
    )(meta, phonon, pair_cols, pair_count, block_order, coupling)

    full = jax.ShapeDtypeStruct(gap_in.shape, jnp.float32)
    passed_out = jax.ShapeDtypeStruct(gap_in.shape, link_type)
    step_params = dict(
        compiler_params=pltpu.CompilerParams(vmem_limit_bytes=24 << 20),
        cost_estimate=pl.CostEstimate(
            flops=STEP_FLOPS, bytes_accessed=100_000, transcendentals=0
        ),
    )

    def step(plan, segment, final, pieces, before, keep=False, span=(0, blocks)):
        copied = final and segment == segments - 1
        width = (span[1] - span[0]) * size
        terms_shape = (2, modes * segment_rows, width)
        if segment < segments - 1:
            outs = [jax.ShapeDtypeStruct((2, padded_rows, width), jnp.float32)]
        else:
            outs = [full, full] if final else [passed_out]
        out_specs = [pl.BlockSpec(memory_space=pl.ANY) if copied else vmem] * len(outs)
        scratch = [pltpu.VMEM((span[1] - span[0], 2 * segment_rows, slots * size), jnp.bfloat16)]
        if keep:
            outs += [jax.ShapeDtypeStruct(terms_shape, jnp.bfloat16)] * 2
            out_specs += [vmem] * 2
        else:
            scratch += [pltpu.VMEM(terms_shape, jnp.bfloat16)] * (2 if segment == 0 else 1)
        if copied:
            scratch += [pltpu.VMEM(gap_in.shape, jnp.float32)] * 2
            scratch += [pltpu.SemaphoreType.DMA((2, blocks // 2))]
        inputs = [*pieces, weights, tables[segment], *before]
        return pl.pallas_call(
            functools.partial(
                step_kernel, dims, segment, span, sides, pairwise, final, keep, len(before)
            ),
            out_shape=outs,
            in_specs=[smem] + [vmem] * len(inputs),
            out_specs=out_specs,
            scratch_shapes=scratch,
            name="step",
            **step_params,
        )(plan, *inputs)

    if not pairwise:
        for iteration in range(ITERS):
            final = iteration == ITERS - 1
            results = step(plan, 0, final, gather_general(passed, half_groups), [])
            passed = results[0]
        return tuple(results)

    def join(near, across, after):
        return pl.pallas_call(
            join_kernel,
            out_shape=jax.ShapeDtypeStruct((2, *gap_in.shape), near.dtype),
            in_specs=[vmem, vmem, pl.BlockSpec(memory_space=pl.ANY)],
            out_specs=vmem,
            compiler_params=pltpu.CompilerParams(vmem_limit_bytes=4 << 20),
            cost_estimate=pl.CostEstimate(flops=1000, bytes_accessed=1000, transcendentals=0),
            name="join",
        )(near, across, after)

    def with_core(near):
        return near + [lax.ppermute(piece, "core", SWAP) for piece in near]

    other_tables = pl.pallas_call(
        functools.partial(other_tables_kernel, dims),
        out_shape=[far_table, near_table],
        in_specs=[smem, smem],
        out_specs=[vmem] * segments,
        compiler_params=pltpu.CompilerParams(vmem_limit_bytes=12 << 20),
        cost_estimate=pl.CostEstimate(
            flops=10_000_000, bytes_accessed=3_000_000, transcendentals=0
        ),
        name="other_tables",
    )(meta, phonon)
    along_x = lax.ppermute(passed, "x", SWAP)
    along_z = lax.ppermute(passed, "zlo", SWAP)
    along_x, plan = lax.optimization_barrier((along_x, plan))
    relayed = lax.ppermute(along_z, "x", SWAP)
    partial, *near_terms = step(plan, 0, False, with_core([passed, along_x]), [], keep=True)
    far = join(along_z, relayed, partial)
    pieces = [far, lax.ppermute(far, "core", SWAP)]
    plan, *other_tables = lax.optimization_barrier((plan, *other_tables))
    own, *far_terms = step(plan, 1, False, pieces, [partial], keep=True)
    inputs = [*other_tables, *near_terms, *far_terms]
    other = pl.pallas_call(
        functools.partial(other_rows_kernel, dims),
        out_shape=jax.ShapeDtypeStruct((own_rows + SPARE_ROWS, row_width), link_type),
        in_specs=[smem] + [vmem] * len(inputs),
        out_specs=vmem,
        name="other_rows",
        **step_params,
    )(plan, *inputs)
    along_x = lax.ppermute(own, "x", SWAP)
    near = with_core([own, along_x])
    middle = blocks // 2
    partial = step(plan, 0, True, near, [], span=(0, middle))
    far = join(other, lax.ppermute(other, "x", SWAP), *partial)
    partial += step(plan, 0, True, near, [], span=(middle, blocks))
    return tuple(step(plan, 1, True, [far, lax.ppermute(far, "core", SWAP)], partial))


def solution(mesh):
    shape = tuple(mesh.shape[axis] for axis in ("parts", "freq", "state"))
    pairwise = shape[1:] == (4, 4)
    parts, freq, state = "parts", "freq", "state"
    if pairwise:
        names = ("parts", "zhi", "zlo", "x", "core")
        mesh = jax.sharding.Mesh(mesh.devices.reshape(shape[0], 2, 2, 2, 2), names)
        freq, state = ("zhi", "zlo"), ("x", "core")
    rows = ("parts", *freq) if pairwise else ("parts", freq)
    groups = ("parts", *state) if pairwise else ("parts", state)
    return jax.shard_map(
        functools.partial(on_device, pairwise, shape[1]),
        mesh=mesh,
        in_specs=(
            P(rows, state),
            P(groups, None, None, None, None),
            P(groups, None),
            P(groups),
            P(parts),
            P(parts),
        ),
        out_specs=(P(rows, state), P(rows, state)),
        check_vma=False,
    )
```

```python
import functools

import jax
import jax.numpy as jnp
from jax import lax
from jax.experimental import pallas as pl
from jax.experimental.pallas import tpu as pltpu
from jax.sharding import PartitionSpec as P

ITERS = 2
CUTOFF = 4.0
LANES = 128
GAP_LIMIT = 10.0
CODE_LIMIT = 32767.0
CODE_POWER = 5
STEP_FLOPS = 1_000_000
SPARE_ROWS = 8
HOLDER, PLACE, LIVE, SIDE, ROWS = 0, 1, 2, 3, 4


def omega_of(index, freq_count):
    return (2.0 * index.astype(jnp.float32) + 1.0 - freq_count) * (CUTOFF / freq_count)


def encoded(gap):
    share = jnp.minimum(jnp.abs(gap) * (1.0 / GAP_LIMIT), 1.0)
    root = jnp.exp2(jnp.log2(jnp.maximum(share, 1e-37)) * (1.0 / CODE_POWER))
    code = jnp.floor(root * CODE_LIMIT + 0.5)
    return jnp.where(gap < 0, -code, code).astype(jnp.int32).astype(jnp.int16)


def decoded(code):
    root = code.astype(jnp.float32) * (1.0 / CODE_LIMIT)
    square = root * root
    return (root * GAP_LIMIT) * (square * square)


def encode_kernel(gap, code, longer):
    code[...] = encoded(gap[...])
    longer[: code.shape[0]] = code[...]


def join_kernel(first, second, after, joined):
    rows = joined.shape[1]
    joined[0] = first[:rows]
    joined[1] = second[:rows]


def split(value):
    high = value.astype(jnp.bfloat16)
    return high, (value - high.astype(jnp.float32)).astype(jnp.bfloat16)


def fill_tables(dims, meta, row_from, phonon, tables):
    freq_count, segments, segment_rows, padded_rows, modes = dims
    shape = (padded_rows, segment_rows)
    row_omega = omega_of(lax.broadcasted_iota(jnp.int32, shape, 0) + meta[row_from], freq_count)
    for segment in range(len(tables)):
        col = lax.broadcasted_iota(jnp.int32, shape, 1) + meta[1 + segment]
        col_omega = omega_of(col, freq_count)
        near = (row_omega - col_omega) ** 2
        far = (row_omega + col_omega) ** 2
        cross = 4.0 * (row_omega * col_omega)
        for mode in range(modes):
            strength = phonon[mode]
            below = near + strength * strength
            above = far + strength * strength
            common = (2.0 * strength) / (below * above)
            columns = slice(mode * segment_rows, (mode + 1) * segment_rows)
            for part, value in enumerate((common * (below + above), common * cross)):
                high, low = split(value)
                tables[segment][part, :padded_rows, columns] = high
                if tables[segment].shape[1] > padded_rows:
                    tables[segment][part, padded_rows:, columns] = low


def other_tables_kernel(dims, meta, phonon, *tables):
    fill_tables(dims, meta, 2, phonon, tables)


def tables_kernel(
    dims, sides, meta, phonon, pair_cols, pair_count, block_order, coupling, plan, weights, *tables
):
    freq_count, segments, segment_rows, padded_rows, modes = dims
    blocks, slots = coupling.shape[:2]
    size = coupling.shape[3]
    for at in range(1 + segments):
        plan[ROWS, at] = meta[at]
    for block in range(blocks):
        for slot in range(slots):
            wanted = pair_cols[block, slot]
            position = jnp.int32(0)
            for at in range(block_order.shape[0]):
                position = jnp.where(block_order[at] == wanted, at, position)
            pair = block * slots + slot
            holder = position // blocks
            plan[HOLDER, pair] = (holder // sides) ^ meta[1 + segments]
            plan[SIDE, pair] = (holder % sides) ^ meta[2 + segments]
            plan[PLACE, pair] = position % blocks
            plan[LIVE, pair] = (pair_count[block] > slot).astype(jnp.int32)
    fill_tables(dims, meta, 0, phonon, tables)
    for block in range(blocks):
        for slot in range(slots):
            for mode in range(modes):
                weights[
                    block, slot * size : (slot + 1) * size, mode * size : (mode + 1) * size
                ] = coupling[block, slot, mode].T


def step_kernel(dims, segment, span, sides, coded, final, keep, parted, plan, *refs):
    freq_count, segments, segment_rows, padded_rows, modes = dims
    refs = list(refs)
    first, last = segment == 0, segment == segments - 1
    take = lambda count: [refs.pop() for _ in range(count)][::-1]
    copied = last and final
    if copied:
        *held, sems = take(3)
    terms = [] if keep else take(2 if first else 1)
    ratios = refs.pop()
    terms = terms or take(2)
    outs = take(2 if copied else 1)
    inputs = refs
    before = [inputs.pop() for _ in range(0 if first else parted)][::-1]
    weights, table = inputs[-2:]
    pieces = []
    for piece in inputs[:-2]:
        if len(piece.shape) == 3:
            pieces += [piece.at[at] for at in range(piece.shape[0])]
        else:
            pieces.append(piece)
    holders = len(pieces) // sides
    blocks = span[1] - span[0]
    size = LANES
    slots = weights.shape[1] // size
    shape = (segment_rows, size)
    col = lax.broadcasted_iota(jnp.int32, shape, 0) + plan[ROWS, 1 + segment]
    col_omega = omega_of(col, freq_count)
    square = col_omega * col_omega

    def fetch(pair):
        column = pl.multiple_of(plan[PLACE, pair] * size, size)
        wanted = plan[SIDE, pair] * holders + plan[HOLDER, pair]
        value = pieces[0][:, pl.ds(column, size)]
        for at in range(1, len(pieces)):
            value = lax.select(wanted == at, pieces[at][:, pl.ds(column, size)], value)
        return decoded(value) if coded else value

    def find_ratios(block):
        for slot in range(slots):
            pair = (span[0] + block) * slots + slot
            gap = fetch(pair)
            live = plan[LIVE, pair].astype(jnp.float32)
            inverse = lax.rsqrt(square + gap * gap) * live
            lanes = slice(slot * size, (slot + 1) * size)
            ratios[block, :segment_rows, lanes] = (gap * inverse).astype(jnp.bfloat16)
            ratios[block, segment_rows:, lanes] = (col_omega * inverse).astype(jnp.bfloat16)

    def find_terms(block):
        lanes = slice(block * size, (block + 1) * size)
        for start in range(0, modes, 2):
            stop = min(start + 2, modes)
            found = jnp.dot(
                ratios[block],
                weights[span[0] + block, :, start * size : stop * size],
                preferred_element_type=jnp.float32,
            )
            pieces_of = split(found) if len(terms) > 1 else [found.astype(jnp.bfloat16)]
            for mode in range(start, stop):
                rows = slice(mode * segment_rows, (mode + 1) * segment_rows)
                taken = slice((mode - start) * size, (mode - start + 1) * size)
                for part in range(2):
                    source = slice(part * segment_rows, (part + 1) * segment_rows)
                    for held_terms, value in zip(terms, pieces_of):
                        held_terms[part, rows, lanes] = value[source, taken]

    def earlier(part, lanes):
        width = before[0].shape[-1]
        start = lanes.start % width
        return before[lanes.start // width][part, :, start : start + lanes.stop - lanes.start]

    def find_sums(lanes):
        def total_of(part):
            views = [held_terms.at[part, :, lanes] for held_terms in terms]
            total = table_sums(padded_rows, table.at[part], *views)
            return total if first else total + earlier(part, lanes)

        if not last:
            for part in range(2):
                outs[0][part, :, lanes] = total_of(part)
            return
        own_rows = outs[0].shape[0]
        width = lanes.stop - lanes.start
        row = lax.broadcasted_iota(jnp.int32, (own_rows, width), 0) + plan[ROWS, 0]
        temperature = CUTOFF / freq_count
        renorm = 1.0 + temperature * total_of(1)[:own_rows] / omega_of(row, freq_count)
        if final:
            held[1][:, lanes] = renorm
            copy_out(1, lanes).start()
        gap = temperature * total_of(0)[:own_rows] / renorm
        if final:
            held[0][:, lanes] = gap
            copy_out(0, lanes).start()
        else:
            outs[0][:, lanes] = encoded(gap) if coded else gap

    def copy_out(at, lanes):
        width = lanes.stop - lanes.start
        return pltpu.make_async_copy(
            held[at].at[:, pl.ds(lanes.start, width)],
            outs[at].at[:, pl.ds(lanes.start, width)],
            sems.at[at, lanes.start // width],
        )

    halves = [slice(start * size, (start + 2) * size) for start in range(0, blocks, 2)]
    find_ratios(0)
    for block in range(blocks):
        if block + 1 < blocks:
            find_ratios(block + 1)
        find_terms(block)
        if block % 2 == 0 and block > 1:
            find_sums(halves[block // 2 - 1])
    find_sums(halves[-1])
    if copied:
        for lanes in halves:
            for at in range(2):
                copy_out(at, lanes).wait()


def table_sums(padded_rows, table, high, low=None):
    both = jnp.dot(table[...], high[...], preferred_element_type=jnp.float32)
    if table.shape[0] == padded_rows:
        return both
    rest = jnp.dot(table[:padded_rows], low[...], preferred_element_type=jnp.float32)
    return both[:padded_rows] + (both[padded_rows:] + rest)


def other_rows_kernel(dims, plan, *refs):
    freq_count, segments, segment_rows, padded_rows, modes = dims
    tables, terms, code = refs[:segments], refs[segments:-1], refs[-1]
    states = code.shape[1]
    temperature = CUTOFF / freq_count
    for start in range(0, states, 2 * LANES):
        lanes = slice(start, min(start + 2 * LANES, states))

        def total_of(part):
            total = None
            for segment in range(segments):
                views = [terms[2 * segment + at].at[part, :, lanes] for at in range(2)]
                piece = table_sums(padded_rows, tables[segment].at[part], *views)
                total = piece if total is None else total + piece
            return total

        row = lax.broadcasted_iota(jnp.int32, (padded_rows, lanes.stop - start), 0)
        omega = omega_of(row + plan[ROWS, 2], freq_count)
        renorm = 1.0 + temperature * total_of(1) / omega
        code[:padded_rows, lanes] = encoded(temperature * total_of(0) / renorm)


SWAP = [(0, 1), (1, 0)]


def gather_general(gap, half_groups):
    everyone = lax.all_gather(gap, "state", axis=0, tiled=False)
    rows = lax.all_gather(everyone, "freq", axis=1, tiled=True)
    own_rows = gap.shape[0]
    start = (lax.axis_index("freq") // half_groups) * (half_groups * own_rows)
    return [lax.dynamic_slice_in_dim(rows, start, half_groups * own_rows, 1)]


def on_device(pairwise, freq_groups, gap_in, coupling, pair_cols, pair_count, block_order, phonon):
    own_rows, row_width = gap_in.shape
    blocks, slots, modes, size, _ = coupling.shape
    freq_count = own_rows * freq_groups
    half_rows = freq_count // 2
    half_groups = freq_groups // 2
    padded_rows = -(-own_rows // 16) * 16
    if pairwise:
        segments, sides = 2, 2
        half = lax.axis_index("zhi") * half_rows
        own = half + lax.axis_index("zlo") * own_rows
        other = half + (1 - lax.axis_index("zlo")) * own_rows
        meta = [own, own, other, lax.axis_index("x"), lax.axis_index("core")]
    else:
        segments, sides = 1, 1
        freq_at = lax.axis_index("freq")
        meta = [freq_at * own_rows, (freq_at // half_groups) * half_rows, 0, 0]
    meta = jnp.stack([jnp.asarray(value, jnp.int32) for value in meta])
    segment_rows = half_rows // segments
    dims = (freq_count, segments, segment_rows, padded_rows, modes)
    smem = pl.BlockSpec(memory_space=pltpu.SMEM)
    vmem = pl.BlockSpec(memory_space=pltpu.VMEM)
    link_type = jnp.int16 if pairwise else jnp.float32

    passed = gap_in
    if pairwise:
        passed, longer = pl.pallas_call(
            encode_kernel,
            out_shape=[
                jax.ShapeDtypeStruct(gap_in.shape, link_type),
                jax.ShapeDtypeStruct((own_rows + SPARE_ROWS, row_width), link_type),
            ],
            in_specs=[vmem],
            out_specs=[vmem, vmem],
            compiler_params=pltpu.CompilerParams(vmem_limit_bytes=8 << 20),
            cost_estimate=pl.CostEstimate(
                flops=10_000_000_000, bytes_accessed=40_000_000, transcendentals=0
            ),
            name="encode",
        )(gap_in)

    near_table, far_table = [
        jax.ShapeDtypeStruct((2, count * padded_rows, modes * segment_rows), jnp.bfloat16)
        for count in (2, 1)
    ]
    plan, weights, *tables = pl.pallas_call(
        functools.partial(tables_kernel, dims, sides),
        out_shape=[
            jax.ShapeDtypeStruct((5, max(blocks * slots, 1 + segments)), jnp.int32),
            jax.ShapeDtypeStruct((blocks, slots * size, modes * size), jnp.bfloat16),
        ]
        + [near_table, far_table][:segments],
        in_specs=[smem] * 5 + [vmem],
        out_specs=[smem] + [vmem] * (1 + segments),
        compiler_params=pltpu.CompilerParams(vmem_limit_bytes=24 << 20),
        cost_estimate=pl.CostEstimate(
            flops=10_000_000, bytes_accessed=8_000_000, transcendentals=0
        ),
        name="tables",
    )(meta, phonon, pair_cols, pair_count, block_order, coupling)

    full = jax.ShapeDtypeStruct(gap_in.shape, jnp.float32)
    passed_out = jax.ShapeDtypeStruct(gap_in.shape, link_type)
    step_params = dict(
        compiler_params=pltpu.CompilerParams(vmem_limit_bytes=24 << 20),
        cost_estimate=pl.CostEstimate(
            flops=STEP_FLOPS, bytes_accessed=100_000, transcendentals=0
        ),
    )

    def step(plan, segment, final, pieces, before, keep=False, span=(0, blocks)):
        copied = final and segment == segments - 1
        width = (span[1] - span[0]) * size
        terms_shape = (2, modes * segment_rows, width)
        if segment < segments - 1:
            outs = [jax.ShapeDtypeStruct((2, padded_rows, width), jnp.float32)]
        else:
            outs = [full, full] if final else [passed_out]
        out_specs = [pl.BlockSpec(memory_space=pl.ANY) if copied else vmem] * len(outs)
        scratch = [pltpu.VMEM((span[1] - span[0], 2 * segment_rows, slots * size), jnp.bfloat16)]
        if keep:
            outs += [jax.ShapeDtypeStruct(terms_shape, jnp.bfloat16)] * 2
            out_specs += [vmem] * 2
        else:
            scratch += [pltpu.VMEM(terms_shape, jnp.bfloat16)] * (2 if segment == 0 else 1)
        if copied:
            scratch += [pltpu.VMEM(gap_in.shape, jnp.float32)] * 2
            scratch += [pltpu.SemaphoreType.DMA((2, blocks // 2))]
        inputs = [*pieces, weights, tables[segment], *before]
        return pl.pallas_call(
            functools.partial(
                step_kernel, dims, segment, span, sides, pairwise, final, keep, len(before)
            ),
            out_shape=outs,
            in_specs=[smem] + [vmem] * len(inputs),
            out_specs=out_specs,
            scratch_shapes=scratch,
            name="step",
            **step_params,
        )(plan, *inputs)

    if not pairwise:
        for iteration in range(ITERS):
            final = iteration == ITERS - 1
            results = step(plan, 0, final, gather_general(passed, half_groups), [])
            passed = results[0]
        return tuple(results)

    def join(near, across, after):
        return pl.pallas_call(
            join_kernel,
            out_shape=jax.ShapeDtypeStruct((2, *gap_in.shape), near.dtype),
            in_specs=[vmem, vmem, pl.BlockSpec(memory_space=pl.ANY)],
            out_specs=vmem,
            compiler_params=pltpu.CompilerParams(vmem_limit_bytes=4 << 20),
            cost_estimate=pl.CostEstimate(flops=1000, bytes_accessed=1000, transcendentals=0),
            name="join",
        )(near, across, after)

    def with_core(near):
        return near + [lax.ppermute(piece, "core", SWAP) for piece in near]

    other_tables = pl.pallas_call(
        functools.partial(other_tables_kernel, dims),
        out_shape=[far_table, near_table],
        in_specs=[smem, smem],
        out_specs=[vmem] * segments,
        compiler_params=pltpu.CompilerParams(vmem_limit_bytes=12 << 20),
        cost_estimate=pl.CostEstimate(
            flops=10_000_000, bytes_accessed=3_000_000, transcendentals=0
        ),
        name="other_tables",
    )(meta, phonon)
    along_x = lax.ppermute(passed, "x", SWAP)
    along_z = lax.ppermute(longer, "zlo", SWAP)
    along_z, plan = lax.optimization_barrier((along_z, plan))
    relayed = lax.ppermute(along_z, "x", SWAP)
    partial, *near_terms = step(plan, 0, False, with_core([passed, along_x]), [], keep=True)
    far = join(along_z, relayed, partial)
    pieces = [far, lax.ppermute(far, "core", SWAP)]
    plan, *other_tables = lax.optimization_barrier((plan, *other_tables))
    own, *far_terms = step(plan, 1, False, pieces, [partial], keep=True)
    inputs = [*other_tables, *near_terms, *far_terms]
    other = pl.pallas_call(
        functools.partial(other_rows_kernel, dims),
        out_shape=jax.ShapeDtypeStruct((own_rows + SPARE_ROWS, row_width), link_type),
        in_specs=[smem] + [vmem] * len(inputs),
        out_specs=vmem,
        name="other_rows",
        **step_params,
    )(plan, *inputs)
    along_x = lax.ppermute(own, "x", SWAP)
    near = with_core([own, along_x])
    middle = blocks // 2
    partial = step(plan, 0, True, near, [], span=(0, middle))
    far = join(other, lax.ppermute(other, "x", SWAP), *partial)
    partial += step(plan, 0, True, near, [], span=(middle, blocks))
    return tuple(step(plan, 1, True, [far, lax.ppermute(far, "core", SWAP)], partial))


def solution(mesh):
    shape = tuple(mesh.shape[axis] for axis in ("parts", "freq", "state"))
    pairwise = shape[1:] == (4, 4)
    parts, freq, state = "parts", "freq", "state"
    if pairwise:
        names = ("parts", "zhi", "zlo", "x", "core")
        mesh = jax.sharding.Mesh(mesh.devices.reshape(shape[0], 2, 2, 2, 2), names)
        freq, state = ("zhi", "zlo"), ("x", "core")
    rows = ("parts", *freq) if pairwise else ("parts", freq)
    groups = ("parts", *state) if pairwise else ("parts", state)
    return jax.shard_map(
        functools.partial(on_device, pairwise, shape[1]),
        mesh=mesh,
        in_specs=(
            P(rows, state),
            P(groups, None, None, None, None),
            P(groups, None),
            P(groups),
            P(parts),
            P(parts),
        ),
        out_specs=(P(rows, state), P(rows, state)),
        check_vma=False,
    )
```

```python
import functools

import jax
import jax.numpy as jnp
from jax import lax
from jax.experimental import pallas as pl
from jax.experimental.pallas import tpu as pltpu
from jax.sharding import PartitionSpec as P

ITERS = 2
CUTOFF = 4.0
LANES = 128
GAP_LIMIT = 10.0
CODE_LIMIT = 32767.0
CODE_POWER = 5
STEP_FLOPS = 1_000_000
SPARE_ROWS = 8
HOLDER, PLACE, LIVE, SIDE, ROWS = 0, 1, 2, 3, 4


def omega_of(index, freq_count):
    return (2.0 * index.astype(jnp.float32) + 1.0 - freq_count) * (CUTOFF / freq_count)


def encoded(gap):
    share = jnp.minimum(jnp.abs(gap) * (1.0 / GAP_LIMIT), 1.0)
    root = jnp.exp2(jnp.log2(jnp.maximum(share, 1e-37)) * (1.0 / CODE_POWER))
    code = jnp.floor(root * CODE_LIMIT + 0.5)
    return jnp.where(gap < 0, -code, code).astype(jnp.int32).astype(jnp.int16)


def decoded(code):
    root = code.astype(jnp.float32) * (1.0 / CODE_LIMIT)
    square = root * root
    return (root * GAP_LIMIT) * (square * square)


def encode_kernel(gap, code, longer):
    code[...] = encoded(gap[...])
    longer[: code.shape[0]] = code[...]


def join_kernel(first, second, after, joined):
    rows = joined.shape[1]
    joined[0] = first[:rows]
    joined[1] = second[:rows]


def split(value):
    high = value.astype(jnp.bfloat16)
    return high, (value - high.astype(jnp.float32)).astype(jnp.bfloat16)


def fill_tables(dims, meta, row_from, phonon, tables):
    freq_count, segments, segment_rows, padded_rows, modes = dims
    shape = (padded_rows, segment_rows)
    row_omega = omega_of(lax.broadcasted_iota(jnp.int32, shape, 0) + meta[row_from], freq_count)
    for segment in range(len(tables)):
        col = lax.broadcasted_iota(jnp.int32, shape, 1) + meta[1 + segment]
        col_omega = omega_of(col, freq_count)
        near = (row_omega - col_omega) ** 2
        far = (row_omega + col_omega) ** 2
        cross = 4.0 * (row_omega * col_omega)
        for mode in range(modes):
            strength = phonon[mode]
            below = near + strength * strength
            above = far + strength * strength
            common = (2.0 * strength) / (below * above)
            columns = slice(mode * segment_rows, (mode + 1) * segment_rows)
            for part, value in enumerate((common * (below + above), common * cross)):
                high, low = split(value)
                tables[segment][part, :padded_rows, columns] = high
                if tables[segment].shape[1] > padded_rows:
                    tables[segment][part, padded_rows:, columns] = low


def other_tables_kernel(dims, meta, phonon, *tables):
    fill_tables(dims, meta, 2, phonon, tables)


def tables_kernel(
    dims, sides, meta, phonon, pair_cols, pair_count, block_order, coupling, plan, weights, *tables
):
    freq_count, segments, segment_rows, padded_rows, modes = dims
    blocks, slots = coupling.shape[:2]
    size = coupling.shape[3]
    for at in range(1 + segments):
        plan[ROWS, at] = meta[at]
    for block in range(blocks):
        for slot in range(slots):
            wanted = pair_cols[block, slot]
            position = jnp.int32(0)
            for at in range(block_order.shape[0]):
                position = jnp.where(block_order[at] == wanted, at, position)
            pair = block * slots + slot
            holder = position // blocks
            plan[HOLDER, pair] = (holder // sides) ^ meta[1 + segments]
            plan[SIDE, pair] = (holder % sides) ^ meta[2 + segments]
            plan[PLACE, pair] = position % blocks
            plan[LIVE, pair] = (pair_count[block] > slot).astype(jnp.int32)
    fill_tables(dims, meta, 0, phonon, tables)
    for block in range(blocks):
        for slot in range(slots):
            for mode in range(modes):
                weights[
                    block, slot * size : (slot + 1) * size, mode * size : (mode + 1) * size
                ] = coupling[block, slot, mode].T


def step_kernel(dims, segment, span, sides, coded, final, keep, parted, plan, *refs):
    freq_count, segments, segment_rows, padded_rows, modes = dims
    refs = list(refs)
    first, last = segment == 0, segment == segments - 1
    take = lambda count: [refs.pop() for _ in range(count)][::-1]
    copied = last and final
    if copied:
        *held, sems = take(3)
    terms = [] if keep else take(2 if first else 1)
    ratios = refs.pop()
    terms = terms or take(2)
    outs = take(2 if copied else 1)
    inputs = refs
    before = [inputs.pop() for _ in range(0 if first else parted)][::-1]
    weights, table = inputs[-2:]
    pieces = []
    for piece in inputs[:-2]:
        if len(piece.shape) == 3:
            pieces += [piece.at[at] for at in range(piece.shape[0])]
        else:
            pieces.append(piece)
    holders = len(pieces) // sides
    blocks = span[1] - span[0]
    size = LANES
    slots = weights.shape[1] // size
    shape = (segment_rows, size)
    col = lax.broadcasted_iota(jnp.int32, shape, 0) + plan[ROWS, 1 + segment]
    col_omega = omega_of(col, freq_count)
    square = col_omega * col_omega

    def fetch(pair):
        column = pl.multiple_of(plan[PLACE, pair] * size, size)
        wanted = plan[SIDE, pair] * holders + plan[HOLDER, pair]
        value = pieces[0][:, pl.ds(column, size)]
        for at in range(1, len(pieces)):
            value = lax.select(wanted == at, pieces[at][:, pl.ds(column, size)], value)
        return decoded(value) if coded else value

    def find_ratios(block):
        for slot in range(slots):
            pair = (span[0] + block) * slots + slot
            gap = fetch(pair)
            live = plan[LIVE, pair].astype(jnp.float32)
            inverse = lax.rsqrt(square + gap * gap) * live
            lanes = slice(slot * size, (slot + 1) * size)
            ratios[block, :segment_rows, lanes] = (gap * inverse).astype(jnp.bfloat16)
            ratios[block, segment_rows:, lanes] = (col_omega * inverse).astype(jnp.bfloat16)

    def find_terms(block):
        lanes = slice(block * size, (block + 1) * size)
        for start in range(0, modes, 2):
            stop = min(start + 2, modes)
            found = jnp.dot(
                ratios[block],
                weights[span[0] + block, :, start * size : stop * size],
                preferred_element_type=jnp.float32,
            )
            pieces_of = split(found) if len(terms) > 1 else [found.astype(jnp.bfloat16)]
            for mode in range(start, stop):
                rows = slice(mode * segment_rows, (mode + 1) * segment_rows)
                taken = slice((mode - start) * size, (mode - start + 1) * size)
                for part in range(2):
                    source = slice(part * segment_rows, (part + 1) * segment_rows)
                    for held_terms, value in zip(terms, pieces_of):
                        held_terms[part, rows, lanes] = value[source, taken]

    def earlier(part, lanes):
        width = before[0].shape[-1]
        start = lanes.start % width
        return before[lanes.start // width][part, :, start : start + lanes.stop - lanes.start]

    def find_sums(lanes):
        def total_of(part):
            views = [held_terms.at[part, :, lanes] for held_terms in terms]
            total = table_sums(padded_rows, table.at[part], *views)
            return total if first else total + earlier(part, lanes)

        if not last:
            for part in range(2):
                outs[0][part, :, lanes] = total_of(part)
            return
        own_rows = outs[0].shape[0]
        width = lanes.stop - lanes.start
        row = lax.broadcasted_iota(jnp.int32, (own_rows, width), 0) + plan[ROWS, 0]
        temperature = CUTOFF / freq_count
        renorm = 1.0 + temperature * total_of(1)[:own_rows] / omega_of(row, freq_count)
        if final:
            held[1][:, lanes] = renorm
            copy_out(1, lanes).start()
        gap = temperature * total_of(0)[:own_rows] / renorm
        if final:
            held[0][:, lanes] = gap
            copy_out(0, lanes).start()
        else:
            outs[0][:, lanes] = encoded(gap) if coded else gap

    def copy_out(at, lanes):
        width = lanes.stop - lanes.start
        return pltpu.make_async_copy(
            held[at].at[:, pl.ds(lanes.start, width)],
            outs[at].at[:, pl.ds(lanes.start, width)],
            sems.at[at, lanes.start // width],
        )

    halves = [slice(start * size, (start + 2) * size) for start in range(0, blocks, 2)]
    find_ratios(0)
    for block in range(blocks):
        if block + 1 < blocks:
            find_ratios(block + 1)
        find_terms(block)
        if block % 2 == 0 and block > 1:
            find_sums(halves[block // 2 - 1])
    find_sums(halves[-1])
    if copied:
        for lanes in halves:
            for at in range(2):
                copy_out(at, lanes).wait()


def table_sums(padded_rows, table, high, low=None):
    both = jnp.dot(table[...], high[...], preferred_element_type=jnp.float32)
    if table.shape[0] == padded_rows:
        return both
    rest = jnp.dot(table[:padded_rows], low[...], preferred_element_type=jnp.float32)
    return both[:padded_rows] + (both[padded_rows:] + rest)


def other_rows_kernel(dims, plan, *refs):
    freq_count, segments, segment_rows, padded_rows, modes = dims
    tables, terms, code = refs[:segments], refs[segments:-1], refs[-1]
    states = code.shape[1]
    temperature = CUTOFF / freq_count
    for start in range(0, states, 2 * LANES):
        lanes = slice(start, min(start + 2 * LANES, states))

        def total_of(part):
            total = None
            for segment in range(segments):
                views = [terms[2 * segment + at].at[part, :, lanes] for at in range(2)]
                piece = table_sums(padded_rows, tables[segment].at[part], *views)
                total = piece if total is None else total + piece
            return total

        row = lax.broadcasted_iota(jnp.int32, (padded_rows, lanes.stop - start), 0)
        omega = omega_of(row + plan[ROWS, 2], freq_count)
        renorm = 1.0 + temperature * total_of(1) / omega
        code[:padded_rows, lanes] = encoded(temperature * total_of(0) / renorm)


SWAP = [(0, 1), (1, 0)]


def gather_general(gap, half_groups):
    everyone = lax.all_gather(gap, "state", axis=0, tiled=False)
    rows = lax.all_gather(everyone, "freq", axis=1, tiled=True)
    own_rows = gap.shape[0]
    start = (lax.axis_index("freq") // half_groups) * (half_groups * own_rows)
    return [lax.dynamic_slice_in_dim(rows, start, half_groups * own_rows, 1)]


def on_device(pairwise, freq_groups, gap_in, coupling, pair_cols, pair_count, block_order, phonon):
    own_rows, row_width = gap_in.shape
    blocks, slots, modes, size, _ = coupling.shape
    freq_count = own_rows * freq_groups
    half_rows = freq_count // 2
    half_groups = freq_groups // 2
    padded_rows = -(-own_rows // 16) * 16
    if pairwise:
        segments, sides = 2, 2
        half = lax.axis_index("zhi") * half_rows
        own = half + lax.axis_index("zlo") * own_rows
        other = half + (1 - lax.axis_index("zlo")) * own_rows
        meta = [own, own, other, lax.axis_index("x"), lax.axis_index("core")]
    else:
        segments, sides = 1, 1
        freq_at = lax.axis_index("freq")
        meta = [freq_at * own_rows, (freq_at // half_groups) * half_rows, 0, 0]
    meta = jnp.stack([jnp.asarray(value, jnp.int32) for value in meta])
    segment_rows = half_rows // segments
    dims = (freq_count, segments, segment_rows, padded_rows, modes)
    smem = pl.BlockSpec(memory_space=pltpu.SMEM)
    vmem = pl.BlockSpec(memory_space=pltpu.VMEM)
    link_type = jnp.int16 if pairwise else jnp.float32

    passed = gap_in
    if pairwise:
        passed, longer = pl.pallas_call(
            encode_kernel,
            out_shape=[
                jax.ShapeDtypeStruct(gap_in.shape, link_type),
                jax.ShapeDtypeStruct((own_rows + SPARE_ROWS, row_width), link_type),
            ],
            in_specs=[vmem],
            out_specs=[vmem, vmem],
            compiler_params=pltpu.CompilerParams(vmem_limit_bytes=8 << 20),
            cost_estimate=pl.CostEstimate(
                flops=10_000_000_000, bytes_accessed=40_000_000, transcendentals=0
            ),
            name="encode",
        )(gap_in)

    near_table, far_table = [
        jax.ShapeDtypeStruct((2, count * padded_rows, modes * segment_rows), jnp.bfloat16)
        for count in (2, 1)
    ]
    plan, weights, *tables = pl.pallas_call(
        functools.partial(tables_kernel, dims, sides),
        out_shape=[
            jax.ShapeDtypeStruct((5, max(blocks * slots, 1 + segments)), jnp.int32),
            jax.ShapeDtypeStruct((blocks, slots * size, modes * size), jnp.bfloat16),
        ]
        + [near_table, far_table][:segments],
        in_specs=[smem] * 5 + [vmem],
        out_specs=[smem] + [vmem] * (1 + segments),
        compiler_params=pltpu.CompilerParams(vmem_limit_bytes=24 << 20),
        cost_estimate=pl.CostEstimate(
            flops=10_000_000, bytes_accessed=8_000_000, transcendentals=0
        ),
        name="tables",
    )(meta, phonon, pair_cols, pair_count, block_order, coupling)

    full = jax.ShapeDtypeStruct(gap_in.shape, jnp.float32)
    passed_out = jax.ShapeDtypeStruct(gap_in.shape, link_type)
    step_params = dict(
        compiler_params=pltpu.CompilerParams(vmem_limit_bytes=24 << 20),
        cost_estimate=pl.CostEstimate(
            flops=STEP_FLOPS, bytes_accessed=100_000, transcendentals=0
        ),
    )

    def step(plan, segment, final, pieces, before, keep=False, span=(0, blocks)):
        copied = final and segment == segments - 1
        width = (span[1] - span[0]) * size
        terms_shape = (2, modes * segment_rows, width)
        if segment < segments - 1:
            outs = [jax.ShapeDtypeStruct((2, padded_rows, width), jnp.float32)]
        else:
            outs = [full, full] if final else [passed_out]
        out_specs = [pl.BlockSpec(memory_space=pl.ANY) if copied else vmem] * len(outs)
        scratch = [pltpu.VMEM((span[1] - span[0], 2 * segment_rows, slots * size), jnp.bfloat16)]
        if keep:
            outs += [jax.ShapeDtypeStruct(terms_shape, jnp.bfloat16)] * 2
            out_specs += [vmem] * 2
        else:
            scratch += [pltpu.VMEM(terms_shape, jnp.bfloat16)] * (2 if segment == 0 else 1)
        if copied:
            scratch += [pltpu.VMEM(gap_in.shape, jnp.float32)] * 2
            scratch += [pltpu.SemaphoreType.DMA((2, blocks // 2))]
        inputs = [*pieces, weights, tables[segment], *before]
        return pl.pallas_call(
            functools.partial(
                step_kernel, dims, segment, span, sides, pairwise, final, keep, len(before)
            ),
            out_shape=outs,
            in_specs=[smem] + [vmem] * len(inputs),
            out_specs=out_specs,
            scratch_shapes=scratch,
            name="step",
            **step_params,
        )(plan, *inputs)

    if not pairwise:
        for iteration in range(ITERS):
            final = iteration == ITERS - 1
            results = step(plan, 0, final, gather_general(passed, half_groups), [])
            passed = results[0]
        return tuple(results)

    def join(near, across, after):
        return pl.pallas_call(
            join_kernel,
            out_shape=jax.ShapeDtypeStruct((2, *gap_in.shape), near.dtype),
            in_specs=[vmem, vmem, pl.BlockSpec(memory_space=pl.ANY)],
            out_specs=vmem,
            compiler_params=pltpu.CompilerParams(vmem_limit_bytes=4 << 20),
            cost_estimate=pl.CostEstimate(flops=1000, bytes_accessed=1000, transcendentals=0),
            name="join",
        )(near, across, after)

    def with_core(near):
        return near + [lax.ppermute(piece, "core", SWAP) for piece in near]

    other_tables = pl.pallas_call(
        functools.partial(other_tables_kernel, dims),
        out_shape=[far_table, near_table],
        in_specs=[smem, smem],
        out_specs=[vmem] * segments,
        compiler_params=pltpu.CompilerParams(vmem_limit_bytes=12 << 20),
        cost_estimate=pl.CostEstimate(
            flops=10_000_000, bytes_accessed=3_000_000, transcendentals=0
        ),
        name="other_tables",
    )(meta, phonon)
    along_x = lax.ppermute(passed, "x", SWAP)
    along_z = lax.ppermute(longer, "zlo", SWAP)
    across = lax.ppermute(passed, "core", SWAP)
    along_z, across, plan = lax.optimization_barrier((along_z, across, plan))
    relayed = lax.ppermute(along_z, "x", SWAP)
    near = [passed, along_x, across, lax.ppermute(along_x, "core", SWAP)]
    partial, *near_terms = step(plan, 0, False, near, [], keep=True)
    far = join(along_z, relayed, partial)
    pieces = [far, lax.ppermute(far, "core", SWAP)]
    plan, *other_tables = lax.optimization_barrier((plan, *other_tables))
    own, *far_terms = step(plan, 1, False, pieces, [partial], keep=True)
    inputs = [*other_tables, *near_terms, *far_terms]
    other = pl.pallas_call(
        functools.partial(other_rows_kernel, dims),
        out_shape=jax.ShapeDtypeStruct((own_rows + SPARE_ROWS, row_width), link_type),
        in_specs=[smem] + [vmem] * len(inputs),
        out_specs=vmem,
        name="other_rows",
        **step_params,
    )(plan, *inputs)
    along_x = lax.ppermute(own, "x", SWAP)
    near = with_core([own, along_x])
    middle = blocks // 2
    partial = step(plan, 0, True, near, [], span=(0, middle))
    far = join(other, lax.ppermute(other, "x", SWAP), *partial)
    partial += step(plan, 0, True, near, [], span=(middle, blocks))
    return tuple(step(plan, 1, True, [far, lax.ppermute(far, "core", SWAP)], partial))


def solution(mesh):
    shape = tuple(mesh.shape[axis] for axis in ("parts", "freq", "state"))
    pairwise = shape[1:] == (4, 4)
    parts, freq, state = "parts", "freq", "state"
    if pairwise:
        names = ("parts", "zhi", "zlo", "x", "core")
        mesh = jax.sharding.Mesh(mesh.devices.reshape(shape[0], 2, 2, 2, 2), names)
        freq, state = ("zhi", "zlo"), ("x", "core")
    rows = ("parts", *freq) if pairwise else ("parts", freq)
    groups = ("parts", *state) if pairwise else ("parts", state)
    return jax.shard_map(
        functools.partial(on_device, pairwise, shape[1]),
        mesh=mesh,
        in_specs=(
            P(rows, state),
            P(groups, None, None, None, None),
            P(groups, None),
            P(groups),
            P(parts),
            P(parts),
        ),
        out_specs=(P(rows, state), P(rows, state)),
        check_vma=False,
    )
```

```python
import functools

import jax
import jax.numpy as jnp
from jax import lax
from jax.experimental import pallas as pl
from jax.experimental.pallas import tpu as pltpu
from jax.sharding import PartitionSpec as P

ITERS = 2
CUTOFF = 4.0
LANES = 128
GAP_LIMIT = 10.0
CODE_LIMIT = 32767.0
CODE_POWER = 5
STEP_FLOPS = 1_000_000
SPARE_ROWS = 16
HOLDER, PLACE, LIVE, SIDE, ROWS = 0, 1, 2, 3, 4


def omega_of(index, freq_count):
    return (2.0 * index.astype(jnp.float32) + 1.0 - freq_count) * (CUTOFF / freq_count)


def encoded(gap):
    share = jnp.minimum(jnp.abs(gap) * (1.0 / GAP_LIMIT), 1.0)
    root = jnp.exp2(jnp.log2(jnp.maximum(share, 1e-37)) * (1.0 / CODE_POWER))
    code = jnp.floor(root * CODE_LIMIT + 0.5)
    return jnp.where(gap < 0, -code, code).astype(jnp.int32).astype(jnp.int16)


def decoded(code):
    root = code.astype(jnp.float32) * (1.0 / CODE_LIMIT)
    square = root * root
    return (root * GAP_LIMIT) * (square * square)


def encode_kernel(gap, code):
    code[...] = encoded(gap[...])


def join_kernel(first, second, after, joined):
    rows = joined.shape[1]
    joined[0] = first[:rows]
    joined[1] = second[:rows]


def split(value):
    high = value.astype(jnp.bfloat16)
    return high, (value - high.astype(jnp.float32)).astype(jnp.bfloat16)


def fill_tables(dims, meta, row_from, phonon, tables):
    freq_count, segments, segment_rows, padded_rows, modes = dims
    shape = (padded_rows, segment_rows)
    row_omega = omega_of(lax.broadcasted_iota(jnp.int32, shape, 0) + meta[row_from], freq_count)
    for segment in range(len(tables)):
        col = lax.broadcasted_iota(jnp.int32, shape, 1) + meta[1 + segment]
        col_omega = omega_of(col, freq_count)
        near = (row_omega - col_omega) ** 2
        far = (row_omega + col_omega) ** 2
        cross = 4.0 * (row_omega * col_omega)
        for mode in range(modes):
            strength = phonon[mode]
            below = near + strength * strength
            above = far + strength * strength
            common = (2.0 * strength) / (below * above)
            columns = slice(mode * segment_rows, (mode + 1) * segment_rows)
            for part, value in enumerate((common * (below + above), common * cross)):
                high, low = split(value)
                tables[segment][part, :padded_rows, columns] = high
                if tables[segment].shape[1] > padded_rows:
                    tables[segment][part, padded_rows:, columns] = low


def other_tables_kernel(dims, meta, phonon, *tables):
    fill_tables(dims, meta, 2, phonon, tables)


def tables_kernel(
    dims, sides, meta, phonon, pair_cols, pair_count, block_order, coupling, plan, weights, *tables
):
    freq_count, segments, segment_rows, padded_rows, modes = dims
    blocks, slots = coupling.shape[:2]
    size = coupling.shape[3]
    for at in range(1 + segments):
        plan[ROWS, at] = meta[at]
    for block in range(blocks):
        for slot in range(slots):
            wanted = pair_cols[block, slot]
            position = jnp.int32(0)
            for at in range(block_order.shape[0]):
                position = jnp.where(block_order[at] == wanted, at, position)
            pair = block * slots + slot
            holder = position // blocks
            plan[HOLDER, pair] = (holder // sides) ^ meta[1 + segments]
            plan[SIDE, pair] = (holder % sides) ^ meta[2 + segments]
            plan[PLACE, pair] = position % blocks
            plan[LIVE, pair] = (pair_count[block] > slot).astype(jnp.int32)
    fill_tables(dims, meta, 0, phonon, tables)
    for block in range(blocks):
        for slot in range(slots):
            for mode in range(modes):
                weights[
                    block, slot * size : (slot + 1) * size, mode * size : (mode + 1) * size
                ] = coupling[block, slot, mode].T


def step_kernel(dims, segment, span, sides, coded, final, keep, parted, plan, *refs):
    freq_count, segments, segment_rows, padded_rows, modes = dims
    refs = list(refs)
    first, last = segment == 0, segment == segments - 1
    take = lambda count: [refs.pop() for _ in range(count)][::-1]
    copied = last and final
    if copied:
        *held, sems = take(3)
    terms = [] if keep else take(2 if first else 1)
    ratios = refs.pop()
    terms = terms or take(2)
    outs = take(2 if copied else 1)
    inputs = refs
    before = [inputs.pop() for _ in range(0 if first else parted)][::-1]
    weights, table = inputs[-2:]
    pieces = []
    for piece in inputs[:-2]:
        if len(piece.shape) == 3:
            pieces += [piece.at[at] for at in range(piece.shape[0])]
        else:
            pieces.append(piece)
    holders = len(pieces) // sides
    blocks = span[1] - span[0]
    size = LANES
    slots = weights.shape[1] // size
    shape = (segment_rows, size)
    col = lax.broadcasted_iota(jnp.int32, shape, 0) + plan[ROWS, 1 + segment]
    col_omega = omega_of(col, freq_count)
    square = col_omega * col_omega

    def fetch(pair):
        column = pl.multiple_of(plan[PLACE, pair] * size, size)
        wanted = plan[SIDE, pair] * holders + plan[HOLDER, pair]
        value = pieces[0][:segment_rows, pl.ds(column, size)]
        for at in range(1, len(pieces)):
            value = lax.select(wanted == at, pieces[at][:segment_rows, pl.ds(column, size)], value)
        return decoded(value) if coded else value

    def find_ratios(block):
        for slot in range(slots):
            pair = (span[0] + block) * slots + slot
            gap = fetch(pair)
            live = plan[LIVE, pair].astype(jnp.float32)
            inverse = lax.rsqrt(square + gap * gap) * live
            lanes = slice(slot * size, (slot + 1) * size)
            ratios[block, :segment_rows, lanes] = (gap * inverse).astype(jnp.bfloat16)
            ratios[block, segment_rows:, lanes] = (col_omega * inverse).astype(jnp.bfloat16)

    def find_terms(block):
        lanes = slice(block * size, (block + 1) * size)
        for start in range(0, modes, 2):
            stop = min(start + 2, modes)
            found = jnp.dot(
                ratios[block],
                weights[span[0] + block, :, start * size : stop * size],
                preferred_element_type=jnp.float32,
            )
            pieces_of = split(found) if len(terms) > 1 else [found.astype(jnp.bfloat16)]
            for mode in range(start, stop):
                rows = slice(mode * segment_rows, (mode + 1) * segment_rows)
                taken = slice((mode - start) * size, (mode - start + 1) * size)
                for part in range(2):
                    source = slice(part * segment_rows, (part + 1) * segment_rows)
                    for held_terms, value in zip(terms, pieces_of):
                        held_terms[part, rows, lanes] = value[source, taken]

    def earlier(part, lanes):
        width = before[0].shape[-1]
        start = lanes.start % width
        return before[lanes.start // width][part, :, start : start + lanes.stop - lanes.start]

    def find_sums(lanes):
        def total_of(part):
            views = [held_terms.at[part, :, lanes] for held_terms in terms]
            total = table_sums(padded_rows, table.at[part], *views)
            return total if first else total + earlier(part, lanes)

        if not last:
            for part in range(2):
                outs[0][part, :, lanes] = total_of(part)
            return
        own_rows = outs[0].shape[0]
        width = lanes.stop - lanes.start
        row = lax.broadcasted_iota(jnp.int32, (own_rows, width), 0) + plan[ROWS, 0]
        temperature = CUTOFF / freq_count
        renorm = 1.0 + temperature * total_of(1)[:own_rows] / omega_of(row, freq_count)
        if final:
            held[1][:, lanes] = renorm
            copy_out(1, lanes).start()
        gap = temperature * total_of(0)[:own_rows] / renorm
        if final:
            held[0][:, lanes] = gap
            copy_out(0, lanes).start()
        else:
            outs[0][:, lanes] = encoded(gap) if coded else gap

    def copy_out(at, lanes):
        width = lanes.stop - lanes.start
        return pltpu.make_async_copy(
            held[at].at[:, pl.ds(lanes.start, width)],
            outs[at].at[:, pl.ds(lanes.start, width)],
            sems.at[at, lanes.start // width],
        )

    halves = [slice(start * size, (start + 2) * size) for start in range(0, blocks, 2)]
    find_ratios(0)
    for block in range(blocks):
        if block + 1 < blocks:
            find_ratios(block + 1)
        find_terms(block)
        if block % 2 == 0 and block > 1:
            find_sums(halves[block // 2 - 1])
    find_sums(halves[-1])
    if copied:
        for lanes in halves:
            for at in range(2):
                copy_out(at, lanes).wait()


def table_sums(padded_rows, table, high, low=None):
    both = jnp.dot(table[...], high[...], preferred_element_type=jnp.float32)
    if table.shape[0] == padded_rows:
        return both
    rest = jnp.dot(table[:padded_rows], low[...], preferred_element_type=jnp.float32)
    return both[:padded_rows] + (both[padded_rows:] + rest)


def other_rows_kernel(dims, plan, *refs):
    freq_count, segments, segment_rows, padded_rows, modes = dims
    tables, terms, code = refs[:segments], refs[segments:-1], refs[-1]
    states = code.shape[1]
    temperature = CUTOFF / freq_count
    for start in range(0, states, 2 * LANES):
        lanes = slice(start, min(start + 2 * LANES, states))

        def total_of(part):
            total = None
            for segment in range(segments):
                views = [terms[2 * segment + at].at[part, :, lanes] for at in range(2)]
                piece = table_sums(padded_rows, tables[segment].at[part], *views)
                total = piece if total is None else total + piece
            return total

        row = lax.broadcasted_iota(jnp.int32, (padded_rows, lanes.stop - start), 0)
        omega = omega_of(row + plan[ROWS, 2], freq_count)
        renorm = 1.0 + temperature * total_of(1) / omega
        code[:padded_rows, lanes] = encoded(temperature * total_of(0) / renorm)
    code[padded_rows:] = jnp.zeros((SPARE_ROWS, states), code.dtype)


SWAP = [(0, 1), (1, 0)]


def gather_general(gap, half_groups):
    everyone = lax.all_gather(gap, "state", axis=0, tiled=False)
    rows = lax.all_gather(everyone, "freq", axis=1, tiled=True)
    own_rows = gap.shape[0]
    start = (lax.axis_index("freq") // half_groups) * (half_groups * own_rows)
    return [lax.dynamic_slice_in_dim(rows, start, half_groups * own_rows, 1)]


def on_device(pairwise, freq_groups, gap_in, coupling, pair_cols, pair_count, block_order, phonon):
    own_rows, row_width = gap_in.shape
    blocks, slots, modes, size, _ = coupling.shape
    freq_count = own_rows * freq_groups
    half_rows = freq_count // 2
    half_groups = freq_groups // 2
    padded_rows = -(-own_rows // 16) * 16
    if pairwise:
        segments, sides = 2, 2
        half = lax.axis_index("zhi") * half_rows
        own = half + lax.axis_index("zlo") * own_rows
        other = half + (1 - lax.axis_index("zlo")) * own_rows
        meta = [own, own, other, lax.axis_index("x"), lax.axis_index("core")]
    else:
        segments, sides = 1, 1
        freq_at = lax.axis_index("freq")
        meta = [freq_at * own_rows, (freq_at // half_groups) * half_rows, 0, 0]
    meta = jnp.stack([jnp.asarray(value, jnp.int32) for value in meta])
    segment_rows = half_rows // segments
    dims = (freq_count, segments, segment_rows, padded_rows, modes)
    smem = pl.BlockSpec(memory_space=pltpu.SMEM)
    vmem = pl.BlockSpec(memory_space=pltpu.VMEM)
    link_type = jnp.int16 if pairwise else jnp.float32

    passed = gap_in
    if pairwise:
        passed = pl.pallas_call(
            encode_kernel,
            out_shape=jax.ShapeDtypeStruct(gap_in.shape, link_type),
            in_specs=[vmem],
            out_specs=vmem,
            compiler_params=pltpu.CompilerParams(vmem_limit_bytes=8 << 20),
            cost_estimate=pl.CostEstimate(
                flops=10_000_000_000, bytes_accessed=40_000_000, transcendentals=0
            ),
            name="encode",
        )(gap_in)

    near_table, far_table = [
        jax.ShapeDtypeStruct((2, count * padded_rows, modes * segment_rows), jnp.bfloat16)
        for count in (2, 1)
    ]
    plan, weights, *tables = pl.pallas_call(
        functools.partial(tables_kernel, dims, sides),
        out_shape=[
            jax.ShapeDtypeStruct((5, max(blocks * slots, 1 + segments)), jnp.int32),
            jax.ShapeDtypeStruct((blocks, slots * size, modes * size), jnp.bfloat16),
        ]
        + [near_table, far_table][:segments],
        in_specs=[smem] * 5 + [vmem],
        out_specs=[smem] + [vmem] * (1 + segments),
        compiler_params=pltpu.CompilerParams(vmem_limit_bytes=24 << 20),
        cost_estimate=pl.CostEstimate(
            flops=10_000_000, bytes_accessed=8_000_000, transcendentals=0
        ),
        name="tables",
    )(meta, phonon, pair_cols, pair_count, block_order, coupling)

    full = jax.ShapeDtypeStruct(gap_in.shape, jnp.float32)
    passed_out = jax.ShapeDtypeStruct(gap_in.shape, link_type)
    step_params = dict(
        compiler_params=pltpu.CompilerParams(vmem_limit_bytes=24 << 20),
        cost_estimate=pl.CostEstimate(
            flops=STEP_FLOPS, bytes_accessed=100_000, transcendentals=0
        ),
    )

    def step(plan, segment, final, pieces, before, keep=False, span=(0, blocks)):
        copied = final and segment == segments - 1
        width = (span[1] - span[0]) * size
        terms_shape = (2, modes * segment_rows, width)
        if segment < segments - 1:
            outs = [jax.ShapeDtypeStruct((2, padded_rows, width), jnp.float32)]
        else:
            outs = [full, full] if final else [passed_out]
        out_specs = [pl.BlockSpec(memory_space=pl.ANY) if copied else vmem] * len(outs)
        scratch = [pltpu.VMEM((span[1] - span[0], 2 * segment_rows, slots * size), jnp.bfloat16)]
        if keep:
            outs += [jax.ShapeDtypeStruct(terms_shape, jnp.bfloat16)] * 2
            out_specs += [vmem] * 2
        else:
            scratch += [pltpu.VMEM(terms_shape, jnp.bfloat16)] * (2 if segment == 0 else 1)
        if copied:
            scratch += [pltpu.VMEM(gap_in.shape, jnp.float32)] * 2
            scratch += [pltpu.SemaphoreType.DMA((2, blocks // 2))]
        inputs = [*pieces, weights, tables[segment], *before]
        return pl.pallas_call(
            functools.partial(
                step_kernel, dims, segment, span, sides, pairwise, final, keep, len(before)
            ),
            out_shape=outs,
            in_specs=[smem] + [vmem] * len(inputs),
            out_specs=out_specs,
            scratch_shapes=scratch,
            name="step",
            **step_params,
        )(plan, *inputs)

    if not pairwise:
        for iteration in range(ITERS):
            final = iteration == ITERS - 1
            results = step(plan, 0, final, gather_general(passed, half_groups), [])
            passed = results[0]
        return tuple(results)

    def join(near, across, after):
        return pl.pallas_call(
            join_kernel,
            out_shape=jax.ShapeDtypeStruct((2, *gap_in.shape), near.dtype),
            in_specs=[vmem, vmem, pl.BlockSpec(memory_space=pl.ANY)],
            out_specs=vmem,
            compiler_params=pltpu.CompilerParams(vmem_limit_bytes=4 << 20),
            cost_estimate=pl.CostEstimate(flops=1000, bytes_accessed=1000, transcendentals=0),
            name="join",
        )(near, across, after)

    def with_core(near):
        return near + [lax.ppermute(piece, "core", SWAP) for piece in near]

    other_tables = pl.pallas_call(
        functools.partial(other_tables_kernel, dims),
        out_shape=[far_table, near_table],
        in_specs=[smem, smem],
        out_specs=[vmem] * segments,
        compiler_params=pltpu.CompilerParams(vmem_limit_bytes=12 << 20),
        cost_estimate=pl.CostEstimate(
            flops=10_000_000, bytes_accessed=3_000_000, transcendentals=0
        ),
        name="other_tables",
    )(meta, phonon)
    along_x = lax.ppermute(passed, "x", SWAP)
    along_z = lax.ppermute(passed, "zlo", SWAP)
    along_x, plan = lax.optimization_barrier((along_x, plan))
    relayed = lax.ppermute(along_z, "x", SWAP)
    partial, *near_terms = step(plan, 0, False, with_core([passed, along_x]), [], keep=True)
    far = join(along_z, relayed, partial)
    pieces = [far, lax.ppermute(far, "core", SWAP)]
    plan, *other_tables = lax.optimization_barrier((plan, *other_tables))
    own, *far_terms = step(plan, 1, False, pieces, [partial], keep=True)
    inputs = [*other_tables, *near_terms, *far_terms]
    other = pl.pallas_call(
        functools.partial(other_rows_kernel, dims),
        out_shape=jax.ShapeDtypeStruct((own_rows + SPARE_ROWS, row_width), link_type),
        in_specs=[smem] + [vmem] * len(inputs),
        out_specs=vmem,
        name="other_rows",
        **step_params,
    )(plan, *inputs)
    along_x = lax.ppermute(own, "x", SWAP)
    near = with_core([own, along_x])
    across = lax.ppermute(other, "core", SWAP)
    partial = step(plan, 0, True, near, [])
    along_x, *partial = lax.optimization_barrier((lax.ppermute(other, "x", SWAP), *partial))
    far = [other, along_x, across, lax.ppermute(along_x, "core", SWAP)]
    return tuple(step(plan, 1, True, far, partial))


def solution(mesh):
    shape = tuple(mesh.shape[axis] for axis in ("parts", "freq", "state"))
    pairwise = shape[1:] == (4, 4)
    parts, freq, state = "parts", "freq", "state"
    if pairwise:
        names = ("parts", "zhi", "zlo", "x", "core")
        mesh = jax.sharding.Mesh(mesh.devices.reshape(shape[0], 2, 2, 2, 2), names)
        freq, state = ("zhi", "zlo"), ("x", "core")
    rows = ("parts", *freq) if pairwise else ("parts", freq)
    groups = ("parts", *state) if pairwise else ("parts", state)
    return jax.shard_map(
        functools.partial(on_device, pairwise, shape[1]),
        mesh=mesh,
        in_specs=(
            P(rows, state),
            P(groups, None, None, None, None),
            P(groups, None),
            P(groups),
            P(parts),
            P(parts),
        ),
        out_specs=(P(rows, state), P(rows, state)),
        check_vma=False,
    )
```

```python
import functools

import jax
import jax.numpy as jnp
from jax import lax
from jax.experimental import pallas as pl
from jax.experimental.pallas import tpu as pltpu
from jax.sharding import PartitionSpec as P

ITERS = 2
CUTOFF = 4.0
LANES = 128
GAP_LIMIT = 10.0
CODE_LIMIT = 32767.0
CODE_POWER = 5
STEP_FLOPS = 1_000_000
SPARE_ROWS = 16
HOLDER, PLACE, LIVE, SIDE, ROWS = 0, 1, 2, 3, 4


def omega_of(index, freq_count):
    return (2.0 * index.astype(jnp.float32) + 1.0 - freq_count) * (CUTOFF / freq_count)


def encoded(gap):
    share = jnp.minimum(jnp.abs(gap) * (1.0 / GAP_LIMIT), 1.0)
    root = jnp.exp2(jnp.log2(jnp.maximum(share, 1e-37)) * (1.0 / CODE_POWER))
    code = jnp.floor(root * CODE_LIMIT + 0.5)
    return jnp.where(gap < 0, -code, code).astype(jnp.int32).astype(jnp.int16)


def decoded(code):
    root = code.astype(jnp.float32) * (1.0 / CODE_LIMIT)
    square = root * root
    return (root * GAP_LIMIT) * (square * square)


def encode_kernel(gap, code):
    code[...] = encoded(gap[...])


def join_kernel(first, second, after, joined):
    rows = joined.shape[1]
    joined[0] = first[:rows]
    joined[1] = second[:rows]


def split(value):
    high = value.astype(jnp.bfloat16)
    return high, (value - high.astype(jnp.float32)).astype(jnp.bfloat16)


def fill_tables(dims, meta, row_from, phonon, tables):
    freq_count, segments, segment_rows, padded_rows, modes = dims
    shape = (padded_rows, segment_rows)
    row_omega = omega_of(lax.broadcasted_iota(jnp.int32, shape, 0) + meta[row_from], freq_count)
    for segment in range(len(tables)):
        col = lax.broadcasted_iota(jnp.int32, shape, 1) + meta[1 + segment]
        col_omega = omega_of(col, freq_count)
        near = (row_omega - col_omega) ** 2
        far = (row_omega + col_omega) ** 2
        cross = 4.0 * (row_omega * col_omega)
        for mode in range(modes):
            strength = phonon[mode]
            below = near + strength * strength
            above = far + strength * strength
            common = (2.0 * strength) / (below * above)
            columns = slice(mode * segment_rows, (mode + 1) * segment_rows)
            for part, value in enumerate((common * (below + above), common * cross)):
                high, low = split(value)
                tables[segment][part, :padded_rows, columns] = high
                if tables[segment].shape[1] > padded_rows:
                    tables[segment][part, padded_rows:, columns] = low


def other_tables_kernel(dims, meta, phonon, *tables):
    fill_tables(dims, meta, 2, phonon, tables)


def tables_kernel(
    dims, sides, meta, phonon, pair_cols, pair_count, block_order, coupling, plan, weights, *tables
):
    freq_count, segments, segment_rows, padded_rows, modes = dims
    blocks, slots = coupling.shape[:2]
    size = coupling.shape[3]
    for at in range(1 + segments):
        plan[ROWS, at] = meta[at]
    for block in range(blocks):
        for slot in range(slots):
            wanted = pair_cols[block, slot]
            position = jnp.int32(0)
            for at in range(block_order.shape[0]):
                position = jnp.where(block_order[at] == wanted, at, position)
            pair = block * slots + slot
            holder = position // blocks
            plan[HOLDER, pair] = (holder // sides) ^ meta[1 + segments]
            plan[SIDE, pair] = (holder % sides) ^ meta[2 + segments]
            plan[PLACE, pair] = position % blocks
            plan[LIVE, pair] = (pair_count[block] > slot).astype(jnp.int32)
    fill_tables(dims, meta, 0, phonon, tables)
    for block in range(blocks):
        for slot in range(slots):
            for mode in range(modes):
                weights[
                    block, slot * size : (slot + 1) * size, mode * size : (mode + 1) * size
                ] = coupling[block, slot, mode].T


def step_kernel(dims, segment, span, sides, coded, final, keep, parted, plan, *refs):
    freq_count, segments, segment_rows, padded_rows, modes = dims
    refs = list(refs)
    first, last = segment == 0, segment == segments - 1
    take = lambda count: [refs.pop() for _ in range(count)][::-1]
    copied = last and final
    if copied:
        *held, sems = take(3)
    terms = [] if keep else take(2 if first else 1)
    ratios = refs.pop()
    terms = terms or take(2)
    outs = take(2 if copied else 1)
    inputs = refs
    before = [inputs.pop() for _ in range(0 if first else parted)][::-1]
    weights, table = inputs[-2:]
    pieces = []
    for piece in inputs[:-2]:
        if len(piece.shape) == 3:
            pieces += [piece.at[at] for at in range(piece.shape[0])]
        else:
            pieces.append(piece)
    holders = len(pieces) // sides
    blocks = span[1] - span[0]
    size = LANES
    slots = weights.shape[1] // size
    shape = (segment_rows, size)
    col = lax.broadcasted_iota(jnp.int32, shape, 0) + plan[ROWS, 1 + segment]
    col_omega = omega_of(col, freq_count)
    square = col_omega * col_omega

    def fetch(pair):
        column = pl.multiple_of(plan[PLACE, pair] * size, size)
        wanted = plan[SIDE, pair] * holders + plan[HOLDER, pair]
        value = pieces[0][:, pl.ds(column, size)]
        for at in range(1, len(pieces)):
            value = lax.select(wanted == at, pieces[at][:, pl.ds(column, size)], value)
        return decoded(value) if coded else value

    def find_ratios(block):
        for slot in range(slots):
            pair = (span[0] + block) * slots + slot
            gap = fetch(pair)
            live = plan[LIVE, pair].astype(jnp.float32)
            inverse = lax.rsqrt(square + gap * gap) * live
            lanes = slice(slot * size, (slot + 1) * size)
            ratios[block, :segment_rows, lanes] = (gap * inverse).astype(jnp.bfloat16)
            ratios[block, segment_rows:, lanes] = (col_omega * inverse).astype(jnp.bfloat16)

    def find_terms(block):
        lanes = slice(block * size, (block + 1) * size)
        for start in range(0, modes, 2):
            stop = min(start + 2, modes)
            found = jnp.dot(
                ratios[block],
                weights[span[0] + block, :, start * size : stop * size],
                preferred_element_type=jnp.float32,
            )
            pieces_of = split(found) if len(terms) > 1 else [found.astype(jnp.bfloat16)]
            for mode in range(start, stop):
                rows = slice(mode * segment_rows, (mode + 1) * segment_rows)
                taken = slice((mode - start) * size, (mode - start + 1) * size)
                for part in range(2):
                    source = slice(part * segment_rows, (part + 1) * segment_rows)
                    for held_terms, value in zip(terms, pieces_of):
                        held_terms[part, rows, lanes] = value[source, taken]

    def earlier(part, lanes):
        width = before[0].shape[-1]
        start = lanes.start % width
        return before[lanes.start // width][part, :, start : start + lanes.stop - lanes.start]

    def find_sums(lanes):
        def total_of(part):
            views = [held_terms.at[part, :, lanes] for held_terms in terms]
            total = table_sums(padded_rows, table.at[part], *views)
            return total if first else total + earlier(part, lanes)

        if not last:
            for part in range(2):
                outs[0][part, :, lanes] = total_of(part)
            return
        own_rows = outs[0].shape[0]
        width = lanes.stop - lanes.start
        row = lax.broadcasted_iota(jnp.int32, (own_rows, width), 0) + plan[ROWS, 0]
        temperature = CUTOFF / freq_count
        renorm = 1.0 + temperature * total_of(1)[:own_rows] / omega_of(row, freq_count)
        if final:
            held[1][:, lanes] = renorm
            copy_out(1, lanes).start()
        gap = temperature * total_of(0)[:own_rows] / renorm
        if final:
            held[0][:, lanes] = gap
            copy_out(0, lanes).start()
        else:
            outs[0][:, lanes] = encoded(gap) if coded else gap

    def copy_out(at, lanes):
        width = lanes.stop - lanes.start
        return pltpu.make_async_copy(
            held[at].at[:, pl.ds(lanes.start, width)],
            outs[at].at[:, pl.ds(lanes.start, width)],
            sems.at[at, lanes.start // width],
        )

    halves = [slice(start * size, (start + 2) * size) for start in range(0, blocks, 2)]
    find_ratios(0)
    for block in range(blocks):
        if block + 1 < blocks:
            find_ratios(block + 1)
        find_terms(block)
        if block % 2 == 0 and block > 1:
            find_sums(halves[block // 2 - 1])
    find_sums(halves[-1])
    if copied:
        for lanes in halves:
            for at in range(2):
                copy_out(at, lanes).wait()


def table_sums(padded_rows, table, high, low=None):
    both = jnp.dot(table[...], high[...], preferred_element_type=jnp.float32)
    if table.shape[0] == padded_rows:
        return both
    rest = jnp.dot(table[:padded_rows], low[...], preferred_element_type=jnp.float32)
    return both[:padded_rows] + (both[padded_rows:] + rest)


def other_rows_kernel(dims, plan, *refs):
    freq_count, segments, segment_rows, padded_rows, modes = dims
    tables, terms, code = refs[:segments], refs[segments:-1], refs[-1]
    states = code.shape[1]
    temperature = CUTOFF / freq_count
    for start in range(0, states, 2 * LANES):
        lanes = slice(start, min(start + 2 * LANES, states))

        def total_of(part):
            total = None
            for segment in range(segments):
                views = [terms[2 * segment + at].at[part, :, lanes] for at in range(2)]
                piece = table_sums(padded_rows, tables[segment].at[part], *views)
                total = piece if total is None else total + piece
            return total

        row = lax.broadcasted_iota(jnp.int32, (padded_rows, lanes.stop - start), 0)
        omega = omega_of(row + plan[ROWS, 2], freq_count)
        renorm = 1.0 + temperature * total_of(1) / omega
        code[:padded_rows, lanes] = encoded(temperature * total_of(0) / renorm)
    code[padded_rows:] = jnp.zeros((SPARE_ROWS, states), code.dtype)


SWAP = [(0, 1), (1, 0)]


def gather_general(gap, half_groups):
    everyone = lax.all_gather(gap, "state", axis=0, tiled=False)
    rows = lax.all_gather(everyone, "freq", axis=1, tiled=True)
    own_rows = gap.shape[0]
    start = (lax.axis_index("freq") // half_groups) * (half_groups * own_rows)
    return [lax.dynamic_slice_in_dim(rows, start, half_groups * own_rows, 1)]


def on_device(pairwise, freq_groups, gap_in, coupling, pair_cols, pair_count, block_order, phonon):
    own_rows, row_width = gap_in.shape
    blocks, slots, modes, size, _ = coupling.shape
    freq_count = own_rows * freq_groups
    half_rows = freq_count // 2
    half_groups = freq_groups // 2
    padded_rows = -(-own_rows // 16) * 16
    if pairwise:
        segments, sides = 2, 2
        half = lax.axis_index("zhi") * half_rows
        own = half + lax.axis_index("zlo") * own_rows
        other = half + (1 - lax.axis_index("zlo")) * own_rows
        meta = [own, own, other, lax.axis_index("x"), lax.axis_index("core")]
    else:
        segments, sides = 1, 1
        freq_at = lax.axis_index("freq")
        meta = [freq_at * own_rows, (freq_at // half_groups) * half_rows, 0, 0]
    meta = jnp.stack([jnp.asarray(value, jnp.int32) for value in meta])
    segment_rows = half_rows // segments
    dims = (freq_count, segments, segment_rows, padded_rows, modes)
    smem = pl.BlockSpec(memory_space=pltpu.SMEM)
    vmem = pl.BlockSpec(memory_space=pltpu.VMEM)
    link_type = jnp.int16 if pairwise else jnp.float32

    passed = gap_in
    if pairwise:
        passed = pl.pallas_call(
            encode_kernel,
            out_shape=jax.ShapeDtypeStruct(gap_in.shape, link_type),
            in_specs=[vmem],
            out_specs=vmem,
            compiler_params=pltpu.CompilerParams(vmem_limit_bytes=8 << 20),
            cost_estimate=pl.CostEstimate(
                flops=10_000_000_000, bytes_accessed=40_000_000, transcendentals=0
            ),
            name="encode",
        )(gap_in)

    near_table, far_table = [
        jax.ShapeDtypeStruct((2, count * padded_rows, modes * segment_rows), jnp.bfloat16)
        for count in (2, 1)
    ]
    plan, weights, *tables = pl.pallas_call(
        functools.partial(tables_kernel, dims, sides),
        out_shape=[
            jax.ShapeDtypeStruct((5, max(blocks * slots, 1 + segments)), jnp.int32),
            jax.ShapeDtypeStruct((blocks, slots * size, modes * size), jnp.bfloat16),
        ]
        + [near_table, far_table][:segments],
        in_specs=[smem] * 5 + [vmem],
        out_specs=[smem] + [vmem] * (1 + segments),
        compiler_params=pltpu.CompilerParams(vmem_limit_bytes=24 << 20),
        cost_estimate=pl.CostEstimate(
            flops=10_000_000, bytes_accessed=8_000_000, transcendentals=0
        ),
        name="tables",
    )(meta, phonon, pair_cols, pair_count, block_order, coupling)

    full = jax.ShapeDtypeStruct(gap_in.shape, jnp.float32)
    passed_out = jax.ShapeDtypeStruct(gap_in.shape, link_type)
    step_params = dict(
        compiler_params=pltpu.CompilerParams(vmem_limit_bytes=24 << 20),
        cost_estimate=pl.CostEstimate(
            flops=STEP_FLOPS, bytes_accessed=100_000, transcendentals=0
        ),
    )

    def step(plan, segment, final, pieces, before, keep=False, span=(0, blocks)):
        copied = final and segment == segments - 1
        width = (span[1] - span[0]) * size
        terms_shape = (2, modes * segment_rows, width)
        if segment < segments - 1:
            outs = [jax.ShapeDtypeStruct((2, padded_rows, width), jnp.float32)]
        else:
            outs = [full, full] if final else [passed_out]
        out_specs = [pl.BlockSpec(memory_space=pl.ANY) if copied else vmem] * len(outs)
        scratch = [pltpu.VMEM((span[1] - span[0], 2 * segment_rows, slots * size), jnp.bfloat16)]
        if keep:
            outs += [jax.ShapeDtypeStruct(terms_shape, jnp.bfloat16)] * 2
            out_specs += [vmem] * 2
        else:
            scratch += [pltpu.VMEM(terms_shape, jnp.bfloat16)] * (2 if segment == 0 else 1)
        if copied:
            scratch += [pltpu.VMEM(gap_in.shape, jnp.float32)] * 2
            scratch += [pltpu.SemaphoreType.DMA((2, blocks // 2))]
        inputs = [*pieces, weights, tables[segment], *before]
        return pl.pallas_call(
            functools.partial(
                step_kernel, dims, segment, span, sides, pairwise, final, keep, len(before)
            ),
            out_shape=outs,
            in_specs=[smem] + [vmem] * len(inputs),
            out_specs=out_specs,
            scratch_shapes=scratch,
            name="step",
            **step_params,
        )(plan, *inputs)

    if not pairwise:
        for iteration in range(ITERS):
            final = iteration == ITERS - 1
            results = step(plan, 0, final, gather_general(passed, half_groups), [])
            passed = results[0]
        return tuple(results)

    def join(near, across, after):
        return pl.pallas_call(
            join_kernel,
            out_shape=jax.ShapeDtypeStruct((2, *gap_in.shape), near.dtype),
            in_specs=[vmem, vmem, pl.BlockSpec(memory_space=pl.ANY)],
            out_specs=vmem,
            compiler_params=pltpu.CompilerParams(vmem_limit_bytes=4 << 20),
            cost_estimate=pl.CostEstimate(flops=1000, bytes_accessed=1000, transcendentals=0),
            name="join",
        )(near, across, after)

    def with_core(near):
        return near + [lax.ppermute(piece, "core", SWAP) for piece in near]

    other_tables = pl.pallas_call(
        functools.partial(other_tables_kernel, dims),
        out_shape=[far_table, near_table],
        in_specs=[smem, smem],
        out_specs=[vmem] * segments,
        compiler_params=pltpu.CompilerParams(vmem_limit_bytes=12 << 20),
        cost_estimate=pl.CostEstimate(
            flops=10_000_000, bytes_accessed=3_000_000, transcendentals=0
        ),
        name="other_tables",
    )(meta, phonon)
    along_x = lax.ppermute(passed, "x", SWAP)
    along_z = lax.ppermute(passed, "zlo", SWAP)
    along_x, plan = lax.optimization_barrier((along_x, plan))
    relayed = lax.ppermute(along_z, "x", SWAP)
    partial, *near_terms = step(plan, 0, False, with_core([passed, along_x]), [], keep=True)
    across = lax.ppermute(along_z, "core", SWAP)
    relayed, partial = lax.optimization_barrier((relayed, partial))
    pieces = [along_z, relayed, across, lax.ppermute(relayed, "core", SWAP)]
    plan, *other_tables = lax.optimization_barrier((plan, *other_tables))
    own, *far_terms = step(plan, 1, False, pieces, [partial], keep=True)
    inputs = [*other_tables, *near_terms, *far_terms]
    other = pl.pallas_call(
        functools.partial(other_rows_kernel, dims),
        out_shape=jax.ShapeDtypeStruct((own_rows + SPARE_ROWS, row_width), link_type),
        in_specs=[smem] + [vmem] * len(inputs),
        out_specs=vmem,
        name="other_rows",
        **step_params,
    )(plan, *inputs)
    along_x = lax.ppermute(own, "x", SWAP)
    near = with_core([own, along_x])
    middle = blocks // 2
    partial = step(plan, 0, True, near, [], span=(0, middle))
    far = join(other, lax.ppermute(other, "x", SWAP), *partial)
    partial += step(plan, 0, True, near, [], span=(middle, blocks))
    return tuple(step(plan, 1, True, [far, lax.ppermute(far, "core", SWAP)], partial))


def solution(mesh):
    shape = tuple(mesh.shape[axis] for axis in ("parts", "freq", "state"))
    pairwise = shape[1:] == (4, 4)
    parts, freq, state = "parts", "freq", "state"
    if pairwise:
        names = ("parts", "zhi", "zlo", "x", "core")
        mesh = jax.sharding.Mesh(mesh.devices.reshape(shape[0], 2, 2, 2, 2), names)
        freq, state = ("zhi", "zlo"), ("x", "core")
    rows = ("parts", *freq) if pairwise else ("parts", freq)
    groups = ("parts", *state) if pairwise else ("parts", state)
    return jax.shard_map(
        functools.partial(on_device, pairwise, shape[1]),
        mesh=mesh,
        in_specs=(
            P(rows, state),
            P(groups, None, None, None, None),
            P(groups, None),
            P(groups),
            P(parts),
            P(parts),
        ),
        out_specs=(P(rows, state), P(rows, state)),
        check_vma=False,
    )
```
